512 devices in a mesh: dp: 4 (over y), row: 16 (over z), col: 8 (over x, core).
Axes of the slice: x: 4, y: 4, z: 16, core: 2. Of those that a mesh axis runs over, the one named last changes fastest.
Arguments:
- activations: bfloat16 [4, 3072, 4096], P('dp', 'col', 'row'), may hold values from -6 to 6
- out_grads: bfloat16 [4, 3072, 14336], P('dp', 'row', 'col'), may hold values from -0.078125 to 0.078125
- query_ids: int32 [4, 3072], P('dp'), may hold values from 0 to 383, never falling along the last dimension, each value on 1 to 32 neighbouring positions
- clip_bound: int32 [1], replicated, may hold values from 160 to 459
Outputs:
- weight_grad: float32 [4096, 14336], P('row', 'col')
The draws below stay inside these ranges and needn't reach their ends.
Inputs may be any that keep to these rules, and one draw needn't show every extreme that they name: `query_ids`: within each data group the ids never fall along the tokens; each query holds 1 to 32 consecutive tokens, and one holds exactly 32.
All inputs are finite; a program needn't handle non-finite values.
Results may differ from the reference program's by a relative error of at most 0.0003.
The reference program's roundings to bfloat16 on the way (of `scaled`) count: a program that leaves them out, or rounds other values in their place, can miss the bound.
Values may be sent and summed in bfloat16 or wider, within the bound.
A program may use at most 64 MiB of HBM per device.

```python
import math
import jax
import jax.numpy as jnp
import numpy as np
from jax import lax

D = 4096
FF = 14336
TILE = 32
TOKG = 3072
QUERIES = 384
N_DP = 4


def levels(key, dims, pieces, smallest, high):
    level = 1.0
    for dim, blocks in pieces:
        steps = jax.random.uniform(jax.random.fold_in(jax.random.fold_in(key, 6), dim), (blocks,), jnp.float32, smallest / len(pieces), high / len(pieces))
        level = level * jnp.repeat(jnp.exp(steps), dims[dim] // blocks).reshape((-1,) + (1,) * (len(dims) - 1 - dim))
    return level


def length_profile(count, total, most, skew):
    portions = [(1 << 20) // math.isqrt(standing ** skew) + 1 for standing in range(2, count + 1)]
    surplus, counts = total - most - (count - 1), [1] * (count - 1)
    while surplus > 0:
        movable = [i for i in range(count - 1) if counts[i] < most]
        whole, left = sum([portions[i] for i in movable]), surplus
        for i in movable:
            more = min(most - counts[i], max(1, left * portions[i] // whole), surplus)
            counts[i] = counts[i] + more
            surplus = surplus - more
    return np.array([most] + counts)


def ragged(own_key, amount, total, most, lean):
    if amount == 2:
        one = jax.random.randint(own_key, (), max(1, total - most), min(most, total - 1) + 1)
        return jnp.stack([one, total - one])
    tallies = jnp.asarray(length_profile(amount, total, most, lean), jnp.int32)
    couples = (amount - 1) // 2
    donor, taker = tallies[1:1 + 2 * couples:2], tallies[2:2 + 2 * couples:2]
    margin = jnp.minimum(donor - 1, most - taker)
    shifted = jax.random.randint(jax.random.fold_in(own_key, 1), (couples,), 0, 1 << 20) % (margin + 1)
    tallies = tallies.at[1:1 + 2 * couples:2].set(donor - shifted).at[2:2 + 2 * couples:2].set(taker + shifted)
    return tallies[jax.random.permutation(jax.random.fold_in(own_key, 2), amount)]


def gaussian(own_key, dims, scale, bound, shards=(), kind=jnp.bfloat16):
    entries = scale * jax.random.normal(own_key, dims, jnp.float32)
    if shards:
        entries = entries * levels(own_key, dims, shards, -0.22, 0.18)
    return jnp.clip(entries, -bound, bound).astype(kind)


def setup_inputs(seed: int = 0) -> dict:
    splits = jax.random.split(jax.random.key(seed), 5)
    return {
        "activations": gaussian(splits[0], (N_DP, TOKG, D), 1.0, 6.0, ((0, 4), (1, 8), (2, 16))),
        "out_grads": gaussian(splits[1], (N_DP, TOKG, FF), (600 * (D * FF * TILE) ** -0.5), 0.078125, ((0, 4), (1, 16), (2, 8))),
        "query_ids": jax.vmap(lambda own: jnp.searchsorted(jnp.cumsum(ragged(own, QUERIES, TOKG, TILE, 0)), jnp.arange(TOKG), side="right"))(jax.random.split(splits[2], N_DP)).reshape((N_DP, TOKG)).astype(jnp.int32),
        "clip_bound": jax.random.randint(splits[3], (1,), 160, 460).astype(jnp.int32),
    }


def banded(rows):
    tiles = rows.astype(jnp.float32).reshape(-1, TILE, rows.shape[1])
    before = jnp.concatenate([jnp.zeros_like(tiles[:1]), tiles[:-1]], 0)
    same = jnp.einsum('kiw,kjw->kij', tiles, tiles)
    cross = jnp.einsum('kiw,kjw->kij', tiles, before)
    return (same, cross)

def query_squares(act_pair, grad_pair, idents, queries):
    id_tiles = idents.reshape(-1, TILE)
    id_prev = jnp.concatenate([jnp.full((1, TILE), -1, jnp.int32), id_tiles[:-1]], 0)
    match_same = id_tiles[:, :, None] == id_tiles[:, None, :]
    match_cross = id_tiles[:, :, None] == id_prev[:, None, :]
    weights = lax.optimization_barrier(jnp.sum(jnp.where(match_same, act_pair[0] * grad_pair[0], 0.0), -1))
    weights = weights + 2.0 * lax.optimization_barrier(jnp.sum(jnp.where(match_cross, act_pair[1] * grad_pair[1], 0.0), -1))
    onehot = (idents[:, None] == jnp.arange(queries, dtype=jnp.int32)[None, :]).astype(jnp.float32)
    return (jnp.dot(weights.reshape(1, -1), onehot, precision=lax.Precision.HIGHEST)[0], onehot)

def reference(activations, out_grads, query_ids, clip_bound):
    limit = clip_bound[0].astype(jnp.float32)
    total = jnp.zeros((activations.shape[2], out_grads.shape[2]), jnp.float32)
    for group in range(N_DP):
        squares, onehot = query_squares(banded(activations[group]), banded(out_grads[group]), query_ids[group], QUERIES)
        factor = limit / jnp.maximum(jnp.sqrt(squares), limit)
        scale = jnp.dot(onehot, factor, precision=lax.Precision.HIGHEST)
        scaled = (activations[group].astype(jnp.float32) * scale[:, None]).astype(jnp.bfloat16)
        total = total + jnp.dot(scaled.T, out_grads[group], preferred_element_type=jnp.float32)
    return total
```

```python
import functools

import jax
import jax.numpy as jnp
from jax import lax
from jax.experimental import pallas as pl
from jax.experimental.pallas import tpu as pltpu
from jax.sharding import PartitionSpec as P

TILE = 32
LANES = 128
CHUNK = 256
MESH = pl.DeviceIdType.MESH


def packed_band(tile, window):
    zeros = jnp.zeros_like(window)
    dims = (((1,), (1,)), ((), ()))
    low = lax.dot_general(
        tile[:16], jnp.concatenate([window, zeros], 0), dims, preferred_element_type=jnp.float32
    )
    high = lax.dot_general(
        tile[16:], jnp.concatenate([zeros, window], 0), dims, preferred_element_type=jnp.float32
    )
    return low + high


def kernel(
    sizes,
    x_ref, g_ref, ids_ref, clip_ref,
    out_ref,
    gbuf, xbuf, halo, st, idcol, rows,
    asend, abuf, bsend, bbuf, wloc, wall,
    pbuf, rbuf, qbuf,
    lsem, osem, xs, xr, hs, rs, rr, asem, arec, bsem, brec, wsem, wrec, zsem, zrec, ys, yr, qs, qr,
):
    ny, nz, nw, tokens = sizes
    nx = nw // 2
    tz = g_ref.shape[0]
    tc = x_ref.shape[0]
    tiles = tz // TILE
    chunks = g_ref.shape[1] // CHUNK
    steps = nz // 2
    skew = steps // 2
    cut = tz // 2 - 16
    blocks = tokens // LANES
    part = x_ref.shape[1] // ny

    y = lax.axis_index("dp")
    z = lax.axis_index("row")
    w = lax.axis_index("col")
    core = lax.rem(w, 2)
    chip = w // 2

    def z_at(d):
        return lax.rem(z + d, nz)

    def w_at(d):
        return lax.rem(w + d, nw)

    def y_at(d):
        return lax.rem(y + d, ny)

    def copy_to(src, dst, send, recv, **axis):
        return pltpu.make_async_remote_copy(
            src_ref=src, dst_ref=dst, send_sem=send, recv_sem=recv,
            device_id=axis, device_id_type=MESH,
        )

    own_g = pltpu.make_async_copy(g_ref, gbuf.at[pl.ds(pl.multiple_of(z * tz, 32), tz)], lsem.at[0])
    own_x = pltpu.make_async_copy(
        x_ref, xbuf.at[pl.ds(pl.multiple_of(TILE + w * tc, 32), tc)], lsem.at[1]
    )
    own_g.start()
    own_x.start()

    barrier = pltpu.get_barrier_semaphore()
    for d in range(1, nz):
        pl.semaphore_signal(barrier, inc=1, device_id={"row": z_at(d)}, device_id_type=MESH)
    for d in range(1, nw):
        pl.semaphore_signal(barrier, inc=1, device_id={"col": w_at(d)}, device_id_type=MESH)
    for d in range(1, ny):
        pl.semaphore_signal(barrier, inc=1, device_id={"dp": y_at(d)}, device_id_type=MESH)
    pl.semaphore_wait(barrier, nz + nw + ny - 3)

    def x_rows(owner):
        return xbuf.at[pl.ds(pl.multiple_of(TILE + owner * tc, 32), tc)]

    sibling = chip * 2 + 1 - core

    def x_first(d):
        to = sibling if d == 0 else lax.rem(chip + d, nx) * 2 + core
        return copy_to(x_ref, x_rows(w), xs.at[d], xr.at[d], col=to)

    def x_came(d):
        owner = sibling if d == 0 else lax.rem(chip + nx - d, nx) * 2 + core
        return copy_to(x_rows(owner), x_rows(owner), xs.at[d], xr.at[d], col=sibling)

    def x_forward(d):
        owner = lax.rem(chip + nx - d, nx) * 2 + core
        return copy_to(
            x_rows(owner), x_rows(owner), xs.at[nx - 1 + d], xr.at[nx - 1 + d], col=sibling
        )

    def x_forwarded(d):
        owner = lax.rem(chip + nx - d, nx) * 2 + 1 - core
        return copy_to(
            x_rows(owner), x_rows(owner), xs.at[nx - 1 + d], xr.at[nx - 1 + d], col=sibling
        )

    def ring(way, c, s, incoming=False):
        hop = s + 1 if incoming else s
        owner = z_at(nz - hop) if way == 0 else z_at(hop)
        first, count = 0, tz
        if s == steps - 1:
            first, count = (0, cut) if way == 0 else (cut, tz - cut)
        cols = pl.ds(pl.multiple_of(c * CHUNK, CHUNK), CHUNK)
        dst = gbuf.at[pl.ds(pl.multiple_of(owner * tz + first, 16), count), cols]
        src = g_ref.at[pl.ds(first, count), cols] if s == 0 and not incoming else dst
        to = z_at(1) if way == 0 else z_at(nz - 1)
        return copy_to(src, dst, rs.at[way, c, s], rr.at[way, c, s], row=to)

    def halo_copy(incoming=False):
        src = halo if incoming else g_ref.at[pl.ds(tz - TILE, TILE)]
        return copy_to(src, halo, hs.at[0], hs.at[1], row=z_at(1))

    def act_send(d):
        return copy_to(asend.at[d], abuf.at[d], asem.at[d], arec.at[d], row=z_at(d))

    def grad_send(j):
        return copy_to(bsend.at[j], bbuf.at[w], bsem.at[j], brec.at[w], col=j)

    def grad_came(owner):
        return copy_to(bbuf.at[owner], bbuf.at[owner], bsem.at[0], brec.at[owner], col=w_at(1))

    def weight_send(d):
        return copy_to(wloc.at[w], wloc.at[w], wsem.at[d], wrec.at[w], col=w_at(d))

    def weight_came(owner):
        return copy_to(wloc.at[owner], wloc.at[owner], wsem.at[1], wrec.at[owner], col=w_at(1))

    def slab_send(d):
        return copy_to(wall.at[z], wall.at[z], zsem.at[d], zrec.at[d], row=z_at(d))

    def slab_came(d):
        owner = z_at(nz - d)
        return copy_to(wall.at[owner], wall.at[owner], zsem.at[d], zrec.at[d], row=z_at(1))

    def sum_send(c, d):
        src = pbuf.at[c, pl.ds(pl.multiple_of(y_at(d) * part, part), part)]
        return copy_to(src, rbuf.at[c, d], ys.at[c, d], yr.at[c, d], dp=y_at(d))

    def out_rows(c, owner):
        return out_ref.at[
            pl.ds(pl.multiple_of(owner * part, part), part),
            pl.ds(pl.multiple_of(c * CHUNK, CHUNK), CHUNK),
        ]

    def out_send(c, d):
        return copy_to(qbuf.at[c], out_rows(c, y), qs.at[c, d], qr.at[c, d], dp=y_at(d))

    def out_came(c, d):
        owner = y_at(ny - d)
        return copy_to(out_rows(c, owner), out_rows(c, owner), qs.at[c, d], qr.at[c, d], dp=y_at(d))

    def out_own(c):
        return pltpu.make_async_copy(qbuf.at[c], out_rows(c, y), osem.at[c])

    def product(c):
        cols = pl.ds(pl.multiple_of(c * CHUNK, CHUNK), CHUNK)
        depth = tokens // 3 if tokens % (3 * LANES) == 0 else LANES
        for k in range(tokens // depth):
            at = pl.ds(k * depth, depth)
            term = jnp.dot(st[:, at], gbuf[at, cols], preferred_element_type=jnp.float32)
            pbuf[c] = term if k == 0 else pbuf[c] + term
        for d in range(1, ny):
            sum_send(c, d).start()

    def finish(c):
        for d in range(1, ny):
            sum_send(c, d).wait_recv()
        total = pbuf[c, pl.ds(pl.multiple_of(y * part, part), part)]
        for d in range(1, ny):
            total = total + rbuf[c, d]
        qbuf[c] = total
        for d in range(1, ny):
            out_send(c, d).start()
        out_own(c).start()

    def prepare():
        idcol[0:TILE] = jnp.full((TILE, LANES), -1.0, jnp.float32)
        xbuf[0:TILE] = jnp.zeros((TILE, xbuf.shape[1]), xbuf.dtype)
        lane = lax.broadcasted_iota(jnp.int32, (8, LANES), 1)
        none = jnp.full((8, LANES), -1.0, jnp.float32)
        flat = []
        for b in range(blocks):
            row = ids_ref[0:1, b * LANES : (b + 1) * LANES].astype(jnp.float32)
            flat.append(jnp.broadcast_to(row, (8, LANES)))
            idcol[TILE + b * LANES : TILE + (b + 1) * LANES] = jnp.broadcast_to(
                row, (LANES, LANES)
            ).T
        for b in range(blocks):
            before = flat[b - 1] if b > 0 else none
            after = flat[b + 1] if b < blocks - 1 else none
            rows[0, b] = flat[b]
            rows[1, b] = jnp.where(
                lane < TILE, after, jnp.where(lane >= LANES - TILE, before, none)
            )

    def grad_bands():
        own_g.wait()
        halo_copy(incoming=True).wait_recv()
        for j in range(tiles):
            first = pl.multiple_of(z * tz + j * TILE, 32)
            tile = gbuf[pl.ds(first, TILE)]
            before = halo[...] if j == 0 else gbuf[pl.ds(pl.multiple_of(first - TILE, 32), TILE)]
            bsend[j] = packed_band(tile, jnp.concatenate([before, tile], 0))
            @pl.when(w != j)
            def _():
                grad_send(j).start()

    def act_bands():
        own_x.wait()
        x_came(0).wait_recv()
        for d in range(1, nx):
            x_forwarded(d).wait_recv()

        @pl.when(w < tiles)
        def _():
            def one(d, carry):
                first = pl.multiple_of(z_at(d) * tz + w * TILE, 32)
                window = xbuf[pl.ds(first, 2 * TILE)]
                asend[d] = packed_band(window[TILE:], window)
                @pl.when(d > 0)
                def _():
                    act_send(d).start()
                return carry
            lax.fori_loop(0, nz, one, 0)

    def weights():
        @pl.when(w < tiles)
        def _():
            act = asend[0]
            for d in range(1, nz):
                act_send(d).wait_recv()
                act = act + abuf[d]
            bbuf[w] = bsend[w]
            for d in range(1, nw):
                grad_came(w_at(d)).wait_recv()
            grad = bbuf[0]
            for u in range(1, nw):
                grad = grad + bbuf[u]
            tile = z * tiles + w
            first = pl.multiple_of(tile * TILE, 32)
            near = idcol[pl.ds(first, 2 * TILE)]
            lane = lax.broadcasted_iota(jnp.int32, (16, LANES), 1)
            row = lax.broadcasted_iota(jnp.int32, (16, LANES), 0)
            mine = jnp.where(lane < 64, near[TILE : TILE + 16], near[TILE + 16 :])
            wide_lane = lax.broadcasted_iota(jnp.int32, (64, LANES), 1)
            wide_row = lax.broadcasted_iota(jnp.int32, (64, LANES), 0)
            window = jnp.sum(
                jnp.where(lax.rem(wide_lane, 64) == wide_row, near, 0.0), 0, keepdims=True
            )
            cross = lax.rem(lane, 64) < TILE
            factor = jnp.where(cross, jnp.where(tile > 0, 2.0, 0.0), 1.0)
            term = jnp.where(mine == window, act * grad * factor, 0.0)
            low = jnp.sum(jnp.where(lane < 64, term, 0.0), 1, keepdims=True)
            high = jnp.sum(jnp.where(lane < 64, 0.0, term), 1, keepdims=True)
            at = lax.rem(tile, LANES // TILE) * TILE
            spread = jnp.where(lane == row + at, low, 0.0) + jnp.where(
                lane == row + at + 16, high, 0.0
            )
            wloc[w] = jnp.broadcast_to(jnp.sum(spread, 0, keepdims=True), (8, LANES))
            for d in range(1, nw):
                weight_send(d).start()

    def slabs():
        for u in range(tiles):
            @pl.when(w != u)
            def _():
                weight_came(u).wait_recv()
        row = lax.broadcasted_iota(jnp.int32, (8, LANES), 0)
        slab = jnp.zeros((8, LANES), jnp.float32)
        for u in range(tiles):
            slab = slab + jnp.where(row == u, wloc[u], 0.0)
        wall[z] = slab
        for d in range(1, nz):
            slab_send(d).start()

    def scales():
        for d in range(1, nz):
            slab_came(d).wait_recv()
        lane = lax.broadcasted_iota(jnp.int32, (8, LANES), 1)
        none = jnp.zeros((8, LANES), jnp.float32)
        flat = []
        for b in range(blocks):
            row = none
            for k in range(b * (LANES // TILE), (b + 1) * (LANES // TILE)):
                owner, j = divmod(k, tiles)
                row = row + jnp.broadcast_to(wall[owner][j : j + 1], (8, LANES))
            flat.append(row)
        for b in range(blocks):
            before = flat[b - 1] if b > 0 else none
            after = flat[b + 1] if b < blocks - 1 else none
            rows[2, b] = flat[b]
            rows[3, b] = jnp.where(
                lane < TILE, after, jnp.where(lane >= LANES - TILE, before, none)
            )
        limit = clip_ref[0].astype(jnp.float32)

        def one(b, carry):
            at = pl.multiple_of(TILE + b * LANES, 32)
            ids = idcol[pl.ds(at, LANES)]
            near = jnp.where(ids == rows[0, b][0:1], rows[2, b][0:1], 0.0)
            near = near + jnp.where(ids == rows[1, b][0:1], rows[3, b][0:1], 0.0)
            squares = jnp.sum(near, 1, keepdims=True)
            factor = limit / jnp.maximum(jnp.sqrt(jnp.maximum(squares, 0.0)), limit)
            scaled = xbuf[pl.ds(at, LANES)].astype(jnp.float32) * factor
            st[:, pl.ds(pl.multiple_of(b * LANES, LANES), LANES)] = scaled.T.astype(st.dtype)
            return carry

        lax.fori_loop(0, blocks, one, 0)

    def forward_x():
        for d in range(1, nx):
            x_came(d).wait_recv()
            x_forward(d).start()

    extra = {
        (0, 0): prepare,
        (0, 1): grad_bands,
        (1, 0): forward_x,
        (1, 1): act_bands,
        (1, 2): weights,
        (1, 3): slabs,
        (2, 1): scales,
    }
    if skew < 4:
        extra = {(0, 0): prepare}

    def group(c, new, old, done, summed, at=None):
        for i in range(skew):
            for way in range(2):
                if old:
                    ring(way, c - 1, skew + i - 1, incoming=True).wait_recv()
                    ring(way, c - 1, skew + i).start()
                if new:
                    if i > 0:
                        ring(way, c, i - 1, incoming=True).wait_recv()
                    ring(way, c, i).start()
            if i == 0 and done:
                for way in range(2):
                    ring(way, c - 2, steps - 1, incoming=True).wait_recv()
            if i == 0 and summed:
                finish(c - 3)
            if at is not None and (at, i) in extra:
                extra[at, i]()
            if at is not None and skew < 4 and at == 1 and i == skew - 1:
                for step in (grad_bands, forward_x, act_bands, weights, slabs, scales):
                    step()
            if i == min(2, skew - 1) and done:
                product(c - 2)

    for d in range(nx):
        x_first(d).start()
    halo_copy().start()
    group(0, True, False, False, False, at=0)
    group(1, chunks > 1, True, False, False, at=1)
    if chunks > 2:
        group(2, True, True, True, False, at=2)

    def middle(c, carry):
        group(c, True, True, True, True)
        return carry

    lax.fori_loop(3, chunks, middle, 0)
    group(chunks, False, True, True, chunks > 2)
    for way in range(2):
        ring(way, chunks - 1, steps - 1, incoming=True).wait_recv()
    finish(chunks - 2)
    product(chunks - 1)
    finish(chunks - 1)

    def drain(c, carry):
        for s in range(steps):
            for way in range(2):
                ring(way, c, s).wait_send()
        for d in range(1, ny):
            sum_send(c, d).wait_send()
            out_send(c, d).wait_send()
            out_came(c, d).wait_recv()
        out_own(c).wait()
        return carry

    halo_copy().wait_send()
    for d in range(nx):
        x_first(d).wait_send()
    for d in range(1, nx):
        x_forward(d).wait_send()
    for d in range(1, nz):
        slab_send(d).wait_send()
    for j in range(tiles):
        @pl.when(w != j)
        def _():
            grad_send(j).wait_send()

    @pl.when(w < tiles)
    def _():
        for d in range(1, nz):
            act_send(d).wait_send()
        for d in range(1, nw):
            weight_send(d).wait_send()

    lax.fori_loop(0, chunks, drain, 0)


def body(sizes, activations, out_grads, query_ids, clip_bound):
    x_local = activations[0]
    g_local = out_grads[0]
    ny, nz, nw, tokens = sizes
    nx = nw // 2
    features, hidden = x_local.shape[1], g_local.shape[1]
    tiles = g_local.shape[0] // TILE
    chunks = hidden // CHUNK
    steps = nz // 2
    part = features // ny
    dma = pltpu.SemaphoreType.DMA
    f32, bf16 = jnp.float32, jnp.bfloat16
    return pl.pallas_call(
        functools.partial(kernel, sizes),
        out_shape=jax.ShapeDtypeStruct((features, hidden), f32),
        in_specs=[
            pl.BlockSpec(memory_space=pl.ANY),
            pl.BlockSpec(memory_space=pl.ANY),
            pl.BlockSpec(memory_space=pltpu.VMEM),
            pl.BlockSpec(memory_space=pltpu.SMEM),
        ],
        out_specs=pl.BlockSpec(memory_space=pl.ANY),
        scratch_shapes=[
            pltpu.VMEM((tokens, hidden), bf16),
            pltpu.VMEM((TILE + tokens, features), bf16),
            pltpu.VMEM((TILE, hidden), bf16),
            pltpu.VMEM((features, tokens), bf16),
            pltpu.VMEM((TILE + tokens, LANES), f32),
            pltpu.VMEM((4, tokens // LANES, 8, LANES), f32),
            pltpu.VMEM((nz, 16, LANES), f32),
            pltpu.VMEM((nz, 16, LANES), f32),
            pltpu.VMEM((tiles, 16, LANES), f32),
            pltpu.VMEM((nw, 16, LANES), f32),
            pltpu.VMEM((tiles, 8, LANES), f32),
            pltpu.VMEM((nz, 8, LANES), f32),
            pltpu.VMEM((chunks, features, CHUNK), f32),
            pltpu.VMEM((chunks, ny, part, CHUNK), f32),
            pltpu.VMEM((chunks, part, CHUNK), f32),
            dma((2,)), dma((chunks,)),
            dma((2 * nx,)), dma((2 * nx,)),
            dma((2,)),
            dma((2, chunks, steps)), dma((2, chunks, steps)),
            dma((nz,)), dma((nz,)),
            dma((tiles,)), dma((nw,)),
            dma((nw,)), dma((tiles,)),
            dma((nz,)), dma((nz,)),
            dma((chunks, ny)), dma((chunks, ny)),
            dma((chunks, ny)), dma((chunks, ny)),
        ],
        compiler_params=pltpu.CompilerParams(
            collective_id=0, has_side_effects=True, vmem_limit_bytes=48 * 1024 * 1024
        ),
        cost_estimate=pl.CostEstimate(
            flops=2 * tokens * features * hidden, bytes_accessed=1 << 23, transcendentals=0
        ),
    )(x_local, g_local, query_ids, clip_bound)


def solution(mesh):
    sizes = tuple(mesh.shape[a] for a in ("dp", "row", "col"))

    def run(activations, out_grads, query_ids, clip_bound):
        placed = (P("dp", "col", "row"), P("dp", "row", "col"), P("dp", None), P())
        return jax.shard_map(
            functools.partial(body, sizes + (query_ids.shape[1],)),
            mesh=mesh, in_specs=placed, out_specs=P("row", "col"), check_vma=False,
        )(activations, out_grads, query_ids, clip_bound)

    return run
```

```python
import functools

import jax
import jax.numpy as jnp
from jax import lax
from jax.experimental import pallas as pl
from jax.experimental.pallas import tpu as pltpu
from jax.sharding import PartitionSpec as P

TILE = 32
LANES = 128
CHUNK = 256
MESH = pl.DeviceIdType.MESH


def packed_band(tile, window):
    zeros = jnp.zeros_like(window)
    dims = (((1,), (1,)), ((), ()))
    low = lax.dot_general(
        tile[:16], jnp.concatenate([window, zeros], 0), dims, preferred_element_type=jnp.float32
    )
    high = lax.dot_general(
        tile[16:], jnp.concatenate([zeros, window], 0), dims, preferred_element_type=jnp.float32
    )
    return low + high


def kernel(
    sizes,
    x_ref, g_ref, ids_ref, clip_ref,
    out_ref,
    ids_vmem, gbuf, xbuf, halo, st, idcol, rows,
    asend, abuf, bsend, bbuf, wloc, wall,
    pbuf, rbuf, qbuf,
    lsem, osem, xs, xr, hs, rs, rr, asem, arec, bsem, brec, wsem, wrec, zsem, zrec, ys, yr, qs, qr,
):
    ny, nz, nw, tokens = sizes
    nx = nw // 2
    tz = g_ref.shape[0]
    tc = x_ref.shape[0]
    tiles = tz // TILE
    chunks = g_ref.shape[1] // CHUNK
    steps = nz // 2
    cut = tz // 2 - 16
    blocks = tokens // LANES
    part = x_ref.shape[1] // ny

    y = lax.axis_index("dp")
    z = lax.axis_index("row")
    w = lax.axis_index("col")
    core = lax.rem(w, 2)
    chip = w // 2

    def z_at(d):
        return lax.rem(z + d, nz)

    def w_at(d):
        return lax.rem(w + d, nw)

    def y_at(d):
        return lax.rem(y + d, ny)

    def copy_to(src, dst, send, recv, **axis):
        return pltpu.make_async_remote_copy(
            src_ref=src, dst_ref=dst, send_sem=send, recv_sem=recv,
            device_id=axis, device_id_type=MESH,
        )

    own_rows = pl.ds(pl.multiple_of(z * tz, 32), tz)
    own_g = [
        pltpu.make_async_copy(
            g_ref.at[:, pl.ds(c * CHUNK, CHUNK)], gbuf.at[c, own_rows], lsem.at[c]
        )
        for c in range(chunks)
    ]
    own_x = pltpu.make_async_copy(
        x_ref, xbuf.at[pl.ds(pl.multiple_of(TILE + w * tc, 32), tc)], lsem.at[chunks]
    )
    own_ids = pltpu.make_async_copy(ids_ref, ids_vmem, lsem.at[chunks + 1])
    for copy in own_g:
        copy.start()
    own_x.start()
    own_ids.start()

    barrier = pltpu.get_barrier_semaphore()
    for d in range(1, nz):
        pl.semaphore_signal(barrier, inc=1, device_id={"row": z_at(d)}, device_id_type=MESH)
    for d in range(1, nw):
        pl.semaphore_signal(barrier, inc=1, device_id={"col": w_at(d)}, device_id_type=MESH)
    for d in range(1, ny):
        pl.semaphore_signal(barrier, inc=1, device_id={"dp": y_at(d)}, device_id_type=MESH)
    pl.semaphore_wait(barrier, nz + nw + ny - 3)

    def x_rows(owner):
        return xbuf.at[pl.ds(pl.multiple_of(TILE + owner * tc, 32), tc)]

    sibling = chip * 2 + 1 - core

    def x_first(d):
        to = sibling if d == 0 else lax.rem(chip + d, nx) * 2 + core
        return copy_to(x_ref, x_rows(w), xs.at[d], xr.at[d], col=to)

    def x_came(d):
        owner = sibling if d == 0 else lax.rem(chip + nx - d, nx) * 2 + core
        return copy_to(x_rows(owner), x_rows(owner), xs.at[d], xr.at[d], col=sibling)

    def x_forward(d):
        owner = lax.rem(chip + nx - d, nx) * 2 + core
        return copy_to(
            x_rows(owner), x_rows(owner), xs.at[nx - 1 + d], xr.at[nx - 1 + d], col=sibling
        )

    def x_forwarded(d):
        owner = lax.rem(chip + nx - d, nx) * 2 + 1 - core
        return copy_to(
            x_rows(owner), x_rows(owner), xs.at[nx - 1 + d], xr.at[nx - 1 + d], col=sibling
        )

    def ring(way, c, s, incoming=False):
        hop = s + 1 if incoming else s
        owner = z_at(nz - hop) if way == 0 else z_at(hop)
        first, count = 0, tz
        if s == steps - 1:
            first, count = (0, cut) if way == 0 else (cut, tz - cut)
        block = gbuf.at[c, pl.ds(pl.multiple_of(owner * tz + first, 16), count)]
        to = z_at(1) if way == 0 else z_at(nz - 1)
        return copy_to(block, block, rs.at[way, c, s], rr.at[way, c, s], row=to)

    def halo_copy(incoming=False):
        last = pl.ds(pl.multiple_of(z * tz + tz - TILE, 32), TILE)
        src = halo if incoming else gbuf.at[:, last]
        return copy_to(src, halo, hs.at[0], hs.at[1], row=z_at(1))

    def act_send(d):
        return copy_to(asend.at[d], abuf.at[d], asem.at[d], arec.at[d], row=z_at(d))

    def grad_send(j):
        return copy_to(bsend.at[j], bbuf.at[w], bsem.at[j], brec.at[w], col=j)

    def grad_came(owner):
        return copy_to(bbuf.at[owner], bbuf.at[owner], bsem.at[0], brec.at[owner], col=w_at(1))

    def weight_send(d):
        return copy_to(wloc.at[w], wloc.at[w], wsem.at[d], wrec.at[w], col=w_at(d))

    def weight_came(owner):
        return copy_to(wloc.at[owner], wloc.at[owner], wsem.at[1], wrec.at[owner], col=w_at(1))

    def slab_send(d):
        return copy_to(wall.at[z], wall.at[z], zsem.at[d], zrec.at[d], row=z_at(d))

    def slab_came(d):
        owner = z_at(nz - d)
        return copy_to(wall.at[owner], wall.at[owner], zsem.at[d], zrec.at[d], row=z_at(1))

    def sum_send(c, d):
        src = pbuf.at[c, pl.ds(pl.multiple_of(y_at(d) * part, part), part)]
        return copy_to(src, rbuf.at[c, d], ys.at[c, d], yr.at[c, d], dp=y_at(d))

    def out_rows(c, owner):
        return out_ref.at[
            pl.ds(pl.multiple_of(owner * part, part), part),
            pl.ds(pl.multiple_of(c * CHUNK, CHUNK), CHUNK),
        ]

    def out_send(c, d):
        return copy_to(qbuf.at[c], out_rows(c, y), qs.at[c, d], qr.at[c, d], dp=y_at(d))

    def out_came(c, d):
        owner = y_at(ny - d)
        return copy_to(out_rows(c, owner), out_rows(c, owner), qs.at[c, d], qr.at[c, d], dp=y_at(d))

    def out_own(c):
        return pltpu.make_async_copy(qbuf.at[c], out_rows(c, y), osem.at[c])

    def product(c):
        depth = tokens // 3 if tokens % (3 * LANES) == 0 else LANES
        for k in range(tokens // depth):
            at = pl.ds(k * depth, depth)
            term = jnp.dot(st[:, at], gbuf[c, at], preferred_element_type=jnp.float32)
            pbuf[c] = term if k == 0 else pbuf[c] + term
        for d in range(1, ny):
            sum_send(c, d).start()

    def finish(c):
        for d in range(1, ny):
            sum_send(c, d).wait_recv()
        total = pbuf[c, pl.ds(pl.multiple_of(y * part, part), part)]
        for d in range(1, ny):
            total = total + rbuf[c, d]
        qbuf[c] = total
        for d in range(1, ny):
            out_send(c, d).start()
        out_own(c).start()

    def prepare():
        own_ids.wait()
        idcol[0:TILE] = jnp.full((TILE, LANES), -1.0, jnp.float32)
        xbuf[0:TILE] = jnp.zeros((TILE, xbuf.shape[1]), xbuf.dtype)
        lane = lax.broadcasted_iota(jnp.int32, (8, LANES), 1)
        none = jnp.full((8, LANES), -1.0, jnp.float32)
        flat = []
        for b in range(blocks):
            row = ids_vmem[0:1, b * LANES : (b + 1) * LANES].astype(jnp.float32)
            flat.append(jnp.broadcast_to(row, (8, LANES)))
            idcol[TILE + b * LANES : TILE + (b + 1) * LANES] = jnp.broadcast_to(
                row, (LANES, LANES)
            ).T
        for b in range(blocks):
            before = flat[b - 1] if b > 0 else none
            after = flat[b + 1] if b < blocks - 1 else none
            rows[0, b] = flat[b]
            rows[1, b] = jnp.where(
                lane < TILE, after, jnp.where(lane >= LANES - TILE, before, none)
            )

    def grad_bands():
        halo_copy(incoming=True).wait_recv()
        for j in range(tiles):
            first = pl.multiple_of(z * tz + j * TILE, 32)
            band = jnp.zeros((16, LANES), jnp.float32)
            for c in range(chunks):
                tile = gbuf[c, pl.ds(first, TILE)]
                before = pl.ds(pl.multiple_of(first - TILE, 32), TILE)
                before = halo[c] if j == 0 else gbuf[c, before]
                band = band + packed_band(tile, jnp.concatenate([before, tile], 0))
            bsend[j] = band
            @pl.when(w != j)
            def _():
                grad_send(j).start()

    def act_bands():
        x_came(0).wait_recv()
        for d in range(1, nx):
            x_forwarded(d).wait_recv()

        @pl.when(w < tiles)
        def _():
            def one(d, carry):
                first = pl.multiple_of(z_at(d) * tz + w * TILE, 32)
                window = xbuf[pl.ds(first, 2 * TILE)]
                asend[d] = packed_band(window[TILE:], window)
                @pl.when(d > 0)
                def _():
                    act_send(d).start()
                return carry
            lax.fori_loop(0, nz, one, 0)

    def weights():
        @pl.when(w < tiles)
        def _():
            act = asend[0]
            for d in range(1, nz):
                act_send(d).wait_recv()
                act = act + abuf[d]
            bbuf[w] = bsend[w]
            for d in range(1, nw):
                grad_came(w_at(d)).wait_recv()
            grad = bbuf[0]
            for u in range(1, nw):
                grad = grad + bbuf[u]
            tile = z * tiles + w
            first = pl.multiple_of(tile * TILE, 32)
            near = idcol[pl.ds(first, 2 * TILE)]
            lane = lax.broadcasted_iota(jnp.int32, (16, LANES), 1)
            row = lax.broadcasted_iota(jnp.int32, (16, LANES), 0)
            mine = jnp.where(lane < 64, near[TILE : TILE + 16], near[TILE + 16 :])
            wide_lane = lax.broadcasted_iota(jnp.int32, (64, LANES), 1)
            wide_row = lax.broadcasted_iota(jnp.int32, (64, LANES), 0)
            window = jnp.sum(
                jnp.where(lax.rem(wide_lane, 64) == wide_row, near, 0.0), 0, keepdims=True
            )
            cross = lax.rem(lane, 64) < TILE
            factor = jnp.where(cross, jnp.where(tile > 0, 2.0, 0.0), 1.0)
            term = jnp.where(mine == window, act * grad * factor, 0.0)
            low = jnp.sum(jnp.where(lane < 64, term, 0.0), 1, keepdims=True)
            high = jnp.sum(jnp.where(lane < 64, 0.0, term), 1, keepdims=True)
            at = lax.rem(tile, LANES // TILE) * TILE
            spread = jnp.where(lane == row + at, low, 0.0) + jnp.where(
                lane == row + at + 16, high, 0.0
            )
            wloc[w] = jnp.broadcast_to(jnp.sum(spread, 0, keepdims=True), (8, LANES))
            for d in range(1, nw):
                weight_send(d).start()

    def slabs():
        for u in range(tiles):
            @pl.when(w != u)
            def _():
                weight_came(u).wait_recv()
        row = lax.broadcasted_iota(jnp.int32, (8, LANES), 0)
        slab = jnp.zeros((8, LANES), jnp.float32)
        for u in range(tiles):
            slab = slab + jnp.where(row == u, wloc[u], 0.0)
        wall[z] = slab
        for d in range(1, nz):
            slab_send(d).start()

    def scales():
        for d in range(1, nz):
            slab_came(d).wait_recv()
        lane = lax.broadcasted_iota(jnp.int32, (8, LANES), 1)
        none = jnp.zeros((8, LANES), jnp.float32)
        flat = []
        for b in range(blocks):
            row = none
            for k in range(b * (LANES // TILE), (b + 1) * (LANES // TILE)):
                owner, j = divmod(k, tiles)
                row = row + jnp.broadcast_to(wall[owner][j : j + 1], (8, LANES))
            flat.append(row)
        for b in range(blocks):
            before = flat[b - 1] if b > 0 else none
            after = flat[b + 1] if b < blocks - 1 else none
            rows[2, b] = flat[b]
            rows[3, b] = jnp.where(
                lane < TILE, after, jnp.where(lane >= LANES - TILE, before, none)
            )
        limit = clip_ref[0].astype(jnp.float32)

        def one(b, carry):
            at = pl.multiple_of(TILE + b * LANES, 32)
            ids = idcol[pl.ds(at, LANES)]
            near = jnp.where(ids == rows[0, b][0:1], rows[2, b][0:1], 0.0)
            near = near + jnp.where(ids == rows[1, b][0:1], rows[3, b][0:1], 0.0)
            squares = jnp.sum(near, 1, keepdims=True)
            factor = limit / jnp.maximum(jnp.sqrt(jnp.maximum(squares, 0.0)), limit)
            scaled = xbuf[pl.ds(at, LANES)].astype(jnp.float32) * factor
            st[:, pl.ds(pl.multiple_of(b * LANES, LANES), LANES)] = scaled.T.astype(st.dtype)
            return carry

        lax.fori_loop(0, blocks, one, 0)

    def forward_x():
        for d in range(1, nx):
            x_came(d).wait_recv()
            x_forward(d).start()

    extra = {
        0: prepare, 1: grad_bands, 2: forward_x, 3: act_bands, 4: weights, 5: slabs, 6: scales
    }
    if steps < 7:
        def every():
            for step in range(7):
                extra_steps[step]()
        extra_steps, extra = extra, {0: every}

    def ring_sent(c):
        for s in range(steps):
            for way in range(2):
                ring(way, c, s).wait_send()

    def out_done(c):
        for d in range(1, ny):
            sum_send(c, d).wait_send()
            out_send(c, d).wait_send()
            out_came(c, d).wait_recv()
        out_own(c).wait()

    own_x.wait()
    for d in range(nx):
        x_first(d).start()
    for copy in own_g:
        copy.wait()

    for t in range(steps + chunks - 1):
        for c in range(chunks):
            s = t - c
            if 0 <= s < steps:
                for way in range(2):
                    if s > 0:
                        ring(way, c, s - 1, incoming=True).wait_recv()
                    ring(way, c, s).start()
        if t == 0:
            halo_copy().start()
        if t in extra:
            extra[t]()
        c = t - steps
        if c >= 0:
            for way in range(2):
                ring(way, c, steps - 1, incoming=True).wait_recv()
            if c > 0:
                finish(c - 1)
            product(c)
            ring_sent(c)
            if c > 2:
                out_done(c - 3)

    halo_copy().wait_send()
    for d in range(nx):
        x_first(d).wait_send()
    for d in range(1, nx):
        x_forward(d).wait_send()
    for d in range(1, nz):
        slab_send(d).wait_send()
    for j in range(tiles):
        @pl.when(w != j)
        def _():
            grad_send(j).wait_send()

    @pl.when(w < tiles)
    def _():
        for d in range(1, nz):
            act_send(d).wait_send()
        for d in range(1, nw):
            weight_send(d).wait_send()

    for way in range(2):
        ring(way, chunks - 1, steps - 1, incoming=True).wait_recv()
    finish(chunks - 2)
    product(chunks - 1)
    ring_sent(chunks - 1)
    finish(chunks - 1)
    for c in range(max(chunks - 4, 0), chunks):
        out_done(c)


def body(sizes, activations, out_grads, query_ids, clip_bound):
    x_local = activations[0]
    g_local = out_grads[0]
    ny, nz, nw, tokens = sizes
    nx = nw // 2
    features, hidden = x_local.shape[1], g_local.shape[1]
    tiles = g_local.shape[0] // TILE
    chunks = hidden // CHUNK
    steps = nz // 2
    part = features // ny
    dma = pltpu.SemaphoreType.DMA
    f32, bf16 = jnp.float32, jnp.bfloat16
    return pl.pallas_call(
        functools.partial(kernel, sizes),
        out_shape=jax.ShapeDtypeStruct((features, hidden), f32),
        in_specs=[
            pl.BlockSpec(memory_space=pltpu.HBM),
            pl.BlockSpec(memory_space=pltpu.HBM),
            pl.BlockSpec(memory_space=pltpu.HBM),
            pl.BlockSpec(memory_space=pltpu.SMEM),
        ],
        out_specs=pl.BlockSpec(memory_space=pl.ANY),
        scratch_shapes=[
            pltpu.VMEM((1, tokens), jnp.int32),
            pltpu.VMEM((chunks, tokens, CHUNK), bf16),
            pltpu.VMEM((TILE + tokens, features), bf16),
            pltpu.VMEM((chunks, TILE, CHUNK), bf16),
            pltpu.VMEM((features, tokens), bf16),
            pltpu.VMEM((TILE + tokens, LANES), f32),
            pltpu.VMEM((4, tokens // LANES, 8, LANES), f32),
            pltpu.VMEM((nz, 16, LANES), f32),
            pltpu.VMEM((nz, 16, LANES), f32),
            pltpu.VMEM((tiles, 16, LANES), f32),
            pltpu.VMEM((nw, 16, LANES), f32),
            pltpu.VMEM((tiles, 8, LANES), f32),
            pltpu.VMEM((nz, 8, LANES), f32),
            pltpu.VMEM((chunks, features, CHUNK), f32),
            pltpu.VMEM((chunks, ny, part, CHUNK), f32),
            pltpu.VMEM((chunks, part, CHUNK), f32),
            dma((chunks + 2,)), dma((chunks,)),
            dma((2 * nx,)), dma((2 * nx,)),
            dma((2,)),
            dma((2, chunks, steps)), dma((2, chunks, steps)),
            dma((nz,)), dma((nz,)),
            dma((tiles,)), dma((nw,)),
            dma((nw,)), dma((tiles,)),
            dma((nz,)), dma((nz,)),
            dma((chunks, ny)), dma((chunks, ny)),
            dma((chunks, ny)), dma((chunks, ny)),
        ],
        compiler_params=pltpu.CompilerParams(
            collective_id=0, has_side_effects=True, vmem_limit_bytes=48 * 1024 * 1024
        ),
        cost_estimate=pl.CostEstimate(
            flops=2 * tokens * features * hidden, bytes_accessed=1 << 23, transcendentals=0
        ),
    )(x_local, g_local, query_ids, clip_bound)


def solution(mesh):
    sizes = tuple(mesh.shape[a] for a in ("dp", "row", "col"))

    def run(activations, out_grads, query_ids, clip_bound):
        placed = (P("dp", "col", "row"), P("dp", "row", "col"), P("dp", None), P())
        return jax.shard_map(
            functools.partial(body, sizes + (query_ids.shape[1],)),
            mesh=mesh, in_specs=placed, out_specs=P("row", "col"), check_vma=False,
        )(activations, out_grads, query_ids, clip_bound)

    return run
```

```python
import functools

import jax
import jax.numpy as jnp
from jax import lax
from jax.experimental import pallas as pl
from jax.experimental.pallas import tpu as pltpu
from jax.sharding import PartitionSpec as P

TILE = 32
LANES = 128
CHUNK = 256
MESH = pl.DeviceIdType.MESH


def packed_band(tile, window):
    zeros = jnp.zeros_like(window)
    dims = (((1,), (1,)), ((), ()))
    low = lax.dot_general(
        tile[:16], jnp.concatenate([window, zeros], 0), dims, preferred_element_type=jnp.float32
    )
    high = lax.dot_general(
        tile[16:], jnp.concatenate([zeros, window], 0), dims, preferred_element_type=jnp.float32
    )
    return low + high


def kernel(
    sizes,
    x_ref, g_ref, ids_ref, clip_ref,
    out_ref,
    ids_vmem, near, gbuf, xbuf, halo, st, idcol, rows,
    asend, abuf, bsend, bbuf, wloc, wall,
    pbuf, rbuf, qbuf,
    lsem, osem, xs, xr, hs, rs, rr, asem, arec, bsem, brec, wsem, wrec, zsem, zrec, ys, yr, qs, qr,
):
    ny, nz, nw, tokens = sizes
    nx = nw // 2
    tz = g_ref.shape[0]
    tc = x_ref.shape[0]
    tiles = tz // TILE
    chunks = g_ref.shape[1] // CHUNK
    steps = nz // 2
    wide = near.shape[1]
    cut = tz // 2 - 16
    blocks = tokens // LANES
    part = x_ref.shape[1] // ny

    y = lax.axis_index("dp")
    z = lax.axis_index("row")
    w = lax.axis_index("col")
    core = lax.rem(w, 2)
    chip = w // 2

    def z_at(d):
        return lax.rem(z + d, nz)

    def w_at(d):
        return lax.rem(w + d, nw)

    def y_at(d):
        return lax.rem(y + d, ny)

    def copy_to(src, dst, send, recv, **axis):
        return pltpu.make_async_remote_copy(
            src_ref=src, dst_ref=dst, send_sem=send, recv_sem=recv,
            device_id=axis, device_id_type=MESH,
        )

    own_rows = pl.ds(pl.multiple_of(z * tz, 32), tz)
    own_g = [
        pltpu.make_async_copy(
            g_ref.at[:, pl.ds(c * CHUNK, CHUNK)], gbuf.at[c, own_rows], lsem.at[c]
        )
        for c in range(chunks)
    ]
    own_x = pltpu.make_async_copy(
        x_ref, xbuf.at[pl.ds(pl.multiple_of(TILE + w * tc, 32), tc)], lsem.at[chunks]
    )
    own_ids = pltpu.make_async_copy(ids_ref, ids_vmem, lsem.at[chunks + 1])
    for copy in own_g:
        copy.start()
    own_x.start()
    own_ids.start()

    barrier = pltpu.get_barrier_semaphore()
    for d in range(1, nz):
        pl.semaphore_signal(barrier, inc=1, device_id={"row": z_at(d)}, device_id_type=MESH)
    for d in range(1, nw):
        pl.semaphore_signal(barrier, inc=1, device_id={"col": w_at(d)}, device_id_type=MESH)
    for d in range(1, ny):
        pl.semaphore_signal(barrier, inc=1, device_id={"dp": y_at(d)}, device_id_type=MESH)
    pl.semaphore_wait(barrier, nz + nw + ny - 3)

    def x_rows(owner):
        return xbuf.at[pl.ds(pl.multiple_of(TILE + owner * tc, 32), tc)]

    sibling = chip * 2 + 1 - core

    def x_first(d):
        to = sibling if d == 0 else lax.rem(chip + d, nx) * 2 + core
        return copy_to(x_ref, x_rows(w), xs.at[d], xr.at[d], col=to)

    def x_came(d):
        owner = sibling if d == 0 else lax.rem(chip + nx - d, nx) * 2 + core
        return copy_to(x_rows(owner), x_rows(owner), xs.at[d], xr.at[d], col=sibling)

    def x_forward(d):
        owner = lax.rem(chip + nx - d, nx) * 2 + core
        return copy_to(
            x_rows(owner), x_rows(owner), xs.at[nx - 1 + d], xr.at[nx - 1 + d], col=sibling
        )

    def x_forwarded(d):
        owner = lax.rem(chip + nx - d, nx) * 2 + 1 - core
        return copy_to(
            x_rows(owner), x_rows(owner), xs.at[nx - 1 + d], xr.at[nx - 1 + d], col=sibling
        )

    def ring(way, c, s, incoming=False):
        hop = s + 1 if incoming else s
        owner = z_at(nz - hop) if way == 0 else z_at(hop)
        first, count = 0, tz
        if s == steps - 1:
            first, count = (0, cut) if way == 0 else (cut, tz - cut)
        block = gbuf.at[c, pl.ds(pl.multiple_of(owner * tz + first, 16), count)]
        to = z_at(1) if way == 0 else z_at(nz - 1)
        return copy_to(block, block, rs.at[way, c, s], rr.at[way, c, s], row=to)

    def halo_copy(incoming=False):
        last = pl.ds(pl.multiple_of(z * tz + tz - TILE, 32), TILE)
        src = halo if incoming else gbuf.at[:, last]
        return copy_to(src, halo, hs.at[0], hs.at[1], row=z_at(1))

    def act_send(d):
        return copy_to(asend.at[d], abuf.at[d], asem.at[d], arec.at[d], row=z_at(d))

    def grad_send(j):
        return copy_to(bsend.at[j], bbuf.at[w], bsem.at[j], brec.at[w], col=j)

    def grad_came(owner):
        return copy_to(bbuf.at[owner], bbuf.at[owner], bsem.at[0], brec.at[owner], col=w_at(1))

    def weight_send(d):
        return copy_to(wloc.at[w], wloc.at[w], wsem.at[d], wrec.at[w], col=w_at(d))

    def weight_came(owner):
        return copy_to(wloc.at[owner], wloc.at[owner], wsem.at[1], wrec.at[owner], col=w_at(1))

    def slab_send(d):
        return copy_to(wall.at[z], wall.at[z], zsem.at[d], zrec.at[d], row=z_at(d))

    def slab_came(d):
        owner = z_at(nz - d)
        return copy_to(wall.at[owner], wall.at[owner], zsem.at[d], zrec.at[d], row=z_at(1))

    def sum_send(c, d):
        src = pbuf.at[c, pl.ds(pl.multiple_of(y_at(d) * part, part), part)]
        return copy_to(src, rbuf.at[c, d], ys.at[c, d], yr.at[c, d], dp=y_at(d))

    def out_rows(c, owner):
        return out_ref.at[
            pl.ds(pl.multiple_of(owner * part, part), part),
            pl.ds(pl.multiple_of(c * CHUNK, CHUNK), CHUNK),
        ]

    def out_send(c, d):
        return copy_to(qbuf.at[c], out_rows(c, y), qs.at[c, d], qr.at[c, d], dp=y_at(d))

    def out_came(c, d):
        owner = y_at(ny - d)
        return copy_to(out_rows(c, owner), out_rows(c, owner), qs.at[c, d], qr.at[c, d], dp=y_at(d))

    def out_own(c):
        return pltpu.make_async_copy(qbuf.at[c], out_rows(c, y), osem.at[c])

    def product(c):
        depth = tokens // 3 if tokens % (3 * LANES) == 0 else LANES
        for k in range(tokens // depth):
            at = pl.ds(k * depth, depth)
            term = jnp.dot(st[:, at], gbuf[c, at], preferred_element_type=jnp.float32)
            pbuf[c] = term if k == 0 else pbuf[c] + term
        for d in range(1, ny):
            sum_send(c, d).start()

    def finish(c):
        for d in range(1, ny):
            sum_send(c, d).wait_recv()
        total = pbuf[c, pl.ds(pl.multiple_of(y * part, part), part)]
        for d in range(1, ny):
            total = total + rbuf[c, d]
        qbuf[c] = total
        for d in range(1, ny):
            out_send(c, d).start()
        out_own(c).start()

    def prepare():
        own_ids.wait()
        idcol[0:TILE] = jnp.full((TILE, LANES), -1.0, jnp.float32)
        xbuf[0:TILE] = jnp.zeros((TILE, xbuf.shape[1]), xbuf.dtype)
        lane = lax.broadcasted_iota(jnp.int32, (8, LANES), 1)
        none = jnp.full((8, LANES), -1.0, jnp.float32)
        flat = []
        for b in range(blocks):
            row = ids_vmem[0:1, b * LANES : (b + 1) * LANES].astype(jnp.float32)
            flat.append(jnp.broadcast_to(row, (8, LANES)))
            idcol[TILE + b * LANES : TILE + (b + 1) * LANES] = jnp.broadcast_to(
                row, (LANES, LANES)
            ).T
        for b in range(blocks):
            before = flat[b - 1] if b > 0 else none
            after = flat[b + 1] if b < blocks - 1 else none
            rows[0, b] = flat[b]
            rows[1, b] = jnp.where(
                lane < TILE, after, jnp.where(lane >= LANES - TILE, before, none)
            )

    def grad_bands():
        halo_copy(incoming=True).wait_recv()
        pad = jnp.zeros((wide - tz - TILE, CHUNK), gbuf.dtype)
        dims = (((1,), (1,)), ((), ()))
        band = jnp.zeros((tz, wide), jnp.float32)
        for c in range(chunks):
            own = gbuf[c, own_rows]
            window = jnp.concatenate([halo[c], own, pad], 0)
            band = band + lax.dot_general(own, window, dims, preferred_element_type=jnp.float32)
        near[...] = band
        lane = lax.broadcasted_iota(jnp.int32, (16, LANES), 1)
        for j in range(tiles):
            turned = near[j * TILE : (j + 1) * TILE]
            if j > 0:
                turned = pltpu.roll(turned, wide - j * TILE, 1)
            turned = turned[:, :LANES]
            bsend[j] = jnp.where(lane < 64, turned[:16], pltpu.roll(turned[16:], 64, 1))
            @pl.when(w != j)
            def _():
                grad_send(j).start()

    def act_bands():
        x_came(0).wait_recv()
        for d in range(1, nx):
            x_forwarded(d).wait_recv()

        @pl.when(w < tiles)
        def _():
            def one(d, carry):
                first = pl.multiple_of(z_at(d) * tz + w * TILE, 32)
                window = xbuf[pl.ds(first, 2 * TILE)]
                asend[d] = packed_band(window[TILE:], window)
                @pl.when(d > 0)
                def _():
                    act_send(d).start()
                return carry
            lax.fori_loop(0, nz, one, 0)

    def weights():
        @pl.when(w < tiles)
        def _():
            act = asend[0]
            for d in range(1, nz):
                act_send(d).wait_recv()
                act = act + abuf[d]
            bbuf[w] = bsend[w]
            for d in range(1, nw):
                grad_came(w_at(d)).wait_recv()
            grad = bbuf[0]
            for u in range(1, nw):
                grad = grad + bbuf[u]
            tile = z * tiles + w
            first = pl.multiple_of(tile * TILE, 32)
            ids = idcol[pl.ds(first, 2 * TILE)]
            lane = lax.broadcasted_iota(jnp.int32, (16, LANES), 1)
            row = lax.broadcasted_iota(jnp.int32, (16, LANES), 0)
            mine = jnp.where(lane < 64, ids[TILE : TILE + 16], ids[TILE + 16 :])
            wide_lane = lax.broadcasted_iota(jnp.int32, (64, LANES), 1)
            wide_row = lax.broadcasted_iota(jnp.int32, (64, LANES), 0)
            window = jnp.sum(
                jnp.where(lax.rem(wide_lane, 64) == wide_row, ids, 0.0), 0, keepdims=True
            )
            cross = lax.rem(lane, 64) < TILE
            factor = jnp.where(cross, jnp.where(tile > 0, 2.0, 0.0), 1.0)
            term = jnp.where(mine == window, act * grad * factor, 0.0)
            low = jnp.sum(jnp.where(lane < 64, term, 0.0), 1, keepdims=True)
            high = jnp.sum(jnp.where(lane < 64, 0.0, term), 1, keepdims=True)
            at = lax.rem(tile, LANES // TILE) * TILE
            spread = jnp.where(lane == row + at, low, 0.0) + jnp.where(
                lane == row + at + 16, high, 0.0
            )
            wloc[w] = jnp.broadcast_to(jnp.sum(spread, 0, keepdims=True), (8, LANES))
            for d in range(1, nw):
                weight_send(d).start()

    def slabs():
        for u in range(tiles):
            @pl.when(w != u)
            def _():
                weight_came(u).wait_recv()
        row = lax.broadcasted_iota(jnp.int32, (8, LANES), 0)
        slab = jnp.zeros((8, LANES), jnp.float32)
        for u in range(tiles):
            slab = slab + jnp.where(row == u, wloc[u], 0.0)
        wall[z] = slab
        for d in range(1, nz):
            slab_send(d).start()

    def scales():
        for d in range(1, nz):
            slab_came(d).wait_recv()
        lane = lax.broadcasted_iota(jnp.int32, (8, LANES), 1)
        none = jnp.zeros((8, LANES), jnp.float32)
        flat = []
        for b in range(blocks):
            row = none
            for k in range(b * (LANES // TILE), (b + 1) * (LANES // TILE)):
                owner, j = divmod(k, tiles)
                row = row + jnp.broadcast_to(wall[owner][j : j + 1], (8, LANES))
            flat.append(row)
        for b in range(blocks):
            before = flat[b - 1] if b > 0 else none
            after = flat[b + 1] if b < blocks - 1 else none
            rows[2, b] = flat[b]
            rows[3, b] = jnp.where(
                lane < TILE, after, jnp.where(lane >= LANES - TILE, before, none)
            )
        limit = clip_ref[0].astype(jnp.float32)

        def one(b, carry):
            at = pl.multiple_of(TILE + b * LANES, 32)
            ids = idcol[pl.ds(at, LANES)]
            found = jnp.where(ids == rows[0, b][0:1], rows[2, b][0:1], 0.0)
            found = found + jnp.where(ids == rows[1, b][0:1], rows[3, b][0:1], 0.0)
            squares = jnp.sum(found, 1, keepdims=True)
            factor = limit / jnp.maximum(jnp.sqrt(jnp.maximum(squares, 0.0)), limit)
            scaled = xbuf[pl.ds(at, LANES)].astype(jnp.float32) * factor
            st[:, pl.ds(pl.multiple_of(b * LANES, LANES), LANES)] = scaled.T.astype(st.dtype)
            return carry

        lax.fori_loop(0, blocks, one, 0)

    def forward_x():
        for d in range(1, nx):
            x_came(d).wait_recv()
            x_forward(d).start()

    first_slot = [0, 0, 1, 1, 2, 3, 4][:chunks]
    final_slot = first_slot[-1] + steps
    between = {0: (prepare,), 1: (grad_bands,), 2: (forward_x, act_bands), 3: (weights,),
               4: (slabs,), 5: (scales,)}
    if steps < 6:
        between = {0: sum(between.values(), ())}

    def ring_sent(c):
        for s in range(steps):
            for way in range(2):
                ring(way, c, s).wait_send()

    def out_done(c):
        for d in range(1, ny):
            sum_send(c, d).wait_send()
            out_send(c, d).wait_send()
            out_came(c, d).wait_recv()
        out_own(c).wait()

    own_x.wait()
    for d in range(nx):
        x_first(d).start()
    for copy in own_g:
        copy.wait()

    def hop(t, c):
        s = t - first_slot[c]
        if 0 <= s < steps:
            for way in range(2):
                if s > 0:
                    ring(way, c, s - 1, incoming=True).wait_recv()
                ring(way, c, s).start()

    def after(t):
        for c in range(chunks):
            if t == first_slot[c] + steps + 1 and c < chunks - 1:
                finish(c)
        for c in range(chunks):
            if t == first_slot[c] + steps:
                for way in range(2):
                    ring(way, c, steps - 1, incoming=True).wait_recv()
                product(c)
                ring_sent(c)
        for c in range(chunks):
            if t == first_slot[c] + steps + 3:
                out_done(c)

    for t in range(final_slot):
        for c in range(0, chunks, 2):
            hop(t, c)
        if t == 0:
            halo_copy().start()
        for step in between.get(t, ()):
            step()
        for c in range(1, chunks, 2):
            hop(t, c)
        after(t)

    halo_copy().wait_send()
    for d in range(nx):
        x_first(d).wait_send()
    for d in range(1, nx):
        x_forward(d).wait_send()
    for d in range(1, nz):
        slab_send(d).wait_send()
    for j in range(tiles):
        @pl.when(w != j)
        def _():
            grad_send(j).wait_send()

    @pl.when(w < tiles)
    def _():
        for d in range(1, nz):
            act_send(d).wait_send()
        for d in range(1, nw):
            weight_send(d).wait_send()

    after(final_slot)
    finish(chunks - 1)
    for c in range(chunks):
        if first_slot[c] + steps + 3 > final_slot:
            out_done(c)


def body(sizes, activations, out_grads, query_ids, clip_bound):
    x_local = activations[0]
    g_local = out_grads[0]
    ny, nz, nw, tokens = sizes
    nx = nw // 2
    features, hidden = x_local.shape[1], g_local.shape[1]
    tz = g_local.shape[0]
    tiles = tz // TILE
    chunks = hidden // CHUNK
    steps = nz // 2
    part = features // ny
    dma = pltpu.SemaphoreType.DMA
    f32, bf16 = jnp.float32, jnp.bfloat16
    return pl.pallas_call(
        functools.partial(kernel, sizes),
        out_shape=jax.ShapeDtypeStruct((features, hidden), f32),
        in_specs=[
            pl.BlockSpec(memory_space=pltpu.HBM),
            pl.BlockSpec(memory_space=pltpu.HBM),
            pl.BlockSpec(memory_space=pltpu.HBM),
            pl.BlockSpec(memory_space=pltpu.SMEM),
        ],
        out_specs=pl.BlockSpec(memory_space=pl.ANY),
        scratch_shapes=[
            pltpu.VMEM((1, tokens), jnp.int32),
            pltpu.VMEM((tz, -(-(tz + TILE) // LANES) * LANES), f32),
            pltpu.VMEM((chunks, tokens, CHUNK), bf16),
            pltpu.VMEM((TILE + tokens, features), bf16),
            pltpu.VMEM((chunks, TILE, CHUNK), bf16),
            pltpu.VMEM((features, tokens), bf16),
            pltpu.VMEM((TILE + tokens, LANES), f32),
            pltpu.VMEM((4, tokens // LANES, 8, LANES), f32),
            pltpu.VMEM((nz, 16, LANES), f32),
            pltpu.VMEM((nz, 16, LANES), f32),
            pltpu.VMEM((tiles, 16, LANES), f32),
            pltpu.VMEM((nw, 16, LANES), f32),
            pltpu.VMEM((tiles, 8, LANES), f32),
            pltpu.VMEM((nz, 8, LANES), f32),
            pltpu.VMEM((chunks, features, CHUNK), f32),
            pltpu.VMEM((chunks, ny, part, CHUNK), f32),
            pltpu.VMEM((chunks, part, CHUNK), f32),
            dma((chunks + 2,)), dma((chunks,)),
            dma((2 * nx,)), dma((2 * nx,)),
            dma((2,)),
            dma((2, chunks, steps)), dma((2, chunks, steps)),
            dma((nz,)), dma((nz,)),
            dma((tiles,)), dma((nw,)),
            dma((nw,)), dma((tiles,)),
            dma((nz,)), dma((nz,)),
            dma((chunks, ny)), dma((chunks, ny)),
            dma((chunks, ny)), dma((chunks, ny)),
        ],
        compiler_params=pltpu.CompilerParams(
            collective_id=0, has_side_effects=True, vmem_limit_bytes=63 * 1024 * 1024
        ),
        cost_estimate=pl.CostEstimate(
            flops=2 * tokens * features * hidden, bytes_accessed=1 << 23, transcendentals=0
        ),
    )(x_local, g_local, query_ids, clip_bound)


def solution(mesh):
    sizes = tuple(mesh.shape[a] for a in ("dp", "row", "col"))

    def run(activations, out_grads, query_ids, clip_bound):
        placed = (P("dp", "col", "row"), P("dp", "row", "col"), P("dp", None), P())
        return jax.shard_map(
            functools.partial(body, sizes + (query_ids.shape[1],)),
            mesh=mesh, in_specs=placed, out_specs=P("row", "col"), check_vma=False,
        )(activations, out_grads, query_ids, clip_bound)

    return run
```

```python
import functools

import jax
import jax.numpy as jnp
from jax import lax
from jax.experimental import pallas as pl
from jax.experimental.pallas import tpu as pltpu
from jax.sharding import PartitionSpec as P

TILE = 32
LANES = 128
CHUNK = 256
MESH = pl.DeviceIdType.MESH


def packed_band(tile, window):
    zeros = jnp.zeros_like(window)
    dims = (((1,), (1,)), ((), ()))
    low = lax.dot_general(
        tile[:16], jnp.concatenate([window, zeros], 0), dims, preferred_element_type=jnp.float32
    )
    high = lax.dot_general(
        tile[16:], jnp.concatenate([zeros, window], 0), dims, preferred_element_type=jnp.float32
    )
    return low + high


def kernel(
    sizes,
    x_ref, g_ref, ids_ref, clip_ref,
    out_ref,
    ids_vmem, bands, gbuf, xbuf, halo, st, idcol, rows,
    asend, abuf, bsend, bbuf, wloc, wall,
    pbuf, rfar, rnear, qbuf,
    lsem, osem, xs, xr, hs, rs, rr, asem, arec, bsem, brec, wsem, wrec, zsem, zrec,
    s1, r1, s2, r2, s3, r3, s4, r4,
):
    ny, nz, nw, tokens = sizes
    nx = nw // 2
    tz = g_ref.shape[0]
    tc = x_ref.shape[0]
    tiles = tz // TILE
    chunks = g_ref.shape[1] // CHUNK
    steps = nz // 2
    wide = bands.shape[1]
    cut = tz // 2 - 16
    blocks = tokens // LANES
    part = x_ref.shape[1] // ny

    y = lax.axis_index("dp")
    z = lax.axis_index("row")
    w = lax.axis_index("col")
    core = lax.rem(w, 2)
    chip = w // 2

    def z_at(d):
        return lax.rem(z + d, nz)

    def w_at(d):
        return lax.rem(w + d, nw)

    def y_at(d):
        return lax.rem(y + d, ny)

    def copy_to(src, dst, send, recv, **axis):
        return pltpu.make_async_remote_copy(
            src_ref=src, dst_ref=dst, send_sem=send, recv_sem=recv,
            device_id=axis, device_id_type=MESH,
        )

    own_rows = pl.ds(pl.multiple_of(z * tz, 32), tz)
    own_g = [
        pltpu.make_async_copy(
            g_ref.at[:, pl.ds(c * CHUNK, CHUNK)], gbuf.at[c, own_rows], lsem.at[c]
        )
        for c in range(chunks)
    ]
    own_x = pltpu.make_async_copy(
        x_ref, xbuf.at[pl.ds(pl.multiple_of(TILE + w * tc, 32), tc)], lsem.at[chunks]
    )
    own_ids = pltpu.make_async_copy(ids_ref, ids_vmem, lsem.at[chunks + 1])
    for copy in own_g:
        copy.start()
    own_x.start()
    own_ids.start()

    barrier = pltpu.get_barrier_semaphore()
    for d in range(1, nz):
        pl.semaphore_signal(barrier, inc=1, device_id={"row": z_at(d)}, device_id_type=MESH)
    for d in range(1, nw):
        pl.semaphore_signal(barrier, inc=1, device_id={"col": w_at(d)}, device_id_type=MESH)
    for d in range(1, ny):
        pl.semaphore_signal(barrier, inc=1, device_id={"dp": y_at(d)}, device_id_type=MESH)
    pl.semaphore_wait(barrier, nz + nw + ny - 3)

    def x_rows(owner):
        return xbuf.at[pl.ds(pl.multiple_of(TILE + owner * tc, 32), tc)]

    sibling = chip * 2 + 1 - core

    def x_first(d):
        to = sibling if d == 0 else lax.rem(chip + d, nx) * 2 + core
        return copy_to(x_ref, x_rows(w), xs.at[d], xr.at[d], col=to)

    def x_came(d):
        owner = sibling if d == 0 else lax.rem(chip + nx - d, nx) * 2 + core
        return copy_to(x_rows(owner), x_rows(owner), xs.at[d], xr.at[d], col=sibling)

    def x_forward(d):
        owner = lax.rem(chip + nx - d, nx) * 2 + core
        return copy_to(
            x_rows(owner), x_rows(owner), xs.at[nx - 1 + d], xr.at[nx - 1 + d], col=sibling
        )

    def x_forwarded(d):
        owner = lax.rem(chip + nx - d, nx) * 2 + 1 - core
        return copy_to(
            x_rows(owner), x_rows(owner), xs.at[nx - 1 + d], xr.at[nx - 1 + d], col=sibling
        )

    def ring(way, c, s, incoming=False):
        hop = s + 1 if incoming else s
        owner = z_at(nz - hop) if way == 0 else z_at(hop)
        first, count = 0, tz
        if s == steps - 1:
            first, count = (0, cut) if way == 0 else (cut, tz - cut)
        block = gbuf.at[c, pl.ds(pl.multiple_of(owner * tz + first, 16), count)]
        to = z_at(1) if way == 0 else z_at(nz - 1)
        return copy_to(block, block, rs.at[way, c, s], rr.at[way, c, s], row=to)

    def halo_copy(incoming=False):
        last = pl.ds(pl.multiple_of(z * tz + tz - TILE, 32), TILE)
        src = halo if incoming else gbuf.at[:, last]
        return copy_to(src, halo, hs.at[0], hs.at[1], row=z_at(1))

    def act_send(d):
        return copy_to(asend.at[d], abuf.at[d], asem.at[d], arec.at[d], row=z_at(d))

    def grad_send(j):
        return copy_to(bsend.at[j], bbuf.at[w], bsem.at[j], brec.at[w], col=j)

    def grad_came(owner):
        return copy_to(bbuf.at[owner], bbuf.at[owner], bsem.at[0], brec.at[owner], col=w_at(1))

    def weight_send(d):
        return copy_to(wloc.at[w], wloc.at[w], wsem.at[d], wrec.at[w], col=w_at(d))

    def weight_came(owner):
        return copy_to(wloc.at[owner], wloc.at[owner], wsem.at[1], wrec.at[owner], col=w_at(1))

    def slab_send(d):
        return copy_to(wall.at[z], wall.at[z], zsem.at[d], zrec.at[d], row=z_at(d))

    def slab_came(d):
        owner = z_at(nz - d)
        return copy_to(wall.at[owner], wall.at[owner], zsem.at[d], zrec.at[d], row=z_at(1))

    up, far, down = y_at(1), y_at(2), y_at(3)
    half = part // 2

    def quarter(owner, side=None):
        if side is None:
            return pl.ds(pl.multiple_of(owner * part, part), part)
        return pl.ds(pl.multiple_of(owner * part + side * half, half), half)

    def far_send(c, side):
        return copy_to(
            pbuf.at[c, quarter(far, side)], rfar.at[c, side], s1.at[c, side], r1.at[c, side],
            dp=(up, down)[side],
        )

    def near_send(c, side):
        to = (up, down)[side]
        return copy_to(
            pbuf.at[c, quarter(to)], rnear.at[c, side], s2.at[c, side], r2.at[c, side], dp=to
        )

    def out_at(c, where):
        return out_ref.at[where, pl.ds(c * CHUNK, CHUNK)]

    def out_send(c, side, incoming=False):
        at = out_at(c, quarter((down, up)[side] if incoming else y))
        return copy_to(
            at if incoming else qbuf.at[c], at, s3.at[c, side], r3.at[c, side],
            dp=(up, down)[side],
        )

    def out_forward(c, side, incoming=False):
        at = out_at(c, quarter(far if incoming else (down, up)[side], side))
        return copy_to(at, at, s4.at[c, side], r4.at[c, side], dp=(up, down)[side])

    def out_own(c):
        return pltpu.make_async_copy(qbuf.at[c], out_at(c, quarter(y)), osem.at[c])

    def product(c):
        depth = tokens // 3 if tokens % (3 * LANES) == 0 else LANES
        for k in range(tokens // depth):
            at = pl.ds(k * depth, depth)
            term = jnp.dot(st[:, at], gbuf[c, at], preferred_element_type=jnp.float32)
            pbuf[c] = term if k == 0 else pbuf[c] + term
        for side in range(2):
            far_send(c, side).start()

    def near(c):
        for side in range(2):
            far_send(c, side).wait_recv()
            where = quarter((up, down)[side], side)
            pbuf[c, where] = pbuf[c, where] + rfar[c, side]
            near_send(c, side).start()

    def finish(c):
        total = pbuf[c, quarter(y)]
        for side in range(2):
            near_send(c, side).wait_recv()
            total = total + rnear[c, side]
        qbuf[c] = total
        for side in range(2):
            out_send(c, side).start()
        out_own(c).start()

    def forward_out(c):
        for side in range(2):
            out_send(c, side, incoming=True).wait_recv()
            out_forward(c, side).start()

    def out_done(c):
        for side in range(2):
            out_forward(c, side, incoming=True).wait_recv()
            far_send(c, side).wait_send()
            near_send(c, side).wait_send()
            out_send(c, side).wait_send()
            out_forward(c, side).wait_send()
        out_own(c).wait()

    def prepare():
        own_ids.wait()
        idcol[0:TILE] = jnp.full((TILE, LANES), -1.0, jnp.float32)
        xbuf[0:TILE] = jnp.zeros((TILE, xbuf.shape[1]), xbuf.dtype)
        lane = lax.broadcasted_iota(jnp.int32, (8, LANES), 1)
        none = jnp.full((8, LANES), -1.0, jnp.float32)
        flat = []
        for b in range(blocks):
            row = ids_vmem[0:1, b * LANES : (b + 1) * LANES].astype(jnp.float32)
            flat.append(jnp.broadcast_to(row, (8, LANES)))
            idcol[TILE + b * LANES : TILE + (b + 1) * LANES] = jnp.broadcast_to(
                row, (LANES, LANES)
            ).T
        for b in range(blocks):
            before = flat[b - 1] if b > 0 else none
            after = flat[b + 1] if b < blocks - 1 else none
            rows[0, b] = flat[b]
            rows[1, b] = jnp.where(
                lane < TILE, after, jnp.where(lane >= LANES - TILE, before, none)
            )

    def grad_bands():
        halo_copy(incoming=True).wait_recv()
        pad = jnp.zeros((wide - tz - TILE, CHUNK), gbuf.dtype)
        dims = (((1,), (1,)), ((), ()))
        band = jnp.zeros((tz, wide), jnp.float32)
        for c in range(chunks):
            own = gbuf[c, own_rows]
            window = jnp.concatenate([halo[c], own, pad], 0)
            band = band + lax.dot_general(own, window, dims, preferred_element_type=jnp.float32)
        bands[...] = band
        lane = lax.broadcasted_iota(jnp.int32, (16, LANES), 1)
        for j in range(tiles):
            turned = bands[j * TILE : (j + 1) * TILE]
            if j > 0:
                turned = pltpu.roll(turned, wide - j * TILE, 1)
            turned = turned[:, :LANES]
            bsend[j] = jnp.where(lane < 64, turned[:16], pltpu.roll(turned[16:], 64, 1))
            @pl.when(w != j)
            def _():
                grad_send(j).start()

    def act_bands():
        x_came(0).wait_recv()
        for d in range(1, nx):
            x_forwarded(d).wait_recv()

        @pl.when(w < tiles)
        def _():
            def one(d, carry):
                first = pl.multiple_of(z_at(d) * tz + w * TILE, 32)
                window = xbuf[pl.ds(first, 2 * TILE)]
                asend[d] = packed_band(window[TILE:], window)
                @pl.when(d > 0)
                def _():
                    act_send(d).start()
                return carry
            lax.fori_loop(0, nz, one, 0)

    def weights():
        @pl.when(w < tiles)
        def _():
            act = asend[0]
            for d in range(1, nz):
                act_send(d).wait_recv()
                act = act + abuf[d]
            bbuf[w] = bsend[w]
            for d in range(1, nw):
                grad_came(w_at(d)).wait_recv()
            grad = bbuf[0]
            for u in range(1, nw):
                grad = grad + bbuf[u]
            tile = z * tiles + w
            first = pl.multiple_of(tile * TILE, 32)
            ids = idcol[pl.ds(first, 2 * TILE)]
            lane = lax.broadcasted_iota(jnp.int32, (16, LANES), 1)
            row = lax.broadcasted_iota(jnp.int32, (16, LANES), 0)
            mine = jnp.where(lane < 64, ids[TILE : TILE + 16], ids[TILE + 16 :])
            wide_lane = lax.broadcasted_iota(jnp.int32, (64, LANES), 1)
            wide_row = lax.broadcasted_iota(jnp.int32, (64, LANES), 0)
            window = jnp.sum(
                jnp.where(lax.rem(wide_lane, 64) == wide_row, ids, 0.0), 0, keepdims=True
            )
            cross = lax.rem(lane, 64) < TILE
            factor = jnp.where(cross, jnp.where(tile > 0, 2.0, 0.0), 1.0)
            term = jnp.where(mine == window, act * grad * factor, 0.0)
            low = jnp.sum(jnp.where(lane < 64, term, 0.0), 1, keepdims=True)
            high = jnp.sum(jnp.where(lane < 64, 0.0, term), 1, keepdims=True)
            at = lax.rem(tile, LANES // TILE) * TILE
            spread = jnp.where(lane == row + at, low, 0.0) + jnp.where(
                lane == row + at + 16, high, 0.0
            )
            wloc[w] = jnp.broadcast_to(jnp.sum(spread, 0, keepdims=True), (8, LANES))
            for d in range(1, nw):
                weight_send(d).start()

    def slabs():
        for u in range(tiles):
            @pl.when(w != u)
            def _():
                weight_came(u).wait_recv()
        row = lax.broadcasted_iota(jnp.int32, (8, LANES), 0)
        slab = jnp.zeros((8, LANES), jnp.float32)
        for u in range(tiles):
            slab = slab + jnp.where(row == u, wloc[u], 0.0)
        wall[z] = slab
        for d in range(1, nz):
            slab_send(d).start()

    def scales():
        for d in range(1, nz):
            slab_came(d).wait_recv()
        lane = lax.broadcasted_iota(jnp.int32, (8, LANES), 1)
        none = jnp.zeros((8, LANES), jnp.float32)
        flat = []
        for b in range(blocks):
            row = none
            for k in range(b * (LANES // TILE), (b + 1) * (LANES // TILE)):
                owner, j = divmod(k, tiles)
                row = row + jnp.broadcast_to(wall[owner][j : j + 1], (8, LANES))
            flat.append(row)
        for b in range(blocks):
            before = flat[b - 1] if b > 0 else none
            after = flat[b + 1] if b < blocks - 1 else none
            rows[2, b] = flat[b]
            rows[3, b] = jnp.where(
                lane < TILE, after, jnp.where(lane >= LANES - TILE, before, none)
            )
        limit = clip_ref[0].astype(jnp.float32)

        def one(b, carry):
            at = pl.multiple_of(TILE + b * LANES, 32)
            ids = idcol[pl.ds(at, LANES)]
            found = jnp.where(ids == rows[0, b][0:1], rows[2, b][0:1], 0.0)
            found = found + jnp.where(ids == rows[1, b][0:1], rows[3, b][0:1], 0.0)
            squares = jnp.sum(found, 1, keepdims=True)
            factor = limit / jnp.maximum(jnp.sqrt(jnp.maximum(squares, 0.0)), limit)
            scaled = xbuf[pl.ds(at, LANES)].astype(jnp.float32) * factor
            st[:, pl.ds(pl.multiple_of(b * LANES, LANES), LANES)] = scaled.T.astype(st.dtype)
            return carry

        lax.fori_loop(0, blocks, one, 0)

    def forward_x():
        for d in range(1, nx):
            x_came(d).wait_recv()
            x_forward(d).start()

    first_slot = [0, 0, 1, 2, 3, 4, 5][:chunks]
    final_slot = first_slot[-1] + steps
    between = {0: (prepare,), 1: (grad_bands,), 2: (forward_x, act_bands), 3: (weights,),
               4: (slabs,), 5: (scales,)}
    if steps < 6:
        between = {0: sum(between.values(), ())}

    def ring_sent(c):
        for s in range(steps):
            for way in range(2):
                ring(way, c, s).wait_send()

    own_x.wait()
    for d in range(nx):
        x_first(d).start()
    for copy in own_g:
        copy.wait()

    def hop(t, c):
        s = t - first_slot[c]
        if 0 <= s < steps:
            for way in range(2):
                if s > 0:
                    ring(way, c, s - 1, incoming=True).wait_recv()
                ring(way, c, s).start()

    def first(c):
        for way in range(2):
            ring(way, c, steps - 1, incoming=True).wait_recv()
        product(c)
        ring_sent(c)

    def stages(p):
        for c in range(chunks):
            stage = p - 2 * (first_slot[c] + steps) - c % 2
            if 0 <= stage < 5:
                (first, near, finish, forward_out, out_done)[stage](c)

    for t in range(final_slot):
        for c in range(0, chunks, 2):
            hop(t, c)
        if t == 0:
            halo_copy().start()
        for step in between.get(t, ()):
            step()
        stages(2 * t)
        for c in range(1, chunks, 2):
            hop(t, c)
        stages(2 * t + 1)

    halo_copy().wait_send()
    for d in range(nx):
        x_first(d).wait_send()
    for d in range(1, nx):
        x_forward(d).wait_send()
    for d in range(1, nz):
        slab_send(d).wait_send()
    for j in range(tiles):
        @pl.when(w != j)
        def _():
            grad_send(j).wait_send()

    @pl.when(w < tiles)
    def _():
        for d in range(1, nz):
            act_send(d).wait_send()
        for d in range(1, nw):
            weight_send(d).wait_send()

    for p in range(2 * final_slot, 2 * final_slot + 6):
        stages(p)


def body(sizes, activations, out_grads, query_ids, clip_bound):
    x_local = activations[0]
    g_local = out_grads[0]
    ny, nz, nw, tokens = sizes
    nx = nw // 2
    features, hidden = x_local.shape[1], g_local.shape[1]
    tz = g_local.shape[0]
    tiles = tz // TILE
    chunks = hidden // CHUNK
    steps = nz // 2
    part = features // ny
    dma = pltpu.SemaphoreType.DMA
    f32, bf16 = jnp.float32, jnp.bfloat16
    return pl.pallas_call(
        functools.partial(kernel, sizes),
        out_shape=jax.ShapeDtypeStruct((features, hidden), f32),
        in_specs=[
            pl.BlockSpec(memory_space=pltpu.HBM),
            pl.BlockSpec(memory_space=pltpu.HBM),
            pl.BlockSpec(memory_space=pltpu.HBM),
            pl.BlockSpec(memory_space=pltpu.SMEM),
        ],
        out_specs=pl.BlockSpec(memory_space=pl.ANY),
        scratch_shapes=[
            pltpu.VMEM((1, tokens), jnp.int32),
            pltpu.VMEM((tz, -(-(tz + TILE) // LANES) * LANES), f32),
            pltpu.VMEM((chunks, tokens, CHUNK), bf16),
            pltpu.VMEM((TILE + tokens, features), bf16),
            pltpu.VMEM((chunks, TILE, CHUNK), bf16),
            pltpu.VMEM((features, tokens), bf16),
            pltpu.VMEM((TILE + tokens, LANES), f32),
            pltpu.VMEM((4, tokens // LANES, 8, LANES), f32),
            pltpu.VMEM((nz, 16, LANES), f32),
            pltpu.VMEM((nz, 16, LANES), f32),
            pltpu.VMEM((tiles, 16, LANES), f32),
            pltpu.VMEM((nw, 16, LANES), f32),
            pltpu.VMEM((tiles, 8, LANES), f32),
            pltpu.VMEM((nz, 8, LANES), f32),
            pltpu.VMEM((chunks, features, CHUNK), f32),
            pltpu.VMEM((chunks, 2, part // 2, CHUNK), f32),
            pltpu.VMEM((chunks, 2, part, CHUNK), f32),
            pltpu.VMEM((chunks, part, CHUNK), f32),
            dma((chunks + 2,)), dma((chunks,)),
            dma((2 * nx,)), dma((2 * nx,)),
            dma((2,)),
            dma((2, chunks, steps)), dma((2, chunks, steps)),
            dma((nz,)), dma((nz,)),
            dma((tiles,)), dma((nw,)),
            dma((nw,)), dma((tiles,)),
            dma((nz,)), dma((nz,)),
            *[dma((chunks, 2))] * 8,
        ],
        compiler_params=pltpu.CompilerParams(
            collective_id=0, has_side_effects=True, vmem_limit_bytes=63 * 1024 * 1024
        ),
        cost_estimate=pl.CostEstimate(
            flops=2 * tokens * features * hidden, bytes_accessed=1 << 23, transcendentals=0
        ),
    )(x_local, g_local, query_ids, clip_bound)


def solution(mesh):
    sizes = tuple(mesh.shape[a] for a in ("dp", "row", "col"))

    def run(activations, out_grads, query_ids, clip_bound):
        placed = (P("dp", "col", "row"), P("dp", "row", "col"), P("dp", None), P())
        return jax.shard_map(
            functools.partial(body, sizes + (query_ids.shape[1],)),
            mesh=mesh, in_specs=placed, out_specs=P("row", "col"), check_vma=False,
        )(activations, out_grads, query_ids, clip_bound)

    return run
```

```python
import functools

import jax
import jax.numpy as jnp
from jax import lax
from jax.experimental import pallas as pl
from jax.experimental.pallas import tpu as pltpu
from jax.sharding import PartitionSpec as P

TILE = 32
LANES = 128
CHUNK = 256
MESH = pl.DeviceIdType.MESH


def packed_band(tile, window):
    zeros = jnp.zeros_like(window)
    dims = (((1,), (1,)), ((), ()))
    low = lax.dot_general(
        tile[:16], jnp.concatenate([window, zeros], 0), dims, preferred_element_type=jnp.float32
    )
    high = lax.dot_general(
        tile[16:], jnp.concatenate([zeros, window], 0), dims, preferred_element_type=jnp.float32
    )
    return low + high


def kernel(
    sizes,
    x_ref, g_ref, ids_ref, clip_ref,
    out_ref,
    ids_vmem, bands, gbuf, xbuf, halo, st, idcol, rows,
    asend, abuf, bsend, bbuf, wloc, wall,
    pbuf, rfar, rnear, qbuf,
    lsem, osem, xs, xr, hs, rs, rr, asem, arec, bsem, brec, wsem, wrec, zsem, zrec,
    s1, r1, s2, r2, s3, r3, s4, r4,
):
    ny, nz, nw, tokens = sizes
    nx = nw // 2
    tz = g_ref.shape[0]
    tc = x_ref.shape[0]
    tiles = tz // TILE
    chunks = g_ref.shape[1] // CHUNK
    steps = nz // 2
    wide = bands.shape[1]
    blocks = tokens // LANES
    part = x_ref.shape[1] // ny

    y = lax.axis_index("dp")
    z = lax.axis_index("row")
    w = lax.axis_index("col")
    core = lax.rem(w, 2)
    chip = w // 2

    def z_at(d):
        return lax.rem(z + d, nz)

    def w_at(d):
        return lax.rem(w + d, nw)

    def y_at(d):
        return lax.rem(y + d, ny)

    def copy_to(src, dst, send, recv, **axis):
        return pltpu.make_async_remote_copy(
            src_ref=src, dst_ref=dst, send_sem=send, recv_sem=recv,
            device_id=axis, device_id_type=MESH,
        )

    own_rows = pl.ds(pl.multiple_of(z * tz, 32), tz)
    own_g = [
        pltpu.make_async_copy(
            g_ref.at[:, pl.ds(c * CHUNK, CHUNK)], gbuf.at[c, own_rows], lsem.at[c]
        )
        for c in range(chunks)
    ]
    own_x = pltpu.make_async_copy(
        x_ref, xbuf.at[pl.ds(pl.multiple_of(TILE + w * tc, 32), tc)], lsem.at[chunks]
    )
    own_ids = pltpu.make_async_copy(ids_ref, ids_vmem, lsem.at[chunks + 1])
    for copy in own_g:
        copy.start()
    own_x.start()
    own_ids.start()

    barrier = pltpu.get_barrier_semaphore()
    for d in range(1, nz):
        pl.semaphore_signal(barrier, inc=1, device_id={"row": z_at(d)}, device_id_type=MESH)
    for d in range(1, nw):
        pl.semaphore_signal(barrier, inc=1, device_id={"col": w_at(d)}, device_id_type=MESH)
    for d in range(1, ny):
        pl.semaphore_signal(barrier, inc=1, device_id={"dp": y_at(d)}, device_id_type=MESH)
    pl.semaphore_wait(barrier, nz + nw + ny - 3)

    def x_rows(owner):
        return xbuf.at[pl.ds(pl.multiple_of(TILE + owner * tc, 32), tc)]

    sibling = chip * 2 + 1 - core

    def x_first(d):
        to = sibling if d == 0 else lax.rem(chip + d, nx) * 2 + core
        return copy_to(x_ref, x_rows(w), xs.at[d], xr.at[d], col=to)

    def x_came(d):
        owner = sibling if d == 0 else lax.rem(chip + nx - d, nx) * 2 + core
        return copy_to(x_rows(owner), x_rows(owner), xs.at[d], xr.at[d], col=sibling)

    def x_forward(d):
        owner = lax.rem(chip + nx - d, nx) * 2 + core
        return copy_to(
            x_rows(owner), x_rows(owner), xs.at[nx - 1 + d], xr.at[nx - 1 + d], col=sibling
        )

    def x_forwarded(d):
        owner = lax.rem(chip + nx - d, nx) * 2 + 1 - core
        return copy_to(
            x_rows(owner), x_rows(owner), xs.at[nx - 1 + d], xr.at[nx - 1 + d], col=sibling
        )

    def ring(turn, c, s, incoming=False):
        way = lax.rem(turn + core, 2)
        hop = s + 1 if incoming else s
        owner = z_at(nz + (2 * way - 1) * hop)
        start, count = owner * tz, tz
        if s == steps - 1:
            start, count = owner * tz + way * (tz // 2), tz // 2
        block = gbuf.at[c, pl.ds(pl.multiple_of(start, 32), count)]
        to = z_at(1 + way * (nz - 2))
        return copy_to(block, block, rs.at[way, c, s], rr.at[way, c, s], row=to)

    def halo_copy(incoming=False):
        last = pl.ds(pl.multiple_of(z * tz + tz - TILE, 32), TILE)
        src = halo if incoming else gbuf.at[:, last]
        return copy_to(src, halo, hs.at[0], hs.at[1], row=z_at(1))

    def act_send(d):
        return copy_to(asend.at[d], abuf.at[d], asem.at[d], arec.at[d], row=z_at(d))

    def grad_send(j):
        return copy_to(bsend.at[j], bbuf.at[w], bsem.at[j], brec.at[w], col=j)

    def grad_came(owner):
        return copy_to(bbuf.at[owner], bbuf.at[owner], bsem.at[0], brec.at[owner], col=w_at(1))

    def weight_send(d):
        return copy_to(wloc.at[w], wloc.at[w], wsem.at[d], wrec.at[w], col=w_at(d))

    def weight_came(owner):
        return copy_to(wloc.at[owner], wloc.at[owner], wsem.at[1], wrec.at[owner], col=w_at(1))

    def slab_send(d):
        return copy_to(wall.at[z], wall.at[z], zsem.at[d], zrec.at[d], row=z_at(d))

    def slab_came(d):
        owner = z_at(nz - d)
        return copy_to(wall.at[owner], wall.at[owner], zsem.at[d], zrec.at[d], row=z_at(1))

    up, far, down = y_at(1), y_at(2), y_at(3)
    half = part // 2

    def quarter(owner, side=None):
        if side is None:
            return pl.ds(pl.multiple_of(owner * part, part), part)
        return pl.ds(pl.multiple_of(owner * part + side * half, half), half)

    def far_send(c, side):
        return copy_to(
            pbuf.at[c, quarter(far, side)], rfar.at[c, side], s1.at[c, side], r1.at[c, side],
            dp=(up, down)[side],
        )

    def near_send(c, side):
        to = (up, down)[side]
        return copy_to(
            pbuf.at[c, quarter(to)], rnear.at[c, side], s2.at[c, side], r2.at[c, side], dp=to
        )

    def out_at(c, where):
        return out_ref.at[where, pl.ds(c * CHUNK, CHUNK)]

    def out_send(c, side, incoming=False):
        at = out_at(c, quarter((down, up)[side] if incoming else y))
        return copy_to(
            at if incoming else qbuf.at[c], at, s3.at[c, side], r3.at[c, side],
            dp=(up, down)[side],
        )

    def out_forward(c, side, incoming=False):
        at = out_at(c, quarter(far if incoming else (down, up)[side], side))
        return copy_to(at, at, s4.at[c, side], r4.at[c, side], dp=(up, down)[side])

    def out_own(c):
        return pltpu.make_async_copy(qbuf.at[c], out_at(c, quarter(y)), osem.at[c])

    def product(c):
        depth = tokens // 3 if tokens % (3 * LANES) == 0 else LANES
        for k in range(tokens // depth):
            at = pl.ds(k * depth, depth)
            term = jnp.dot(st[:, at], gbuf[c, at], preferred_element_type=jnp.float32)
            pbuf[c] = term if k == 0 else pbuf[c] + term
        for side in range(2):
            far_send(c, side).start()

    def near(c):
        for side in range(2):
            far_send(c, side).wait_recv()
            where = quarter((up, down)[side], side)
            pbuf[c, where] = pbuf[c, where] + rfar[c, side]
            near_send(c, side).start()

    def finish(c):
        total = pbuf[c, quarter(y)]
        for side in range(2):
            near_send(c, side).wait_recv()
            total = total + rnear[c, side]
        qbuf[c] = total
        for side in range(2):
            out_send(c, side).start()
        out_own(c).start()

    def forward_out(c):
        for side in range(2):
            out_send(c, side, incoming=True).wait_recv()
            out_forward(c, side).start()

    def out_done(c):
        for side in range(2):
            out_forward(c, side, incoming=True).wait_recv()
            far_send(c, side).wait_send()
            near_send(c, side).wait_send()
            out_send(c, side).wait_send()
            out_forward(c, side).wait_send()
        out_own(c).wait()

    def prepare():
        own_ids.wait()
        idcol[0:TILE] = jnp.full((TILE, LANES), -1.0, jnp.float32)
        xbuf[0:TILE] = jnp.zeros((TILE, xbuf.shape[1]), xbuf.dtype)
        lane = lax.broadcasted_iota(jnp.int32, (8, LANES), 1)
        none = jnp.full((8, LANES), -1.0, jnp.float32)
        flat = []
        for b in range(blocks):
            row = ids_vmem[0:1, b * LANES : (b + 1) * LANES].astype(jnp.float32)
            flat.append(jnp.broadcast_to(row, (8, LANES)))
            idcol[TILE + b * LANES : TILE + (b + 1) * LANES] = jnp.broadcast_to(
                row, (LANES, LANES)
            ).T
        for b in range(blocks):
            before = flat[b - 1] if b > 0 else none
            after = flat[b + 1] if b < blocks - 1 else none
            rows[0, b] = flat[b]
            rows[1, b] = jnp.where(
                lane < TILE, after, jnp.where(lane >= LANES - TILE, before, none)
            )

    def grad_bands():
        halo_copy(incoming=True).wait_recv()
        pad = jnp.zeros((wide - tz - TILE, CHUNK), gbuf.dtype)
        dims = (((1,), (1,)), ((), ()))
        band = jnp.zeros((tz, wide), jnp.float32)
        for c in range(chunks):
            own = gbuf[c, own_rows]
            window = jnp.concatenate([halo[c], own, pad], 0)
            band = band + lax.dot_general(own, window, dims, preferred_element_type=jnp.float32)
        bands[...] = band
        lane = lax.broadcasted_iota(jnp.int32, (16, LANES), 1)
        for j in range(tiles):
            turned = bands[j * TILE : (j + 1) * TILE]
            if j > 0:
                turned = pltpu.roll(turned, wide - j * TILE, 1)
            turned = turned[:, :LANES]
            bsend[j] = jnp.where(lane < 64, turned[:16], pltpu.roll(turned[16:], 64, 1))
            @pl.when(w != j)
            def _():
                grad_send(j).start()

    def act_bands():
        x_came(0).wait_recv()
        for d in range(1, nx):
            x_forwarded(d).wait_recv()

        @pl.when(w < tiles)
        def _():
            def one(d, carry):
                first = pl.multiple_of(z_at(d) * tz + w * TILE, 32)
                window = xbuf[pl.ds(first, 2 * TILE)]
                asend[d] = packed_band(window[TILE:], window)
                @pl.when(d > 0)
                def _():
                    act_send(d).start()
                return carry
            lax.fori_loop(0, nz, one, 0)

    def weights():
        @pl.when(w < tiles)
        def _():
            act = asend[0]
            for d in range(1, nz):
                act_send(d).wait_recv()
                act = act + abuf[d]
            bbuf[w] = bsend[w]
            for d in range(1, nw):
                grad_came(w_at(d)).wait_recv()
            grad = bbuf[0]
            for u in range(1, nw):
                grad = grad + bbuf[u]
            tile = z * tiles + w
            first = pl.multiple_of(tile * TILE, 32)
            ids = idcol[pl.ds(first, 2 * TILE)]
            lane = lax.broadcasted_iota(jnp.int32, (16, LANES), 1)
            row = lax.broadcasted_iota(jnp.int32, (16, LANES), 0)
            mine = jnp.where(lane < 64, ids[TILE : TILE + 16], ids[TILE + 16 :])
            wide_lane = lax.broadcasted_iota(jnp.int32, (64, LANES), 1)
            wide_row = lax.broadcasted_iota(jnp.int32, (64, LANES), 0)
            window = jnp.sum(
                jnp.where(lax.rem(wide_lane, 64) == wide_row, ids, 0.0), 0, keepdims=True
            )
            cross = lax.rem(lane, 64) < TILE
            factor = jnp.where(cross, jnp.where(tile > 0, 2.0, 0.0), 1.0)
            term = jnp.where(mine == window, act * grad * factor, 0.0)
            low = jnp.sum(jnp.where(lane < 64, term, 0.0), 1, keepdims=True)
            high = jnp.sum(jnp.where(lane < 64, 0.0, term), 1, keepdims=True)
            at = lax.rem(tile, LANES // TILE) * TILE
            spread = jnp.where(lane == row + at, low, 0.0) + jnp.where(
                lane == row + at + 16, high, 0.0
            )
            wloc[w] = jnp.broadcast_to(jnp.sum(spread, 0, keepdims=True), (8, LANES))
            for d in range(1, nw):
                weight_send(d).start()

    def slabs():
        for u in range(tiles):
            @pl.when(w != u)
            def _():
                weight_came(u).wait_recv()
        row = lax.broadcasted_iota(jnp.int32, (8, LANES), 0)
        slab = jnp.zeros((8, LANES), jnp.float32)
        for u in range(tiles):
            slab = slab + jnp.where(row == u, wloc[u], 0.0)
        wall[z] = slab
        for d in range(1, nz):
            slab_send(d).start()

    def scales():
        for d in range(1, nz):
            slab_came(d).wait_recv()
        lane = lax.broadcasted_iota(jnp.int32, (8, LANES), 1)
        none = jnp.zeros((8, LANES), jnp.float32)
        flat = []
        for b in range(blocks):
            row = none
            for k in range(b * (LANES // TILE), (b + 1) * (LANES // TILE)):
                owner, j = divmod(k, tiles)
                row = row + jnp.broadcast_to(wall[owner][j : j + 1], (8, LANES))
            flat.append(row)
        for b in range(blocks):
            before = flat[b - 1] if b > 0 else none
            after = flat[b + 1] if b < blocks - 1 else none
            rows[2, b] = flat[b]
            rows[3, b] = jnp.where(
                lane < TILE, after, jnp.where(lane >= LANES - TILE, before, none)
            )
        limit = clip_ref[0].astype(jnp.float32)

        def one(b, carry):
            at = pl.multiple_of(TILE + b * LANES, 32)
            ids = idcol[pl.ds(at, LANES)]
            found = jnp.where(ids == rows[0, b][0:1], rows[2, b][0:1], 0.0)
            found = found + jnp.where(ids == rows[1, b][0:1], rows[3, b][0:1], 0.0)
            squares = jnp.sum(found, 1, keepdims=True)
            factor = limit / jnp.maximum(jnp.sqrt(jnp.maximum(squares, 0.0)), limit)
            scaled = xbuf[pl.ds(at, LANES)].astype(jnp.float32) * factor
            st[:, pl.ds(pl.multiple_of(b * LANES, LANES), LANES)] = scaled.T.astype(st.dtype)
            return carry

        lax.fori_loop(0, blocks, one, 0)

    def forward_x():
        for d in range(1, nx):
            x_came(d).wait_recv()
            x_forward(d).start()

    first_slot = [0, 0, 1, 2, 3, 4, 5][:chunks]
    final_slot = first_slot[-1] + steps
    between = {0: (prepare,), 1: (grad_bands,), 2: (forward_x, act_bands), 3: (weights,),
               4: (slabs,), 5: (scales,)}
    if steps < 6:
        between = {0: sum(between.values(), ())}

    def ring_sent(c):
        for s in range(steps):
            for way in range(2):
                ring(way, c, s).wait_send()

    own_x.wait()
    for d in range(nx):
        x_first(d).start()
    for copy in own_g:
        copy.wait()

    def hop(t, c):
        s = t - first_slot[c]
        if 0 <= s < steps:
            for way in range(2):
                if s > 0:
                    ring(way, c, s - 1, incoming=True).wait_recv()
                ring(way, c, s).start()

    def first(c):
        for way in range(2):
            ring(way, c, steps - 1, incoming=True).wait_recv()
        product(c)
        ring_sent(c)

    def stages(p):
        for c in range(chunks):
            stage = p - 2 * (first_slot[c] + steps) - c % 2
            if 0 <= stage < 5:
                (first, near, finish, forward_out, out_done)[stage](c)

    for t in range(final_slot):
        for c in range(0, chunks, 2):
            hop(t, c)
        if t == 0:
            halo_copy().start()
        for step in between.get(t, ()):
            step()
        stages(2 * t)
        for c in range(1, chunks, 2):
            hop(t, c)
        stages(2 * t + 1)

    halo_copy().wait_send()
    for d in range(nx):
        x_first(d).wait_send()
    for d in range(1, nx):
        x_forward(d).wait_send()
    for d in range(1, nz):
        slab_send(d).wait_send()
    for j in range(tiles):
        @pl.when(w != j)
        def _():
            grad_send(j).wait_send()

    @pl.when(w < tiles)
    def _():
        for d in range(1, nz):
            act_send(d).wait_send()
        for d in range(1, nw):
            weight_send(d).wait_send()

    for p in range(2 * final_slot, 2 * final_slot + 6):
        stages(p)


def body(sizes, activations, out_grads, query_ids, clip_bound):
    x_local = activations[0]
    g_local = out_grads[0]
    ny, nz, nw, tokens = sizes
    nx = nw // 2
    features, hidden = x_local.shape[1], g_local.shape[1]
    tz = g_local.shape[0]
    tiles = tz // TILE
    chunks = hidden // CHUNK
    steps = nz // 2
    part = features // ny
    dma = pltpu.SemaphoreType.DMA
    f32, bf16 = jnp.float32, jnp.bfloat16
    return pl.pallas_call(
        functools.partial(kernel, sizes),
        out_shape=jax.ShapeDtypeStruct((features, hidden), f32),
        in_specs=[
            pl.BlockSpec(memory_space=pltpu.HBM),
            pl.BlockSpec(memory_space=pltpu.HBM),
            pl.BlockSpec(memory_space=pltpu.HBM),
            pl.BlockSpec(memory_space=pltpu.SMEM),
        ],
        out_specs=pl.BlockSpec(memory_space=pl.ANY),
        scratch_shapes=[
            pltpu.VMEM((1, tokens), jnp.int32),
            pltpu.VMEM((tz, -(-(tz + TILE) // LANES) * LANES), f32),
            pltpu.VMEM((chunks, tokens, CHUNK), bf16),
            pltpu.VMEM((TILE + tokens, features), bf16),
            pltpu.VMEM((chunks, TILE, CHUNK), bf16),
            pltpu.VMEM((features, tokens), bf16),
            pltpu.VMEM((TILE + tokens, LANES), f32),
            pltpu.VMEM((4, tokens // LANES, 8, LANES), f32),
            pltpu.VMEM((nz, 16, LANES), f32),
            pltpu.VMEM((nz, 16, LANES), f32),
            pltpu.VMEM((tiles, 16, LANES), f32),
            pltpu.VMEM((nw, 16, LANES), f32),
            pltpu.VMEM((tiles, 8, LANES), f32),
            pltpu.VMEM((nz, 8, LANES), f32),
            pltpu.VMEM((chunks, features, CHUNK), f32),
            pltpu.VMEM((chunks, 2, part // 2, CHUNK), f32),
            pltpu.VMEM((chunks, 2, part, CHUNK), f32),
            pltpu.VMEM((chunks, part, CHUNK), f32),
            dma((chunks + 2,)), dma((chunks,)),
            dma((2 * nx,)), dma((2 * nx,)),
            dma((2,)),
            dma((2, chunks, steps)), dma((2, chunks, steps)),
            dma((nz,)), dma((nz,)),
            dma((tiles,)), dma((nw,)),
            dma((nw,)), dma((tiles,)),
            dma((nz,)), dma((nz,)),
            *[dma((chunks, 2))] * 8,
        ],
        compiler_params=pltpu.CompilerParams(
            collective_id=0, has_side_effects=True, vmem_limit_bytes=63 * 1024 * 1024
        ),
        cost_estimate=pl.CostEstimate(
            flops=2 * tokens * features * hidden, bytes_accessed=1 << 23, transcendentals=0
        ),
    )(x_local, g_local, query_ids, clip_bound)


def solution(mesh):
    sizes = tuple(mesh.shape[a] for a in ("dp", "row", "col"))

    def run(activations, out_grads, query_ids, clip_bound):
        placed = (P("dp", "col", "row"), P("dp", "row", "col"), P("dp", None), P())
        return jax.shard_map(
            functools.partial(body, sizes + (query_ids.shape[1],)),
            mesh=mesh, in_specs=placed, out_specs=P("row", "col"), check_vma=False,
        )(activations, out_grads, query_ids, clip_bound)

    return run
```

```python
import functools

import jax
import jax.numpy as jnp
from jax import lax
from jax.experimental import pallas as pl
from jax.experimental.pallas import tpu as pltpu
from jax.sharding import PartitionSpec as P

TILE = 32
LANES = 128
WIDTHS = (512, 512, 512, 256)
FIRST_SLOTS = (0, 1, 3, 4)
MESH = pl.DeviceIdType.MESH


def packed_band(tile, window):
    zeros = jnp.zeros_like(window)
    dims = (((1,), (1,)), ((), ()))
    low = lax.dot_general(
        tile[:16], jnp.concatenate([window, zeros], 0), dims, preferred_element_type=jnp.float32
    )
    high = lax.dot_general(
        tile[16:], jnp.concatenate([zeros, window], 0), dims, preferred_element_type=jnp.float32
    )
    return low + high


def kernel(
    sizes,
    x_ref, g_ref, ids_ref, clip_ref,
    out_ref,
    ids_vmem, bands, gbuf, xbuf, halo, st, idcol, rows,
    asend, abuf, bsend, bbuf, wz, wall,
    pbuf, rfar, rnear, qbuf,
    lsem, osem, xs, xr, hs, rs, rr, asem, arec, bsem, brec, wsem, wrec, zsem, zrec,
    s1, r1, s2, r2, s3, r3, s4, r4,
):
    ny, nz, nw, tokens = sizes
    nx = nw // 2
    tz = g_ref.shape[0]
    tc = x_ref.shape[0]
    tiles = tz // TILE
    chunks = len(WIDTHS)
    columns = [pl.ds(sum(WIDTHS[:c]), WIDTHS[c]) for c in range(chunks)]
    steps = nz // 2
    wide = bands.shape[1]
    blocks = tokens // LANES
    part = x_ref.shape[1] // ny

    y = lax.axis_index("dp")
    z = lax.axis_index("row")
    w = lax.axis_index("col")
    core = lax.rem(w, 2)
    chip = w // 2

    def z_at(d):
        return lax.rem(z + d, nz)

    def w_at(d):
        return lax.rem(w + d, nw)

    def y_at(d):
        return lax.rem(y + d, ny)

    def copy_to(src, dst, send, recv, **axis):
        return pltpu.make_async_remote_copy(
            src_ref=src, dst_ref=dst, send_sem=send, recv_sem=recv,
            device_id=axis, device_id_type=MESH,
        )

    own_rows = pl.ds(pl.multiple_of(z * tz, 32), tz)
    own_g = [
        pltpu.make_async_copy(
            g_ref.at[:, columns[c]], gbuf[c].at[own_rows], lsem.at[c]
        )
        for c in range(chunks)
    ]
    own_x = pltpu.make_async_copy(
        x_ref, xbuf.at[pl.ds(pl.multiple_of(TILE + w * tc, 32), tc)], lsem.at[chunks]
    )
    own_ids = pltpu.make_async_copy(ids_ref, ids_vmem, lsem.at[chunks + 1])
    for copy in own_g:
        copy.start()
    own_x.start()
    own_ids.start()

    barrier = pltpu.get_barrier_semaphore()
    for d in range(1, nz):
        pl.semaphore_signal(barrier, inc=1, device_id={"row": z_at(d)}, device_id_type=MESH)
    for d in range(1, nw):
        pl.semaphore_signal(barrier, inc=1, device_id={"col": w_at(d)}, device_id_type=MESH)
    for d in range(1, ny):
        pl.semaphore_signal(barrier, inc=1, device_id={"dp": y_at(d)}, device_id_type=MESH)
    pl.semaphore_wait(barrier, nz + nw + ny - 3)

    def x_rows(owner):
        return xbuf.at[pl.ds(pl.multiple_of(TILE + owner * tc, 32), tc)]

    sibling = chip * 2 + 1 - core

    def x_first(d):
        to = sibling if d == 0 else lax.rem(chip + d, nx) * 2 + core
        return copy_to(x_ref, x_rows(w), xs.at[d], xr.at[d], col=to)

    def x_came(d):
        owner = sibling if d == 0 else lax.rem(chip + nx - d, nx) * 2 + core
        return copy_to(x_rows(owner), x_rows(owner), xs.at[d], xr.at[d], col=sibling)

    def x_forward(d):
        owner = lax.rem(chip + nx - d, nx) * 2 + core
        return copy_to(
            x_rows(owner), x_rows(owner), xs.at[nx - 1 + d], xr.at[nx - 1 + d], col=sibling
        )

    def x_forwarded(d):
        owner = lax.rem(chip + nx - d, nx) * 2 + 1 - core
        return copy_to(
            x_rows(owner), x_rows(owner), xs.at[nx - 1 + d], xr.at[nx - 1 + d], col=sibling
        )

    def ring(turn, c, s, incoming=False):
        way = lax.rem(turn + core, 2)
        hop = s + 1 if incoming else s
        owner = z_at(nz + (2 * way - 1) * hop)
        start, count = owner * tz, tz
        if s == steps - 1:
            start, count = owner * tz + way * (tz // 2), tz // 2
        block = gbuf[c].at[pl.ds(pl.multiple_of(start, 32), count)]
        to = z_at(1 + way * (nz - 2))
        return copy_to(block, block, rs.at[way, c, s], rr.at[way, c, s], row=to)

    def halo_copy(incoming=False):
        src = halo if incoming else g_ref.at[pl.ds(tz - TILE, TILE)]
        return copy_to(src, halo, hs.at[0], hs.at[1], row=z_at(1))

    def act_send(d):
        return copy_to(asend.at[d], abuf.at[d], asem.at[d], arec.at[d], row=z_at(d))

    def grad_send(j):
        return copy_to(bsend.at[j], bbuf.at[w], bsem.at[j], brec.at[w], col=j)

    def grad_came(owner):
        return copy_to(bbuf.at[owner], bbuf.at[owner], bsem.at[0], brec.at[owner], col=w_at(1))

    def weight_send(d):
        return copy_to(wz.at[z], wz.at[z], zsem.at[d], zrec.at[d], row=z_at(d))

    def weight_came(d):
        owner = z_at(nz - d)
        return copy_to(wz.at[owner], wz.at[owner], zsem.at[d], zrec.at[d], row=z_at(1))

    def slab_send(d):
        return copy_to(wz, wall.at[w], wsem.at[d], wrec.at[w], col=w_at(d))

    def slab_came(owner):
        return copy_to(wall.at[owner], wall.at[owner], wsem.at[1], wrec.at[owner], col=w_at(1))

    up, far, down = y_at(1), y_at(2), y_at(3)
    half = part // 2

    def quarter(owner, side=None):
        if side is None:
            return pl.ds(pl.multiple_of(owner * part, part), part)
        return pl.ds(pl.multiple_of(owner * part + side * half, half), half)

    def far_send(c, side):
        return copy_to(
            pbuf[c].at[quarter(far, side)], rfar[c].at[side], s1.at[c, side], r1.at[c, side],
            dp=(up, down)[side],
        )

    def near_send(c, side):
        to = (up, down)[side]
        return copy_to(
            pbuf[c].at[quarter(to)], rnear[c].at[side], s2.at[c, side], r2.at[c, side], dp=to
        )

    def out_at(c, where):
        return out_ref.at[where, columns[c]]

    def out_send(c, side, incoming=False):
        at = out_at(c, quarter((down, up)[side] if incoming else y))
        return copy_to(
            at if incoming else qbuf[c], at, s3.at[c, side], r3.at[c, side],
            dp=(up, down)[side],
        )

    def out_forward(c, side, incoming=False):
        at = out_at(c, quarter(far if incoming else (down, up)[side], side))
        return copy_to(at, at, s4.at[c, side], r4.at[c, side], dp=(up, down)[side])

    def out_own(c):
        return pltpu.make_async_copy(qbuf[c], out_at(c, quarter(y)), osem.at[c])

    def product(c):
        depth = tokens // 3 if tokens % (3 * LANES) == 0 else LANES
        for k in range(tokens // depth):
            at = pl.ds(k * depth, depth)
            term = jnp.dot(st[:, at], gbuf[c][at], preferred_element_type=jnp.float32)
            pbuf[c][...] = term if k == 0 else pbuf[c][...] + term
        for side in range(2):
            far_send(c, side).start()

    def near(c):
        for side in range(2):
            far_send(c, side).wait_recv()
            where = quarter((up, down)[side], side)
            pbuf[c][where] = pbuf[c][where] + rfar[c][side]
            near_send(c, side).start()

    def finish(c):
        total = pbuf[c][quarter(y)]
        for side in range(2):
            near_send(c, side).wait_recv()
            total = total + rnear[c][side]
        qbuf[c][...] = total
        for side in range(2):
            out_send(c, side).start()
        out_own(c).start()

    def forward_out(c):
        for side in range(2):
            out_send(c, side, incoming=True).wait_recv()
            out_forward(c, side).start()

    def out_done(c):
        for side in range(2):
            out_forward(c, side, incoming=True).wait_recv()
            far_send(c, side).wait_send()
            near_send(c, side).wait_send()
            out_send(c, side).wait_send()
            out_forward(c, side).wait_send()
        out_own(c).wait()

    def prepare():
        own_ids.wait()
        idcol[0:TILE] = jnp.full((TILE, LANES), -1.0, jnp.float32)
        xbuf[0:TILE] = jnp.zeros((TILE, xbuf.shape[1]), xbuf.dtype)
        lane = lax.broadcasted_iota(jnp.int32, (8, LANES), 1)
        none = jnp.full((8, LANES), -1.0, jnp.float32)
        flat = []
        for b in range(blocks):
            row = ids_vmem[0:1, b * LANES : (b + 1) * LANES].astype(jnp.float32)
            flat.append(jnp.broadcast_to(row, (8, LANES)))
            idcol[TILE + b * LANES : TILE + (b + 1) * LANES] = jnp.broadcast_to(
                row, (LANES, LANES)
            ).T
        for b in range(blocks):
            before = flat[b - 1] if b > 0 else none
            after = flat[b + 1] if b < blocks - 1 else none
            rows[0, b] = flat[b]
            rows[1, b] = jnp.where(
                lane < TILE, after, jnp.where(lane >= LANES - TILE, before, none)
            )

    def grad_bands():
        halo_copy(incoming=True).wait_recv()
        dims = (((1,), (1,)), ((), ()))
        band = jnp.zeros((tz, wide), jnp.float32)
        for c in range(chunks):
            own = gbuf[c][own_rows]
            pad = jnp.zeros((wide - tz - TILE, WIDTHS[c]), own.dtype)
            window = jnp.concatenate([halo[:, columns[c]], own, pad], 0)
            band = band + lax.dot_general(own, window, dims, preferred_element_type=jnp.float32)
        bands[...] = band
        lane = lax.broadcasted_iota(jnp.int32, (16, LANES), 1)
        for j in range(tiles):
            turned = bands[j * TILE : (j + 1) * TILE]
            if j > 0:
                turned = pltpu.roll(turned, wide - j * TILE, 1)
            turned = turned[:, :LANES]
            bsend[j] = jnp.where(lane < 64, turned[:16], pltpu.roll(turned[16:], 64, 1))
            @pl.when(w != j)
            def _():
                grad_send(j).start()

    def act_bands():
        x_came(0).wait_recv()
        for d in range(1, nx):
            x_forwarded(d).wait_recv()

        @pl.when(w < tiles)
        def _():
            def one(d, carry):
                first = pl.multiple_of(z_at(d) * tz + w * TILE, 32)
                window = xbuf[pl.ds(first, 2 * TILE)]
                asend[d] = packed_band(window[TILE:], window)
                @pl.when(d > 0)
                def _():
                    act_send(d).start()
                return carry
            lax.fori_loop(0, nz, one, 0)

    def weights():
        @pl.when(w < tiles)
        def _():
            act = asend[0]
            for d in range(1, nz):
                act_send(d).wait_recv()
                act = act + abuf[d]
            bbuf[w] = bsend[w]
            for d in range(1, nw):
                grad_came(w_at(d)).wait_recv()
            grad = bbuf[0]
            for u in range(1, nw):
                grad = grad + bbuf[u]
            tile = z * tiles + w
            first = pl.multiple_of(tile * TILE, 32)
            ids = idcol[pl.ds(first, 2 * TILE)]
            lane = lax.broadcasted_iota(jnp.int32, (16, LANES), 1)
            row = lax.broadcasted_iota(jnp.int32, (16, LANES), 0)
            mine = jnp.where(lane < 64, ids[TILE : TILE + 16], ids[TILE + 16 :])
            wide_lane = lax.broadcasted_iota(jnp.int32, (64, LANES), 1)
            wide_row = lax.broadcasted_iota(jnp.int32, (64, LANES), 0)
            window = jnp.sum(
                jnp.where(lax.rem(wide_lane, 64) == wide_row, ids, 0.0), 0, keepdims=True
            )
            cross = lax.rem(lane, 64) < TILE
            factor = jnp.where(cross, jnp.where(tile > 0, 2.0, 0.0), 1.0)
            term = jnp.where(mine == window, act * grad * factor, 0.0)
            low = jnp.sum(jnp.where(lane < 64, term, 0.0), 1, keepdims=True)
            high = jnp.sum(jnp.where(lane < 64, 0.0, term), 1, keepdims=True)
            at = lax.rem(tile, LANES // TILE) * TILE
            spread = jnp.where(lane == row + at, low, 0.0) + jnp.where(
                lane == row + at + 16, high, 0.0
            )
            wz[z] = jnp.sum(spread, 0, keepdims=True)
            for d in range(1, nz):
                weight_send(d).start()

    def slabs():
        @pl.when(w < tiles)
        def _():
            for d in range(1, nz):
                weight_came(d).wait_recv()
            wall[w] = wz[...]
            for d in range(1, nw):
                slab_send(d).start()

    def scales():
        for u in range(tiles):
            @pl.when(w != u)
            def _():
                slab_came(u).wait_recv()
        lane = lax.broadcasted_iota(jnp.int32, (8, LANES), 1)
        none = jnp.zeros((8, LANES), jnp.float32)
        flat = []
        for b in range(blocks):
            row = none
            for k in range(b * (LANES // TILE), (b + 1) * (LANES // TILE)):
                owner, j = divmod(k, tiles)
                row = row + jnp.broadcast_to(wall[j, owner], (8, LANES))
            flat.append(row)
        for b in range(blocks):
            before = flat[b - 1] if b > 0 else none
            after = flat[b + 1] if b < blocks - 1 else none
            rows[2, b] = flat[b]
            rows[3, b] = jnp.where(
                lane < TILE, after, jnp.where(lane >= LANES - TILE, before, none)
            )
        limit = clip_ref[0].astype(jnp.float32)

        def one(b, carry):
            at = pl.multiple_of(TILE + b * LANES, 32)
            ids = idcol[pl.ds(at, LANES)]
            found = jnp.where(ids == rows[0, b][0:1], rows[2, b][0:1], 0.0)
            found = found + jnp.where(ids == rows[1, b][0:1], rows[3, b][0:1], 0.0)
            squares = jnp.sum(found, 1, keepdims=True)
            factor = limit / jnp.maximum(jnp.sqrt(jnp.maximum(squares, 0.0)), limit)
            scaled = xbuf[pl.ds(at, LANES)].astype(jnp.float32) * factor
            st[:, pl.ds(pl.multiple_of(b * LANES, LANES), LANES)] = scaled.T.astype(st.dtype)
            return carry

        lax.fori_loop(0, blocks, one, 0)

    def forward_x():
        for d in range(1, nx):
            x_came(d).wait_recv()
            x_forward(d).start()

    first_slot = FIRST_SLOTS
    final_slot = first_slot[-1] + steps
    between = {0: (prepare,), 1: (grad_bands,), 2: (forward_x, act_bands), 3: (weights,),
               4: (slabs,), 5: (scales,)}
    if steps < 6:
        between = {0: sum(between.values(), ())}

    def ring_sent(c):
        for s in range(steps):
            for way in range(2):
                ring(way, c, s).wait_send()

    own_x.wait()
    for d in range(nx):
        x_first(d).start()
    for copy in own_g:
        copy.wait()

    def hop(t, c):
        s = t - first_slot[c]
        if 0 <= s < steps:
            for way in range(2):
                if s > 0:
                    ring(way, c, s - 1, incoming=True).wait_recv()
                ring(way, c, s).start()

    def first(c):
        for way in range(2):
            ring(way, c, steps - 1, incoming=True).wait_recv()
        product(c)
        ring_sent(c)

    def stages(p):
        for c in range(chunks):
            stage = p - 2 * (first_slot[c] + steps) - c % 2
            if 0 <= stage < 5:
                (first, near, finish, forward_out, out_done)[stage](c)

    for t in range(final_slot):
        for c in range(0, chunks, 2):
            hop(t, c)
        if t == 0:
            halo_copy().start()
        for step in between.get(t, ()):
            step()
        stages(2 * t)
        for c in range(1, chunks, 2):
            hop(t, c)
        stages(2 * t + 1)

    halo_copy().wait_send()
    for d in range(nx):
        x_first(d).wait_send()
    for d in range(1, nx):
        x_forward(d).wait_send()
    for j in range(tiles):
        @pl.when(w != j)
        def _():
            grad_send(j).wait_send()

    @pl.when(w < tiles)
    def _():
        for d in range(1, nz):
            act_send(d).wait_send()
            weight_send(d).wait_send()
        for d in range(1, nw):
            slab_send(d).wait_send()

    for p in range(2 * final_slot, 2 * final_slot + 6):
        stages(p)


def body(sizes, activations, out_grads, query_ids, clip_bound):
    x_local = activations[0]
    g_local = out_grads[0]
    ny, nz, nw, tokens = sizes
    nx = nw // 2
    features, hidden = x_local.shape[1], g_local.shape[1]
    tz = g_local.shape[0]
    tiles = tz // TILE
    chunks = len(WIDTHS)
    assert sum(WIDTHS) == hidden
    steps = nz // 2
    part = features // ny
    dma = pltpu.SemaphoreType.DMA
    f32, bf16 = jnp.float32, jnp.bfloat16
    return pl.pallas_call(
        functools.partial(kernel, sizes),
        out_shape=jax.ShapeDtypeStruct((features, hidden), f32),
        in_specs=[
            pl.BlockSpec(memory_space=pltpu.HBM),
            pl.BlockSpec(memory_space=pltpu.HBM),
            pl.BlockSpec(memory_space=pltpu.HBM),
            pl.BlockSpec(memory_space=pltpu.SMEM),
        ],
        out_specs=pl.BlockSpec(memory_space=pl.ANY),
        scratch_shapes=[
            pltpu.VMEM((1, tokens), jnp.int32),
            pltpu.VMEM((tz, -(-(tz + TILE) // LANES) * LANES), f32),
            [pltpu.VMEM((tokens, n), bf16) for n in WIDTHS],
            pltpu.VMEM((TILE + tokens, features), bf16),
            pltpu.VMEM((TILE, hidden), bf16),
            pltpu.VMEM((features, tokens), bf16),
            pltpu.VMEM((TILE + tokens, LANES), f32),
            pltpu.VMEM((4, tokens // LANES, 8, LANES), f32),
            pltpu.VMEM((nz, 16, LANES), f32),
            pltpu.VMEM((nz, 16, LANES), f32),
            pltpu.VMEM((tiles, 16, LANES), f32),
            pltpu.VMEM((nw, 16, LANES), f32),
            pltpu.VMEM((nz, 1, LANES), f32),
            pltpu.VMEM((tiles, nz, 1, LANES), f32),
            [pltpu.VMEM((features, n), f32) for n in WIDTHS],
            [pltpu.VMEM((2, part // 2, n), f32) for n in WIDTHS],
            [pltpu.VMEM((2, part, n), f32) for n in WIDTHS],
            [pltpu.VMEM((part, n), f32) for n in WIDTHS],
            dma((chunks + 2,)), dma((chunks,)),
            dma((2 * nx,)), dma((2 * nx,)),
            dma((2,)),
            dma((2, chunks, steps)), dma((2, chunks, steps)),
            dma((nz,)), dma((nz,)),
            dma((tiles,)), dma((nw,)),
            dma((nw,)), dma((tiles,)),
            dma((nz,)), dma((nz,)),
            *[dma((chunks, 2))] * 8,
        ],
        compiler_params=pltpu.CompilerParams(
            collective_id=0, has_side_effects=True, vmem_limit_bytes=63 * 1024 * 1024
        ),
        cost_estimate=pl.CostEstimate(
            flops=2 * tokens * features * hidden, bytes_accessed=1 << 23, transcendentals=0
        ),
    )(x_local, g_local, query_ids, clip_bound)


def solution(mesh):
    sizes = tuple(mesh.shape[a] for a in ("dp", "row", "col"))

    def run(activations, out_grads, query_ids, clip_bound):
        placed = (P("dp", "col", "row"), P("dp", "row", "col"), P("dp", None), P())
        return jax.shard_map(
            functools.partial(body, sizes + (query_ids.shape[1],)),
            mesh=mesh, in_specs=placed, out_specs=P("row", "col"), check_vma=False,
        )(activations, out_grads, query_ids, clip_bound)

    return run
```

```python
import functools

import jax
import jax.numpy as jnp
from jax import lax
from jax.experimental import pallas as pl
from jax.experimental.pallas import tpu as pltpu
from jax.sharding import PartitionSpec as P

TILE = 32
LANES = 128
WIDTHS = (256, 256, 256, 256, 256, 256, 128, 128)
FIRST_SLOTS = (0, 0, 1, 2, 3, 4, 5, 5)
MESH = pl.DeviceIdType.MESH


def packed(products):
    lane = lax.broadcasted_iota(jnp.int32, (TILE, LANES), 1)
    row = lax.broadcasted_iota(jnp.int32, (TILE, LANES), 0)
    near = jnp.where(lane <= row, pltpu.roll(products, LANES - TILE, 1), products)
    group = lax.broadcasted_iota(jnp.int32, (8, LANES), 1) // TILE
    out = near[:8]
    for k in range(1, 4):
        out = jnp.where(group == k, pltpu.roll(near[8 * k : 8 * k + 8], TILE * k, 1), out)
    return out


def kernel(
    sizes,
    x_ref, g_ref, ids_ref, clip_ref,
    out_ref,
    ids_vmem, bands, gbuf, xbuf, st, idcol, rows,
    asend, abuf, bsend, bbuf, wz, wall,
    pbuf, rfar, rnear, qbuf,
    lsem, osem, xs, xr, hs, rs, rr, asem, arec, bsem, brec, wsem, wrec, zsem, zrec,
    s1, r1, s2, r2, s3, r3, s4, r4,
):
    ny, nz, nw, tokens = sizes
    nx = nw // 2
    tz = g_ref.shape[0]
    tc = x_ref.shape[0]
    tiles = tz // TILE
    chunks = len(WIDTHS)
    columns = [pl.ds(sum(WIDTHS[:c]), WIDTHS[c]) for c in range(chunks)]
    steps = nz // 2
    wide = bands.shape[1]
    blocks = tokens // LANES
    part = x_ref.shape[1] // ny

    y = lax.axis_index("dp")
    z = lax.axis_index("row")
    w = lax.axis_index("col")
    core = lax.rem(w, 2)
    chip = w // 2

    def z_at(d):
        return lax.rem(z + d, nz)

    def w_at(d):
        return lax.rem(w + d, nw)

    def y_at(d):
        return lax.rem(y + d, ny)

    def copy_to(src, dst, send, recv, **axis):
        return pltpu.make_async_remote_copy(
            src_ref=src, dst_ref=dst, send_sem=send, recv_sem=recv,
            device_id=axis, device_id_type=MESH,
        )

    own_rows = pl.ds(pl.multiple_of(z * tz, 32), tz)
    own_g = [
        pltpu.make_async_copy(
            g_ref.at[:, columns[c]], gbuf[c].at[own_rows], lsem.at[c]
        )
        for c in range(chunks)
    ]
    own_x = pltpu.make_async_copy(
        x_ref, xbuf.at[pl.ds(pl.multiple_of(TILE + w * tc, 32), tc)], lsem.at[chunks]
    )
    own_ids = pltpu.make_async_copy(ids_ref, ids_vmem, lsem.at[chunks + 1])
    for copy in own_g:
        copy.start()
    own_x.start()
    own_ids.start()

    barrier = pltpu.get_barrier_semaphore()
    for d in range(1, nz):
        pl.semaphore_signal(barrier, inc=1, device_id={"row": z_at(d)}, device_id_type=MESH)
    for d in range(1, nw):
        pl.semaphore_signal(barrier, inc=1, device_id={"col": w_at(d)}, device_id_type=MESH)
    for d in range(1, ny):
        pl.semaphore_signal(barrier, inc=1, device_id={"dp": y_at(d)}, device_id_type=MESH)
    pl.semaphore_wait(barrier, nz + nw + ny - 3)

    def x_rows(owner):
        return xbuf.at[pl.ds(pl.multiple_of(TILE + owner * tc, 32), tc)]

    sibling = chip * 2 + 1 - core

    def x_first(d):
        to = sibling if d == 0 else lax.rem(chip + d, nx) * 2 + core
        return copy_to(x_ref, x_rows(w), xs.at[d], xr.at[d], col=to)

    def x_came(d):
        owner = sibling if d == 0 else lax.rem(chip + nx - d, nx) * 2 + core
        return copy_to(x_rows(owner), x_rows(owner), xs.at[d], xr.at[d], col=sibling)

    def x_forward(d):
        owner = lax.rem(chip + nx - d, nx) * 2 + core
        return copy_to(
            x_rows(owner), x_rows(owner), xs.at[nx - 1 + d], xr.at[nx - 1 + d], col=sibling
        )

    def x_forwarded(d):
        owner = lax.rem(chip + nx - d, nx) * 2 + 1 - core
        return copy_to(
            x_rows(owner), x_rows(owner), xs.at[nx - 1 + d], xr.at[nx - 1 + d], col=sibling
        )

    def ring(way, c, s, incoming=False):
        hop = s + 1 if incoming else s
        owner = z_at(nz - hop) if way == 0 else z_at(hop)
        skip, count = 0, tz
        if s == steps - 1:
            skip, count = way * (tz // 2), tz // 2
        elif s == 0 and way == 0:
            count = tz - TILE
        block = gbuf[c].at[pl.ds(pl.multiple_of(owner * tz + skip, 32), count)]
        to = z_at(1) if way == 0 else z_at(nz - 1)
        return copy_to(block, block, rs.at[way, c, s], rr.at[way, c, s], row=to)

    def halo_copy(c, incoming=False):
        owner = z_at(nz - 1) if incoming else z
        there = gbuf[c].at[pl.ds(pl.multiple_of(owner * tz + tz - TILE, 32), TILE)]
        src = there if incoming else g_ref.at[pl.ds(tz - TILE, TILE), columns[c]]
        return copy_to(src, there, hs.at[0, c], hs.at[1, c], row=z_at(1))

    def act_send(d):
        return copy_to(asend.at[d], abuf.at[d], asem.at[d], arec.at[d], row=z_at(d))

    def grad_send(j):
        return copy_to(bsend.at[j], bbuf.at[w], bsem.at[j], brec.at[w], col=j)

    def grad_came(owner):
        return copy_to(bbuf.at[owner], bbuf.at[owner], bsem.at[0], brec.at[owner], col=w_at(1))

    def weight_send(d):
        return copy_to(wz.at[z], wz.at[z], zsem.at[d], zrec.at[d], row=z_at(d))

    def weight_came(d):
        owner = z_at(nz - d)
        return copy_to(wz.at[owner], wz.at[owner], zsem.at[d], zrec.at[d], row=z_at(1))

    def slab_send(d):
        return copy_to(wz, wall.at[w], wsem.at[d], wrec.at[w], col=w_at(d))

    def slab_came(owner):
        return copy_to(wall.at[owner], wall.at[owner], wsem.at[1], wrec.at[owner], col=w_at(1))

    up, far, down = y_at(1), y_at(2), y_at(3)
    half = part // 2

    def quarter(owner, side=None):
        if side is None:
            return pl.ds(pl.multiple_of(owner * part, part), part)
        return pl.ds(pl.multiple_of(owner * part + side * half, half), half)

    def far_send(c, side):
        return copy_to(
            pbuf[c].at[quarter(far, side)], rfar[c].at[side], s1.at[c, side], r1.at[c, side],
            dp=(up, down)[side],
        )

    def near_send(c, side):
        to = (up, down)[side]
        return copy_to(
            pbuf[c].at[quarter(to)], rnear[c].at[side], s2.at[c, side], r2.at[c, side], dp=to
        )

    def out_at(c, where):
        return out_ref.at[where, columns[c]]

    def out_send(c, side, incoming=False):
        at = out_at(c, quarter((down, up)[side] if incoming else y))
        return copy_to(
            at if incoming else qbuf[c], at, s3.at[c, side], r3.at[c, side],
            dp=(up, down)[side],
        )

    def out_forward(c, side, incoming=False):
        at = out_at(c, quarter(far if incoming else (down, up)[side], side))
        return copy_to(at, at, s4.at[c, side], r4.at[c, side], dp=(up, down)[side])

    def out_own(c):
        return pltpu.make_async_copy(qbuf[c], out_at(c, quarter(y)), osem.at[c])

    def product(c):
        depth = tokens // 3 if tokens % (3 * LANES) == 0 else LANES
        for k in range(tokens // depth):
            at = pl.ds(k * depth, depth)
            term = jnp.dot(st[:, at], gbuf[c][at], preferred_element_type=jnp.float32)
            pbuf[c][...] = term if k == 0 else pbuf[c][...] + term
        for side in range(2):
            far_send(c, side).start()

    def near(c):
        for side in range(2):
            far_send(c, side).wait_recv()
            where = quarter((up, down)[side], side)
            pbuf[c][where] = pbuf[c][where] + rfar[c][side]
            near_send(c, side).start()

    def finish(c):
        total = pbuf[c][quarter(y)]
        for side in range(2):
            near_send(c, side).wait_recv()
            total = total + rnear[c][side]
        qbuf[c][...] = total
        for side in range(2):
            out_send(c, side).start()
        out_own(c).start()

    def forward_out(c):
        for side in range(2):
            out_send(c, side, incoming=True).wait_recv()
            out_forward(c, side).start()

    def out_done(c):
        for side in range(2):
            out_forward(c, side, incoming=True).wait_recv()
            far_send(c, side).wait_send()
            near_send(c, side).wait_send()
            out_send(c, side).wait_send()
            out_forward(c, side).wait_send()
        out_own(c).wait()

    def prepare():
        own_ids.wait()
        idcol[0:TILE] = jnp.full((TILE, LANES), -1.0, jnp.float32)
        xbuf[0:TILE] = jnp.zeros((TILE, xbuf.shape[1]), xbuf.dtype)
        lane = lax.broadcasted_iota(jnp.int32, (8, LANES), 1)
        none = jnp.full((8, LANES), -1.0, jnp.float32)
        flat = []
        for b in range(blocks):
            row = ids_vmem[0:1, b * LANES : (b + 1) * LANES].astype(jnp.float32)
            flat.append(jnp.broadcast_to(row, (8, LANES)))
            idcol[TILE + b * LANES : TILE + (b + 1) * LANES] = jnp.broadcast_to(
                row, (LANES, LANES)
            ).T
        for b in range(blocks):
            before = flat[b - 1] if b > 0 else none
            after = flat[b + 1] if b < blocks - 1 else none
            rows[0, b] = flat[b]
            rows[1, b] = jnp.where(
                lane < TILE, after, jnp.where(lane >= LANES - TILE, before, none)
            )

    def grad_bands():
        before = pl.ds(pl.multiple_of(z_at(nz - 1) * tz + tz - TILE, 32), TILE)
        dims = (((1,), (1,)), ((), ()))
        band = jnp.zeros((tz, wide), jnp.float32)
        for c in range(chunks):
            own = gbuf[c][own_rows]
            pad = jnp.zeros((wide - tz - TILE, WIDTHS[c]), own.dtype)
            window = jnp.concatenate([gbuf[c][before], own, pad], 0)
            band = band + lax.dot_general(own, window, dims, preferred_element_type=jnp.float32)
        bands[...] = band
        for j in range(tiles):
            turned = bands[j * TILE : (j + 1) * TILE]
            if j > 0:
                turned = pltpu.roll(turned, wide - j * TILE, 1)
            bsend[j] = packed(turned[:, :LANES])
            @pl.when(w != j)
            def _():
                grad_send(j).start()

    def act_bands():
        x_came(0).wait_recv()
        for d in range(1, nx):
            x_forwarded(d).wait_recv()

        @pl.when(w < tiles)
        def _():
            def one(d, carry):
                first = pl.multiple_of(z_at(d) * tz + w * TILE, 32)
                window = xbuf[pl.ds(first, 2 * TILE)]
                window = jnp.concatenate([window, jnp.zeros_like(window)], 0)
                dims = (((1,), (1,)), ((), ()))
                asend[d] = packed(
                    lax.dot_general(
                        window[TILE : 2 * TILE], window, dims, preferred_element_type=jnp.float32
                    )
                )
                @pl.when(d > 0)
                def _():
                    act_send(d).start()
                return carry
            lax.fori_loop(0, nz, one, 0)

    def weights():
        @pl.when(w < tiles)
        def _():
            act = asend[0]
            for d in range(1, nz):
                act_send(d).wait_recv()
                act = act + abuf[d]
            bbuf[w] = bsend[w]
            for d in range(1, nw):
                grad_came(w_at(d)).wait_recv()
            grad = bbuf[0]
            for u in range(1, nw):
                grad = grad + bbuf[u]
            tile = z * tiles + w
            first = pl.multiple_of(tile * TILE, 32)
            ids = idcol[pl.ds(first, 2 * TILE)]
            lane = lax.broadcasted_iota(jnp.int32, (8, LANES), 1)
            row = lax.broadcasted_iota(jnp.int32, (8, LANES), 0)
            group, partner = lane // TILE, lax.rem(lane, TILE)
            token = row + 8 * group
            mine = ids[TILE : TILE + 8]
            for k in range(1, 4):
                mine = jnp.where(group == k, ids[TILE + 8 * k : TILE + 8 * k + 8], mine)
            wide_lane = lax.broadcasted_iota(jnp.int32, (TILE, LANES), 1)
            wide_row = lax.broadcasted_iota(jnp.int32, (TILE, LANES), 0)
            pick = lax.rem(wide_lane, TILE) == wide_row
            before = jnp.sum(jnp.where(pick, ids[:TILE], 0.0), 0, keepdims=True)
            same = jnp.sum(jnp.where(pick, ids[TILE:], 0.0), 0, keepdims=True)
            theirs = jnp.where(partner <= token, same, before)
            factor = jnp.where(partner == token, 1.0, 2.0)
            factor = jnp.where(partner <= token, factor, jnp.where(tile > 0, 2.0, 0.0))
            term = jnp.where(mine == theirs, act * grad * factor, 0.0)
            at = lax.rem(tile, LANES // TILE) * TILE
            spread = jnp.zeros((8, LANES), jnp.float32)
            for k in range(4):
                one = jnp.sum(jnp.where(group == k, term, 0.0), 1, keepdims=True)
                spread = spread + jnp.where(lane == row + 8 * k + at, one, 0.0)
            wz[z] = jnp.sum(spread, 0, keepdims=True)
            for d in range(1, nz):
                weight_send(d).start()

    def slabs():
        @pl.when(w < tiles)
        def _():
            for d in range(1, nz):
                weight_came(d).wait_recv()
            wall[w] = wz[...]
            for d in range(1, nw):
                slab_send(d).start()

    def scales():
        for u in range(tiles):
            @pl.when(w != u)
            def _():
                slab_came(u).wait_recv()
        lane = lax.broadcasted_iota(jnp.int32, (8, LANES), 1)
        none = jnp.zeros((8, LANES), jnp.float32)
        flat = []
        for b in range(blocks):
            row = none
            for k in range(b * (LANES // TILE), (b + 1) * (LANES // TILE)):
                owner, j = divmod(k, tiles)
                row = row + jnp.broadcast_to(wall[j, owner], (8, LANES))
            flat.append(row)
        for b in range(blocks):
            before = flat[b - 1] if b > 0 else none
            after = flat[b + 1] if b < blocks - 1 else none
            rows[2, b] = flat[b]
            rows[3, b] = jnp.where(
                lane < TILE, after, jnp.where(lane >= LANES - TILE, before, none)
            )
        limit = clip_ref[0].astype(jnp.float32)

        def one(b, carry):
            at = pl.multiple_of(TILE + b * LANES, 32)
            ids = idcol[pl.ds(at, LANES)]
            found = jnp.where(ids == rows[0, b][0:1], rows[2, b][0:1], 0.0)
            found = found + jnp.where(ids == rows[1, b][0:1], rows[3, b][0:1], 0.0)
            squares = jnp.sum(found, 1, keepdims=True)
            factor = limit / jnp.maximum(jnp.sqrt(jnp.maximum(squares, 0.0)), limit)
            scaled = xbuf[pl.ds(at, LANES)].astype(jnp.float32) * factor
            st[:, pl.ds(pl.multiple_of(b * LANES, LANES), LANES)] = scaled.T.astype(st.dtype)
            return carry

        lax.fori_loop(0, blocks, one, 0)

    def forward_x():
        for d in range(1, nx):
            x_came(d).wait_recv()
            x_forward(d).start()

    first_slot = FIRST_SLOTS
    final_slot = first_slot[-1] + steps
    between = {0: (prepare,), 1: (grad_bands,), 2: (forward_x,), 3: (act_bands,), 4: (weights,),
               5: (slabs,), 6: (scales,)}

    def ring_sent(c):
        for s in range(steps):
            for way in range(2):
                ring(way, c, s).wait_send()

    own_x.wait()
    for d in range(nx):
        x_first(d).start()

    def hop(t, c):
        s = t - first_slot[c]
        if 0 <= s < steps:
            if t == 0:
                own_g[c].wait()
            for way in range(2):
                if s > 0:
                    ring(way, c, s - 1, incoming=True).wait_recv()
                ring(way, c, s).start()

    def first(c):
        for way in range(2):
            ring(way, c, steps - 1, incoming=True).wait_recv()
        product(c)
        ring_sent(c)

    def stages(p):
        for c in range(chunks):
            stage = p - 2 * (first_slot[c] + steps) - c % 2
            if 0 <= stage < 5:
                (first, near, finish, forward_out, out_done)[stage](c)

    for c in range(chunks):
        halo_copy(c).start()
    for t in range(final_slot):
        if t == 1:
            for c in range(chunks):
                halo_copy(c, incoming=True).wait_recv()
                if first_slot[c] > 0:
                    own_g[c].wait()
        for c in range(0, chunks, 2):
            hop(t, c)
        for step in between.get(t, ()):
            step()
        stages(2 * t)
        for c in range(1, chunks, 2):
            hop(t, c)
        stages(2 * t + 1)

    for c in range(chunks):
        halo_copy(c).wait_send()
    for d in range(nx):
        x_first(d).wait_send()
    for d in range(1, nx):
        x_forward(d).wait_send()
    for j in range(tiles):
        @pl.when(w != j)
        def _():
            grad_send(j).wait_send()

    @pl.when(w < tiles)
    def _():
        for d in range(1, nz):
            act_send(d).wait_send()
            weight_send(d).wait_send()
        for d in range(1, nw):
            slab_send(d).wait_send()

    for p in range(2 * final_slot, 2 * final_slot + 6):
        stages(p)


def body(sizes, activations, out_grads, query_ids, clip_bound):
    x_local = activations[0]
    g_local = out_grads[0]
    ny, nz, nw, tokens = sizes
    nx = nw // 2
    features, hidden = x_local.shape[1], g_local.shape[1]
    tz = g_local.shape[0]
    tiles = tz // TILE
    chunks = len(WIDTHS)
    assert sum(WIDTHS) == hidden
    steps = nz // 2
    part = features // ny
    dma = pltpu.SemaphoreType.DMA
    f32, bf16 = jnp.float32, jnp.bfloat16
    return pl.pallas_call(
        functools.partial(kernel, sizes),
        out_shape=jax.ShapeDtypeStruct((features, hidden), f32),
        in_specs=[
            pl.BlockSpec(memory_space=pltpu.HBM),
            pl.BlockSpec(memory_space=pltpu.HBM),
            pl.BlockSpec(memory_space=pltpu.HBM),
            pl.BlockSpec(memory_space=pltpu.SMEM),
        ],
        out_specs=pl.BlockSpec(memory_space=pl.ANY),
        scratch_shapes=[
            pltpu.VMEM((1, tokens), jnp.int32),
            pltpu.VMEM((tz, -(-(tz + TILE) // LANES) * LANES), f32),
            [pltpu.VMEM((tokens, n), bf16) for n in WIDTHS],
            pltpu.VMEM((TILE + tokens, features), bf16),
            pltpu.VMEM((features, tokens), bf16),
            pltpu.VMEM((TILE + tokens, LANES), f32),
            pltpu.VMEM((4, tokens // LANES, 8, LANES), f32),
            pltpu.VMEM((nz, 8, LANES), f32),
            pltpu.VMEM((nz, 8, LANES), f32),
            pltpu.VMEM((tiles, 8, LANES), f32),
            pltpu.VMEM((nw, 8, LANES), f32),
            pltpu.VMEM((nz, 1, LANES), f32),
            pltpu.VMEM((tiles, nz, 1, LANES), f32),
            [pltpu.VMEM((features, n), f32) for n in WIDTHS],
            [pltpu.VMEM((2, part // 2, n), f32) for n in WIDTHS],
            [pltpu.VMEM((2, part, n), f32) for n in WIDTHS],
            [pltpu.VMEM((part, n), f32) for n in WIDTHS],
            dma((chunks + 2,)), dma((chunks,)),
            dma((2 * nx,)), dma((2 * nx,)),
            dma((2, chunks)),
            dma((2, chunks, steps)), dma((2, chunks, steps)),
            dma((nz,)), dma((nz,)),
            dma((tiles,)), dma((nw,)),
            dma((nw,)), dma((tiles,)),
            dma((nz,)), dma((nz,)),
            *[dma((chunks, 2))] * 8,
        ],
        compiler_params=pltpu.CompilerParams(
            collective_id=0, has_side_effects=True, vmem_limit_bytes=63 * 1024 * 1024
        ),
        cost_estimate=pl.CostEstimate(
            flops=2 * tokens * features * hidden, bytes_accessed=1 << 23, transcendentals=0
        ),
    )(x_local, g_local, query_ids, clip_bound)


def solution(mesh):
    sizes = tuple(mesh.shape[a] for a in ("dp", "row", "col"))

    def run(activations, out_grads, query_ids, clip_bound):
        placed = (P("dp", "col", "row"), P("dp", "row", "col"), P("dp", None), P())
        return jax.shard_map(
            functools.partial(body, sizes + (query_ids.shape[1],)),
            mesh=mesh, in_specs=placed, out_specs=P("row", "col"), check_vma=False,
        )(activations, out_grads, query_ids, clip_bound)

    return run
```

```python
import functools

import jax
import jax.numpy as jnp
from jax import lax
from jax.experimental import pallas as pl
from jax.experimental.pallas import tpu as pltpu
from jax.sharding import PartitionSpec as P

TILE = 32
LANES = 128
WIDTHS = (256, 256, 256, 256, 256, 256, 256)
FIRST_SLOTS = (0, 0, 1, 2, 3, 5, 6)
MESH = pl.DeviceIdType.MESH


def packed(products):
    lane = lax.broadcasted_iota(jnp.int32, (TILE, LANES), 1)
    row = lax.broadcasted_iota(jnp.int32, (TILE, LANES), 0)
    near = jnp.where(lane <= row, pltpu.roll(products, LANES - TILE, 1), products)
    group = lax.broadcasted_iota(jnp.int32, (8, LANES), 1) // TILE
    out = near[:8]
    for k in range(1, 4):
        out = jnp.where(group == k, pltpu.roll(near[8 * k : 8 * k + 8], TILE * k, 1), out)
    return out


def kernel(
    sizes,
    x_ref, g_ref, ids_ref, clip_ref,
    out_ref,
    ids_vmem, bands, gbuf, xbuf, st, idcol, rows,
    asend, abuf, bsend, bbuf, wz, wall,
    pbuf, rfar, rnear, qbuf,
    lsem, osem, xs, xr, hs, rs, rr, asem, arec, bsem, brec, wsem, wrec, zsem, zrec,
    s1, r1, s2, r2, s3, r3, s4, r4,
):
    ny, nz, nw, tokens = sizes
    nx = nw // 2
    tz = g_ref.shape[0]
    tc = x_ref.shape[0]
    tiles = tz // TILE
    chunks = len(WIDTHS)
    columns = [pl.ds(sum(WIDTHS[:c]), WIDTHS[c]) for c in range(chunks)]
    steps = nz // 2
    wide = bands.shape[1]
    blocks = tokens // LANES
    part = x_ref.shape[1] // ny

    y = lax.axis_index("dp")
    z = lax.axis_index("row")
    w = lax.axis_index("col")
    core = lax.rem(w, 2)
    chip = w // 2

    def z_at(d):
        return lax.rem(z + d, nz)

    def w_at(d):
        return lax.rem(w + d, nw)

    def y_at(d):
        return lax.rem(y + d, ny)

    def copy_to(src, dst, send, recv, **axis):
        return pltpu.make_async_remote_copy(
            src_ref=src, dst_ref=dst, send_sem=send, recv_sem=recv,
            device_id=axis, device_id_type=MESH,
        )

    own_rows = pl.ds(pl.multiple_of(z * tz, 32), tz)
    own_g = [
        pltpu.make_async_copy(
            g_ref.at[:, columns[c]], gbuf[c].at[own_rows], lsem.at[c]
        )
        for c in range(chunks)
    ]
    own_x = pltpu.make_async_copy(
        x_ref, xbuf.at[pl.ds(pl.multiple_of(TILE + w * tc, 32), tc)], lsem.at[chunks]
    )
    own_ids = pltpu.make_async_copy(ids_ref, ids_vmem, lsem.at[chunks + 1])
    for copy in own_g:
        copy.start()
    own_x.start()
    own_ids.start()

    barrier = pltpu.get_barrier_semaphore()
    for d in range(1, nz):
        pl.semaphore_signal(barrier, inc=1, device_id={"row": z_at(d)}, device_id_type=MESH)
    for d in range(1, nw):
        pl.semaphore_signal(barrier, inc=1, device_id={"col": w_at(d)}, device_id_type=MESH)
    for d in range(1, ny):
        pl.semaphore_signal(barrier, inc=1, device_id={"dp": y_at(d)}, device_id_type=MESH)
    pl.semaphore_wait(barrier, nz + nw + ny - 3)

    def x_rows(owner):
        return xbuf.at[pl.ds(pl.multiple_of(TILE + owner * tc, 32), tc)]

    sibling = chip * 2 + 1 - core

    def x_first(d):
        to = sibling if d == 0 else lax.rem(chip + d, nx) * 2 + core
        return copy_to(x_ref, x_rows(w), xs.at[d], xr.at[d], col=to)

    def x_came(d):
        owner = sibling if d == 0 else lax.rem(chip + nx - d, nx) * 2 + core
        return copy_to(x_rows(owner), x_rows(owner), xs.at[d], xr.at[d], col=sibling)

    def x_forward(d):
        owner = lax.rem(chip + nx - d, nx) * 2 + core
        return copy_to(
            x_rows(owner), x_rows(owner), xs.at[nx - 1 + d], xr.at[nx - 1 + d], col=sibling
        )

    def x_forwarded(d):
        owner = lax.rem(chip + nx - d, nx) * 2 + 1 - core
        return copy_to(
            x_rows(owner), x_rows(owner), xs.at[nx - 1 + d], xr.at[nx - 1 + d], col=sibling
        )

    def ring(way, c, s, incoming=False):
        hop = s + 1 if incoming else s
        owner = z_at(nz - hop) if way == 0 else z_at(hop)
        skip, count = 0, tz
        if s == steps - 1:
            skip, count = way * (tz // 2), tz // 2
        elif s == 0 and way == 0:
            count = tz - TILE
        block = gbuf[c].at[pl.ds(pl.multiple_of(owner * tz + skip, 32), count)]
        to = z_at(1) if way == 0 else z_at(nz - 1)
        return copy_to(block, block, rs.at[way, c, s], rr.at[way, c, s], row=to)

    def halo_copy(c, incoming=False):
        owner = z_at(nz - 1) if incoming else z
        there = gbuf[c].at[pl.ds(pl.multiple_of(owner * tz + tz - TILE, 32), TILE)]
        src = there if incoming else g_ref.at[pl.ds(tz - TILE, TILE), columns[c]]
        return copy_to(src, there, hs.at[0, c], hs.at[1, c], row=z_at(1))

    def act_send(d):
        return copy_to(asend.at[d], abuf.at[d], asem.at[d], arec.at[d], row=z_at(d))

    def grad_send(j):
        return copy_to(bsend.at[j], bbuf.at[w], bsem.at[j], brec.at[w], col=j)

    def grad_came(owner):
        return copy_to(bbuf.at[owner], bbuf.at[owner], bsem.at[0], brec.at[owner], col=w_at(1))

    def weight_send(d):
        return copy_to(wz.at[z], wz.at[z], zsem.at[d], zrec.at[d], row=z_at(d))

    def weight_came(d):
        owner = z_at(nz - d)
        return copy_to(wz.at[owner], wz.at[owner], zsem.at[d], zrec.at[d], row=z_at(1))

    def slab_send(d):
        return copy_to(wz, wall.at[w], wsem.at[d], wrec.at[w], col=w_at(d))

    def slab_came(owner):
        return copy_to(wall.at[owner], wall.at[owner], wsem.at[1], wrec.at[owner], col=w_at(1))

    up, far, down = y_at(1), y_at(2), y_at(3)
    half = part // 2

    def quarter(owner, side=None):
        if side is None:
            return pl.ds(pl.multiple_of(owner * part, part), part)
        return pl.ds(pl.multiple_of(owner * part + side * half, half), half)

    def far_send(c, side):
        return copy_to(
            pbuf[c].at[quarter(far, side)], rfar[c].at[side], s1.at[c, side], r1.at[c, side],
            dp=(up, down)[side],
        )

    def near_send(c, side):
        to = (up, down)[side]
        return copy_to(
            pbuf[c].at[quarter(to)], rnear[c].at[side], s2.at[c, side], r2.at[c, side], dp=to
        )

    def out_at(c, where):
        return out_ref.at[where, columns[c]]

    def out_send(c, side, incoming=False):
        at = out_at(c, quarter((down, up)[side] if incoming else y))
        return copy_to(
            at if incoming else qbuf[c], at, s3.at[c, side], r3.at[c, side],
            dp=(up, down)[side],
        )

    def out_forward(c, side, incoming=False):
        at = out_at(c, quarter(far if incoming else (down, up)[side], side))
        return copy_to(at, at, s4.at[c, side], r4.at[c, side], dp=(up, down)[side])

    def out_own(c):
        return pltpu.make_async_copy(qbuf[c], out_at(c, quarter(y)), osem.at[c])

    def product(c):
        depth = tokens // 3 if tokens % (3 * LANES) == 0 else LANES
        for k in range(tokens // depth):
            at = pl.ds(k * depth, depth)
            term = jnp.dot(st[:, at], gbuf[c][at], preferred_element_type=jnp.float32)
            pbuf[c][...] = term if k == 0 else pbuf[c][...] + term
        for side in range(2):
            far_send(c, side).start()

    def product_pair(c, i):
        pair = lax.rem(lax.rem(z + steps, nz) // 2 + i, steps)
        at = pl.ds(pl.multiple_of(pair * 2 * tz, LANES), 2 * tz)
        return jnp.dot(st[:, at], gbuf[c][at], preferred_element_type=jnp.float32)

    def product_most(c):
        pbuf[c][...] = product_pair(c, 1)

        def one(i, carry):
            pbuf[c][...] = pbuf[c][...] + product_pair(c, i)
            return carry

        lax.fori_loop(2, steps, one, 0)

    def product_rest(c):
        pbuf[c][...] = pbuf[c][...] + product_pair(c, 0)
        for side in range(2):
            far_send(c, side).start()

    def near(c):
        for side in range(2):
            far_send(c, side).wait_recv()
            where = quarter((up, down)[side], side)
            pbuf[c][where] = pbuf[c][where] + rfar[c][side]
            near_send(c, side).start()

    def finish(c):
        total = pbuf[c][quarter(y)]
        for side in range(2):
            near_send(c, side).wait_recv()
            total = total + rnear[c][side]
        qbuf[c][...] = total
        for side in range(2):
            out_send(c, side).start()
        out_own(c).start()

    def forward_out(c):
        for side in range(2):
            out_send(c, side, incoming=True).wait_recv()
            out_forward(c, side).start()

    def out_done(c):
        for side in range(2):
            out_forward(c, side, incoming=True).wait_recv()
            far_send(c, side).wait_send()
            near_send(c, side).wait_send()
            out_send(c, side).wait_send()
            out_forward(c, side).wait_send()
        out_own(c).wait()

    def prepare():
        own_ids.wait()
        idcol[0:TILE] = jnp.full((TILE, LANES), -1.0, jnp.float32)
        xbuf[0:TILE] = jnp.zeros((TILE, xbuf.shape[1]), xbuf.dtype)
        lane = lax.broadcasted_iota(jnp.int32, (8, LANES), 1)
        none = jnp.full((8, LANES), -1.0, jnp.float32)
        flat = []
        for b in range(blocks):
            row = ids_vmem[0:1, b * LANES : (b + 1) * LANES].astype(jnp.float32)
            flat.append(jnp.broadcast_to(row, (8, LANES)))
            idcol[TILE + b * LANES : TILE + (b + 1) * LANES] = jnp.broadcast_to(
                row, (LANES, LANES)
            ).T
        for b in range(blocks):
            before = flat[b - 1] if b > 0 else none
            after = flat[b + 1] if b < blocks - 1 else none
            rows[0, b] = flat[b]
            rows[1, b] = jnp.where(
                lane < TILE, after, jnp.where(lane >= LANES - TILE, before, none)
            )

    def grad_bands():
        before = pl.ds(pl.multiple_of(z_at(nz - 1) * tz + tz - TILE, 32), TILE)
        dims = (((1,), (1,)), ((), ()))
        band = jnp.zeros((tz, wide), jnp.float32)
        for c in range(chunks):
            own = gbuf[c][own_rows]
            pad = jnp.zeros((wide - tz - TILE, WIDTHS[c]), own.dtype)
            window = jnp.concatenate([gbuf[c][before], own, pad], 0)
            band = band + lax.dot_general(own, window, dims, preferred_element_type=jnp.float32)
        bands[...] = band
        for j in range(tiles):
            turned = bands[j * TILE : (j + 1) * TILE]
            if j > 0:
                turned = pltpu.roll(turned, wide - j * TILE, 1)
            bsend[j] = packed(turned[:, :LANES])
            @pl.when(w != j)
            def _():
                grad_send(j).start()

    def act_bands():
        x_came(0).wait_recv()
        for d in range(1, nx):
            x_forwarded(d).wait_recv()

        @pl.when(w < tiles)
        def _():
            def one(d, carry):
                first = pl.multiple_of(z_at(d) * tz + w * TILE, 32)
                window = xbuf[pl.ds(first, 2 * TILE)]
                window = jnp.concatenate([window, jnp.zeros_like(window)], 0)
                dims = (((1,), (1,)), ((), ()))
                asend[d] = packed(
                    lax.dot_general(
                        window[TILE : 2 * TILE], window, dims, preferred_element_type=jnp.float32
                    )
                )
                @pl.when(d > 0)
                def _():
                    act_send(d).start()
                return carry
            lax.fori_loop(0, nz, one, 0)

    def weights():
        @pl.when(w < tiles)
        def _():
            act = asend[0]
            for d in range(1, nz):
                act_send(d).wait_recv()
                act = act + abuf[d]
            bbuf[w] = bsend[w]
            for d in range(1, nw):
                grad_came(w_at(d)).wait_recv()
            grad = bbuf[0]
            for u in range(1, nw):
                grad = grad + bbuf[u]
            tile = z * tiles + w
            first = pl.multiple_of(tile * TILE, 32)
            ids = idcol[pl.ds(first, 2 * TILE)]
            lane = lax.broadcasted_iota(jnp.int32, (8, LANES), 1)
            row = lax.broadcasted_iota(jnp.int32, (8, LANES), 0)
            group, partner = lane // TILE, lax.rem(lane, TILE)
            token = row + 8 * group
            mine = ids[TILE : TILE + 8]
            for k in range(1, 4):
                mine = jnp.where(group == k, ids[TILE + 8 * k : TILE + 8 * k + 8], mine)
            wide_lane = lax.broadcasted_iota(jnp.int32, (TILE, LANES), 1)
            wide_row = lax.broadcasted_iota(jnp.int32, (TILE, LANES), 0)
            pick = lax.rem(wide_lane, TILE) == wide_row
            before = jnp.sum(jnp.where(pick, ids[:TILE], 0.0), 0, keepdims=True)
            same = jnp.sum(jnp.where(pick, ids[TILE:], 0.0), 0, keepdims=True)
            theirs = jnp.where(partner <= token, same, before)
            factor = jnp.where(partner == token, 1.0, 2.0)
            factor = jnp.where(partner <= token, factor, jnp.where(tile > 0, 2.0, 0.0))
            term = jnp.where(mine == theirs, act * grad * factor, 0.0)
            at = lax.rem(tile, LANES // TILE) * TILE
            spread = jnp.zeros((8, LANES), jnp.float32)
            for k in range(4):
                one = jnp.sum(jnp.where(group == k, term, 0.0), 1, keepdims=True)
                spread = spread + jnp.where(lane == row + 8 * k + at, one, 0.0)
            wz[z] = jnp.sum(spread, 0, keepdims=True)
            for d in range(1, nz):
                weight_send(d).start()

    def slabs():
        @pl.when(w < tiles)
        def _():
            for d in range(1, nz):
                weight_came(d).wait_recv()
            wall[w] = wz[...]
            for d in range(1, nw):
                slab_send(d).start()

    def scales():
        for u in range(tiles):
            @pl.when(w != u)
            def _():
                slab_came(u).wait_recv()
        lane = lax.broadcasted_iota(jnp.int32, (8, LANES), 1)
        none = jnp.zeros((8, LANES), jnp.float32)
        flat = []
        for b in range(blocks):
            row = none
            for k in range(b * (LANES // TILE), (b + 1) * (LANES // TILE)):
                owner, j = divmod(k, tiles)
                row = row + jnp.broadcast_to(wall[j, owner], (8, LANES))
            flat.append(row)
        for b in range(blocks):
            before = flat[b - 1] if b > 0 else none
            after = flat[b + 1] if b < blocks - 1 else none
            rows[2, b] = flat[b]
            rows[3, b] = jnp.where(
                lane < TILE, after, jnp.where(lane >= LANES - TILE, before, none)
            )
        limit = clip_ref[0].astype(jnp.float32)

        def one(b, carry):
            at = pl.multiple_of(TILE + b * LANES, 32)
            ids = idcol[pl.ds(at, LANES)]
            found = jnp.where(ids == rows[0, b][0:1], rows[2, b][0:1], 0.0)
            found = found + jnp.where(ids == rows[1, b][0:1], rows[3, b][0:1], 0.0)
            squares = jnp.sum(found, 1, keepdims=True)
            factor = limit / jnp.maximum(jnp.sqrt(jnp.maximum(squares, 0.0)), limit)
            scaled = xbuf[pl.ds(at, LANES)].astype(jnp.float32) * factor
            st[:, pl.ds(pl.multiple_of(b * LANES, LANES), LANES)] = scaled.T.astype(st.dtype)
            return carry

        lax.fori_loop(0, blocks, one, 0)

    def forward_x():
        for d in range(1, nx):
            x_came(d).wait_recv()
            x_forward(d).start()

    first_slot = FIRST_SLOTS
    final_slot = first_slot[-1] + steps
    between = {0: (prepare,), 1: (grad_bands,), 2: (forward_x,), 3: (act_bands,), 4: (weights,),
               5: (slabs,), 6: (scales,)}

    def ring_sent(c):
        for s in range(steps):
            for way in range(2):
                ring(way, c, s).wait_send()

    own_x.wait()
    for d in range(nx):
        x_first(d).start()

    def hop(t, c):
        s = t - first_slot[c]
        if 0 <= s < steps:
            if t == 0:
                own_g[c].wait()
            for way in range(2):
                if s > 0:
                    ring(way, c, s - 1, incoming=True).wait_recv()
                ring(way, c, s).start()

    def first(c):
        for way in range(2):
            ring(way, c, steps - 1, incoming=True).wait_recv()
        if c == chunks - 1:
            product_rest(c)
        else:
            product(c)
        ring_sent(c)

    def stages(p):
        for c in range(chunks):
            stage, between_stages = divmod(p - 2 * (first_slot[c] + steps) - c % 2, 2)
            if 0 <= stage < 5 and between_stages == 0:
                (first, near, finish, forward_out, out_done)[stage](c)

    for c in range(chunks):
        halo_copy(c).start()
    for t in range(final_slot):
        if t == 1:
            for c in range(chunks):
                halo_copy(c, incoming=True).wait_recv()
                if first_slot[c] > 0:
                    own_g[c].wait()
        for c in range(0, chunks, 2):
            hop(t, c)
        for step in between.get(t, ()):
            step()
        stages(2 * t)
        for c in range(1, chunks, 2):
            hop(t, c)
        stages(2 * t + 1)
    product_most(chunks - 1)

    for c in range(chunks):
        halo_copy(c).wait_send()
    for d in range(nx):
        x_first(d).wait_send()
    for d in range(1, nx):
        x_forward(d).wait_send()
    for j in range(tiles):
        @pl.when(w != j)
        def _():
            grad_send(j).wait_send()

    @pl.when(w < tiles)
    def _():
        for d in range(1, nz):
            act_send(d).wait_send()
            weight_send(d).wait_send()
        for d in range(1, nw):
            slab_send(d).wait_send()

    for p in range(2 * final_slot, 2 * final_slot + 10):
        stages(p)


def body(sizes, activations, out_grads, query_ids, clip_bound):
    x_local = activations[0]
    g_local = out_grads[0]
    ny, nz, nw, tokens = sizes
    nx = nw // 2
    features, hidden = x_local.shape[1], g_local.shape[1]
    tz = g_local.shape[0]
    tiles = tz // TILE
    chunks = len(WIDTHS)
    assert sum(WIDTHS) == hidden
    steps = nz // 2
    part = features // ny
    dma = pltpu.SemaphoreType.DMA
    f32, bf16 = jnp.float32, jnp.bfloat16
    return pl.pallas_call(
        functools.partial(kernel, sizes),
        out_shape=jax.ShapeDtypeStruct((features, hidden), f32),
        in_specs=[
            pl.BlockSpec(memory_space=pltpu.HBM),
            pl.BlockSpec(memory_space=pltpu.HBM),
            pl.BlockSpec(memory_space=pltpu.HBM),
            pl.BlockSpec(memory_space=pltpu.SMEM),
        ],
        out_specs=pl.BlockSpec(memory_space=pl.ANY),
        scratch_shapes=[
            pltpu.VMEM((1, tokens), jnp.int32),
            pltpu.VMEM((tz, -(-(tz + TILE) // LANES) * LANES), f32),
            [pltpu.VMEM((tokens, n), bf16) for n in WIDTHS],
            pltpu.VMEM((TILE + tokens, features), bf16),
            pltpu.VMEM((features, tokens), bf16),
            pltpu.VMEM((TILE + tokens, LANES), f32),
            pltpu.VMEM((4, tokens // LANES, 8, LANES), f32),
            pltpu.VMEM((nz, 8, LANES), f32),
            pltpu.VMEM((nz, 8, LANES), f32),
            pltpu.VMEM((tiles, 8, LANES), f32),
            pltpu.VMEM((nw, 8, LANES), f32),
            pltpu.VMEM((nz, 1, LANES), f32),
            pltpu.VMEM((tiles, nz, 1, LANES), f32),
            [pltpu.VMEM((features, n), f32) for n in WIDTHS],
            [pltpu.VMEM((2, part // 2, n), f32) for n in WIDTHS],
            [pltpu.VMEM((2, part, n), f32) for n in WIDTHS],
            [pltpu.VMEM((part, n), f32) for n in WIDTHS],
            dma((chunks + 2,)), dma((chunks,)),
            dma((2 * nx,)), dma((2 * nx,)),
            dma((2, chunks)),
            dma((2, chunks, steps)), dma((2, chunks, steps)),
            dma((nz,)), dma((nz,)),
            dma((tiles,)), dma((nw,)),
            dma((nw,)), dma((tiles,)),
            dma((nz,)), dma((nz,)),
            *[dma((chunks, 2))] * 8,
        ],
        compiler_params=pltpu.CompilerParams(
            collective_id=0, has_side_effects=True, vmem_limit_bytes=63 * 1024 * 1024
        ),
        cost_estimate=pl.CostEstimate(
            flops=2 * tokens * features * hidden, bytes_accessed=1 << 23, transcendentals=0
        ),
    )(x_local, g_local, query_ids, clip_bound)


def solution(mesh):
    sizes = tuple(mesh.shape[a] for a in ("dp", "row", "col"))

    def run(activations, out_grads, query_ids, clip_bound):
        placed = (P("dp", "col", "row"), P("dp", "row", "col"), P("dp", None), P())
        return jax.shard_map(
            functools.partial(body, sizes + (query_ids.shape[1],)),
            mesh=mesh, in_specs=placed, out_specs=P("row", "col"), check_vma=False,
        )(activations, out_grads, query_ids, clip_bound)

    return run
```

```python
import functools

import jax
import jax.numpy as jnp
from jax import lax
from jax.experimental import pallas as pl
from jax.experimental.pallas import tpu as pltpu
from jax.sharding import PartitionSpec as P

TILE = 32
LANES = 128
WIDTHS = (256, 256, 256, 256, 256, 256, 256)
FIRST_SLOTS = (0, 0, 1, 2, 3, 5, 6)
MESH = pl.DeviceIdType.MESH


def packed(products):
    lane = lax.broadcasted_iota(jnp.int32, (TILE, LANES), 1)
    row = lax.broadcasted_iota(jnp.int32, (TILE, LANES), 0)
    near = jnp.where(lane <= row, pltpu.roll(products, LANES - TILE, 1), products)
    group = lax.broadcasted_iota(jnp.int32, (8, LANES), 1) // TILE
    out = near[:8]
    for k in range(1, 4):
        out = jnp.where(group == k, pltpu.roll(near[8 * k : 8 * k + 8], TILE * k, 1), out)
    return out


def kernel(
    sizes,
    x_ref, g_ref, ids_ref, clip_ref,
    out_ref,
    ids_vmem, bands, gbuf, xbuf, st, idcol, rows,
    asend, abuf, bsend, bbuf, wz, wall,
    pbuf, rfar, rnear, qbuf,
    lsem, osem, xs, xr, hs, rs, rr, asem, arec, bsem, brec, wsem, wrec, zsem, zrec,
    s1, r1, s2, r2, s3, r3, s4, r4,
):
    ny, nz, nw, tokens = sizes
    nx = nw // 2
    tz = g_ref.shape[0]
    tc = x_ref.shape[0]
    tiles = tz // TILE
    chunks = len(WIDTHS)
    columns = [pl.ds(sum(WIDTHS[:c]), WIDTHS[c]) for c in range(chunks)]
    steps = nz // 2
    wide = bands.shape[1]
    blocks = tokens // LANES
    part = x_ref.shape[1] // ny

    y = lax.axis_index("dp")
    z = lax.axis_index("row")
    w = lax.axis_index("col")
    core = lax.rem(w, 2)
    chip = w // 2

    def z_at(d):
        return lax.rem(z + d, nz)

    def w_at(d):
        return lax.rem(w + d, nw)

    def y_at(d):
        return lax.rem(y + d, ny)

    def copy_to(src, dst, send, recv, **axis):
        return pltpu.make_async_remote_copy(
            src_ref=src, dst_ref=dst, send_sem=send, recv_sem=recv,
            device_id=axis, device_id_type=MESH,
        )

    own_rows = pl.ds(pl.multiple_of(z * tz, 32), tz)
    own_g = [
        pltpu.make_async_copy(
            g_ref.at[:, columns[c]], gbuf[c].at[own_rows], lsem.at[c]
        )
        for c in range(chunks)
    ]
    own_x = pltpu.make_async_copy(
        x_ref, xbuf.at[pl.ds(pl.multiple_of(TILE + w * tc, 32), tc)], lsem.at[chunks]
    )
    own_ids = pltpu.make_async_copy(ids_ref, ids_vmem, lsem.at[chunks + 1])
    for copy in own_g:
        copy.start()
    own_x.start()
    own_ids.start()

    barrier = pltpu.get_barrier_semaphore()
    for d in range(1, nz):
        pl.semaphore_signal(barrier, inc=1, device_id={"row": z_at(d)}, device_id_type=MESH)
    for d in range(1, nw):
        pl.semaphore_signal(barrier, inc=1, device_id={"col": w_at(d)}, device_id_type=MESH)
    for d in range(1, ny):
        pl.semaphore_signal(barrier, inc=1, device_id={"dp": y_at(d)}, device_id_type=MESH)
    pl.semaphore_wait(barrier, nz + nw + ny - 3)

    def x_rows(owner):
        return xbuf.at[pl.ds(pl.multiple_of(TILE + owner * tc, 32), tc)]

    sibling = chip * 2 + 1 - core

    def x_first(d):
        to = sibling if d == 0 else lax.rem(chip + d, nx) * 2 + core
        return copy_to(x_ref, x_rows(w), xs.at[d], xr.at[d], col=to)

    def x_came(d):
        owner = sibling if d == 0 else lax.rem(chip + nx - d, nx) * 2 + core
        return copy_to(x_rows(owner), x_rows(owner), xs.at[d], xr.at[d], col=sibling)

    def x_forward(d):
        owner = lax.rem(chip + nx - d, nx) * 2 + core
        return copy_to(
            x_rows(owner), x_rows(owner), xs.at[nx - 1 + d], xr.at[nx - 1 + d], col=sibling
        )

    def x_forwarded(d):
        owner = lax.rem(chip + nx - d, nx) * 2 + 1 - core
        return copy_to(
            x_rows(owner), x_rows(owner), xs.at[nx - 1 + d], xr.at[nx - 1 + d], col=sibling
        )

    def ring(way, c, s, incoming=False):
        hop = s + 1 if incoming else s
        owner = z_at(nz - hop) if way == 0 else z_at(hop)
        skip, count = 0, tz
        if s == steps - 1:
            skip, count = way * (tz // 2), tz // 2
        elif s == 0 and way == 0:
            count = tz - TILE
        block = gbuf[c].at[pl.ds(pl.multiple_of(owner * tz + skip, 32), count)]
        src = block
        if s == 0 and not incoming:
            src = g_ref.at[pl.ds(0, count), columns[c]]
        to = z_at(1) if way == 0 else z_at(nz - 1)
        return copy_to(src, block, rs.at[way, c, s], rr.at[way, c, s], row=to)

    def halo_copy(c, incoming=False):
        owner = z_at(nz - 1) if incoming else z
        there = gbuf[c].at[pl.ds(pl.multiple_of(owner * tz + tz - TILE, 32), TILE)]
        src = there if incoming else g_ref.at[pl.ds(tz - TILE, TILE), columns[c]]
        return copy_to(src, there, hs.at[0, c], hs.at[1, c], row=z_at(1))

    def act_send(d):
        return copy_to(asend.at[d], abuf.at[d], asem.at[d], arec.at[d], row=z_at(d))

    def grad_send(j):
        return copy_to(bsend.at[j], bbuf.at[w], bsem.at[j], brec.at[w], col=j)

    def grad_came(owner):
        return copy_to(bbuf.at[owner], bbuf.at[owner], bsem.at[0], brec.at[owner], col=w_at(1))

    def weight_send(d):
        return copy_to(wz.at[z], wz.at[z], zsem.at[d], zrec.at[d], row=z_at(d))

    def weight_came(d):
        owner = z_at(nz - d)
        return copy_to(wz.at[owner], wz.at[owner], zsem.at[d], zrec.at[d], row=z_at(1))

    def slab_send(d):
        return copy_to(wz, wall.at[w], wsem.at[d], wrec.at[w], col=w_at(d))

    def slab_came(owner):
        return copy_to(wall.at[owner], wall.at[owner], wsem.at[1], wrec.at[owner], col=w_at(1))

    up, far, down = y_at(1), y_at(2), y_at(3)
    half = part // 2

    def quarter(owner, side=None):
        if side is None:
            return pl.ds(pl.multiple_of(owner * part, part), part)
        return pl.ds(pl.multiple_of(owner * part + side * half, half), half)

    def far_send(c, side):
        return copy_to(
            pbuf[c].at[quarter(far, side)], rfar[c].at[side], s1.at[c, side], r1.at[c, side],
            dp=(up, down)[side],
        )

    def near_send(c, side):
        to = (up, down)[side]
        return copy_to(
            pbuf[c].at[quarter(to)], rnear[c].at[side], s2.at[c, side], r2.at[c, side], dp=to
        )

    def out_at(c, where):
        return out_ref.at[where, columns[c]]

    def out_send(c, side, incoming=False):
        at = out_at(c, quarter((down, up)[side] if incoming else y))
        return copy_to(
            at if incoming else qbuf[c], at, s3.at[c, side], r3.at[c, side],
            dp=(up, down)[side],
        )

    def out_forward(c, side, incoming=False):
        at = out_at(c, quarter(far if incoming else (down, up)[side], side))
        return copy_to(at, at, s4.at[c, side], r4.at[c, side], dp=(up, down)[side])

    def out_own(c):
        return pltpu.make_async_copy(qbuf[c], out_at(c, quarter(y)), osem.at[c])

    def product(c):
        depth = tokens // 3 if tokens % (3 * LANES) == 0 else LANES
        for k in range(tokens // depth):
            at = pl.ds(k * depth, depth)
            term = jnp.dot(st[:, at], gbuf[c][at], preferred_element_type=jnp.float32)
            pbuf[c][...] = term if k == 0 else pbuf[c][...] + term
        for side in range(2):
            far_send(c, side).start()

    def product_pair(c, i):
        pair = lax.rem(lax.rem(z + steps, nz) // 2 + i, steps)
        at = pl.ds(pl.multiple_of(pair * 2 * tz, LANES), 2 * tz)
        return jnp.dot(st[:, at], gbuf[c][at], preferred_element_type=jnp.float32)

    def product_most(c):
        pbuf[c][...] = product_pair(c, 1)

        def one(i, carry):
            pbuf[c][...] = pbuf[c][...] + product_pair(c, i)
            return carry

        lax.fori_loop(2, steps, one, 0)

    def product_rest(c):
        pbuf[c][...] = pbuf[c][...] + product_pair(c, 0)
        for side in range(2):
            far_send(c, side).start()

    def near(c):
        for side in range(2):
            far_send(c, side).wait_recv()
            where = quarter((up, down)[side], side)
            pbuf[c][where] = pbuf[c][where] + rfar[c][side]
            near_send(c, side).start()

    def finish(c):
        total = pbuf[c][quarter(y)]
        for side in range(2):
            near_send(c, side).wait_recv()
            total = total + rnear[c][side]
        qbuf[c][...] = total
        for side in range(2):
            out_send(c, side).start()
        out_own(c).start()

    def forward_out(c):
        for side in range(2):
            out_send(c, side, incoming=True).wait_recv()
            out_forward(c, side).start()

    def out_done(c):
        for side in range(2):
            out_forward(c, side, incoming=True).wait_recv()
            far_send(c, side).wait_send()
            near_send(c, side).wait_send()
            out_send(c, side).wait_send()
            out_forward(c, side).wait_send()
        out_own(c).wait()

    def prepare():
        own_ids.wait()
        idcol[0:TILE] = jnp.full((TILE, LANES), -1.0, jnp.float32)
        xbuf[0:TILE] = jnp.zeros((TILE, xbuf.shape[1]), xbuf.dtype)
        lane = lax.broadcasted_iota(jnp.int32, (8, LANES), 1)
        none = jnp.full((8, LANES), -1.0, jnp.float32)
        flat = []
        for b in range(blocks):
            row = ids_vmem[0:1, b * LANES : (b + 1) * LANES].astype(jnp.float32)
            flat.append(jnp.broadcast_to(row, (8, LANES)))
            idcol[TILE + b * LANES : TILE + (b + 1) * LANES] = jnp.broadcast_to(
                row, (LANES, LANES)
            ).T
        for b in range(blocks):
            before = flat[b - 1] if b > 0 else none
            after = flat[b + 1] if b < blocks - 1 else none
            rows[0, b] = flat[b]
            rows[1, b] = jnp.where(
                lane < TILE, after, jnp.where(lane >= LANES - TILE, before, none)
            )

    def grad_bands():
        before = pl.ds(pl.multiple_of(z_at(nz - 1) * tz + tz - TILE, 32), TILE)
        dims = (((1,), (1,)), ((), ()))
        band = jnp.zeros((tz, wide), jnp.float32)
        for c in range(chunks):
            own = gbuf[c][own_rows]
            pad = jnp.zeros((wide - tz - TILE, WIDTHS[c]), own.dtype)
            window = jnp.concatenate([gbuf[c][before], own, pad], 0)
            band = band + lax.dot_general(own, window, dims, preferred_element_type=jnp.float32)
        bands[...] = band
        for j in range(tiles):
            turned = bands[j * TILE : (j + 1) * TILE]
            if j > 0:
                turned = pltpu.roll(turned, wide - j * TILE, 1)
            bsend[j] = packed(turned[:, :LANES])
            @pl.when(w != j)
            def _():
                grad_send(j).start()

    def act_bands():
        x_came(0).wait_recv()
        for d in range(1, nx):
            x_forwarded(d).wait_recv()

        @pl.when(w < tiles)
        def _():
            def one(d, carry):
                first = pl.multiple_of(z_at(d) * tz + w * TILE, 32)
                window = xbuf[pl.ds(first, 2 * TILE)]
                window = jnp.concatenate([window, jnp.zeros_like(window)], 0)
                dims = (((1,), (1,)), ((), ()))
                asend[d] = packed(
                    lax.dot_general(
                        window[TILE : 2 * TILE], window, dims, preferred_element_type=jnp.float32
                    )
                )
                @pl.when(d > 0)
                def _():
                    act_send(d).start()
                return carry
            lax.fori_loop(0, nz, one, 0)

    def weights():
        @pl.when(w < tiles)
        def _():
            act = asend[0]
            for d in range(1, nz):
                act_send(d).wait_recv()
                act = act + abuf[d]
            bbuf[w] = bsend[w]
            for d in range(1, nw):
                grad_came(w_at(d)).wait_recv()
            grad = bbuf[0]
            for u in range(1, nw):
                grad = grad + bbuf[u]
            tile = z * tiles + w
            first = pl.multiple_of(tile * TILE, 32)
            ids = idcol[pl.ds(first, 2 * TILE)]
            lane = lax.broadcasted_iota(jnp.int32, (8, LANES), 1)
            row = lax.broadcasted_iota(jnp.int32, (8, LANES), 0)
            group, partner = lane // TILE, lax.rem(lane, TILE)
            token = row + 8 * group
            mine = ids[TILE : TILE + 8]
            for k in range(1, 4):
                mine = jnp.where(group == k, ids[TILE + 8 * k : TILE + 8 * k + 8], mine)
            wide_lane = lax.broadcasted_iota(jnp.int32, (TILE, LANES), 1)
            wide_row = lax.broadcasted_iota(jnp.int32, (TILE, LANES), 0)
            pick = lax.rem(wide_lane, TILE) == wide_row
            before = jnp.sum(jnp.where(pick, ids[:TILE], 0.0), 0, keepdims=True)
            same = jnp.sum(jnp.where(pick, ids[TILE:], 0.0), 0, keepdims=True)
            theirs = jnp.where(partner <= token, same, before)
            factor = jnp.where(partner == token, 1.0, 2.0)
            factor = jnp.where(partner <= token, factor, jnp.where(tile > 0, 2.0, 0.0))
            term = jnp.where(mine == theirs, act * grad * factor, 0.0)
            at = lax.rem(tile, LANES // TILE) * TILE
            spread = jnp.zeros((8, LANES), jnp.float32)
            for k in range(4):
                one = jnp.sum(jnp.where(group == k, term, 0.0), 1, keepdims=True)
                spread = spread + jnp.where(lane == row + 8 * k + at, one, 0.0)
            wz[z] = jnp.sum(spread, 0, keepdims=True)
            for d in range(1, nz):
                weight_send(d).start()

    def slabs():
        @pl.when(w < tiles)
        def _():
            for d in range(1, nz):
                weight_came(d).wait_recv()
            wall[w] = wz[...]
            for d in range(1, nw):
                slab_send(d).start()

    def scales():
        for u in range(tiles):
            @pl.when(w != u)
            def _():
                slab_came(u).wait_recv()
        lane = lax.broadcasted_iota(jnp.int32, (8, LANES), 1)
        none = jnp.zeros((8, LANES), jnp.float32)
        flat = []
        for b in range(blocks):
            row = none
            for k in range(b * (LANES // TILE), (b + 1) * (LANES // TILE)):
                owner, j = divmod(k, tiles)
                row = row + jnp.broadcast_to(wall[j, owner], (8, LANES))
            flat.append(row)
        for b in range(blocks):
            before = flat[b - 1] if b > 0 else none
            after = flat[b + 1] if b < blocks - 1 else none
            rows[2, b] = flat[b]
            rows[3, b] = jnp.where(
                lane < TILE, after, jnp.where(lane >= LANES - TILE, before, none)
            )
        limit = clip_ref[0].astype(jnp.float32)

        def one(b, carry):
            at = pl.multiple_of(TILE + b * LANES, 32)
            ids = idcol[pl.ds(at, LANES)]
            found = jnp.where(ids == rows[0, b][0:1], rows[2, b][0:1], 0.0)
            found = found + jnp.where(ids == rows[1, b][0:1], rows[3, b][0:1], 0.0)
            squares = jnp.sum(found, 1, keepdims=True)
            factor = limit / jnp.maximum(jnp.sqrt(jnp.maximum(squares, 0.0)), limit)
            scaled = xbuf[pl.ds(at, LANES)].astype(jnp.float32) * factor
            st[:, pl.ds(pl.multiple_of(b * LANES, LANES), LANES)] = scaled.T.astype(st.dtype)
            return carry

        lax.fori_loop(0, blocks, one, 0)

    def forward_x():
        for d in range(1, nx):
            x_came(d).wait_recv()
            x_forward(d).start()

    first_slot = FIRST_SLOTS
    final_slot = first_slot[-1] + steps
    between = {0: (prepare,), 1: (grad_bands,), 2: (forward_x,), 3: (act_bands,), 4: (weights,),
               5: (slabs,), 6: (scales,)}

    def ring_sent(c):
        for s in range(steps):
            for way in range(2):
                ring(way, c, s).wait_send()

    def hop(t, c):
        s = t - first_slot[c]
        if 0 <= s < steps:
            for way in range(2):
                if s > 0:
                    ring(way, c, s - 1, incoming=True).wait_recv()
                ring(way, c, s).start()

    def first(c):
        for way in range(2):
            ring(way, c, steps - 1, incoming=True).wait_recv()
        if c == chunks - 1:
            product_rest(c)
        else:
            product(c)
        ring_sent(c)

    def stages(p):
        for c in range(chunks):
            stage, between_stages = divmod(p - 2 * (first_slot[c] + steps) - c % 2, 2)
            if 0 <= stage < 5 and between_stages == 0:
                (first, near, finish, forward_out, out_done)[stage](c)

    for t in range(final_slot):
        if t == 1:
            for c in range(chunks):
                halo_copy(c, incoming=True).wait_recv()
                own_g[c].wait()
        for c in range(0, chunks, 2):
            hop(t, c)
        if t == 0:
            for d in range(nx):
                x_first(d).start()
            for c in range(chunks):
                halo_copy(c).start()
            own_x.wait()
        for step in between.get(t, ()):
            step()
        stages(2 * t)
        for c in range(1, chunks, 2):
            hop(t, c)
        stages(2 * t + 1)
    product_most(chunks - 1)

    for c in range(chunks):
        halo_copy(c).wait_send()
    for d in range(nx):
        x_first(d).wait_send()
    for d in range(1, nx):
        x_forward(d).wait_send()
    for j in range(tiles):
        @pl.when(w != j)
        def _():
            grad_send(j).wait_send()

    @pl.when(w < tiles)
    def _():
        for d in range(1, nz):
            act_send(d).wait_send()
            weight_send(d).wait_send()
        for d in range(1, nw):
            slab_send(d).wait_send()

    for p in range(2 * final_slot, 2 * final_slot + 10):
        stages(p)


def body(sizes, activations, out_grads, query_ids, clip_bound):
    x_local = activations[0]
    g_local = out_grads[0]
    ny, nz, nw, tokens = sizes
    nx = nw // 2
    features, hidden = x_local.shape[1], g_local.shape[1]
    tz = g_local.shape[0]
    tiles = tz // TILE
    chunks = len(WIDTHS)
    assert sum(WIDTHS) == hidden
    steps = nz // 2
    part = features // ny
    dma = pltpu.SemaphoreType.DMA
    f32, bf16 = jnp.float32, jnp.bfloat16
    return pl.pallas_call(
        functools.partial(kernel, sizes),
        out_shape=jax.ShapeDtypeStruct((features, hidden), f32),
        in_specs=[
            pl.BlockSpec(memory_space=pltpu.HBM),
            pl.BlockSpec(memory_space=pltpu.HBM),
            pl.BlockSpec(memory_space=pltpu.HBM),
            pl.BlockSpec(memory_space=pltpu.SMEM),
        ],
        out_specs=pl.BlockSpec(memory_space=pl.ANY),
        scratch_shapes=[
            pltpu.VMEM((1, tokens), jnp.int32),
            pltpu.VMEM((tz, -(-(tz + TILE) // LANES) * LANES), f32),
            [pltpu.VMEM((tokens, n), bf16) for n in WIDTHS],
            pltpu.VMEM((TILE + tokens, features), bf16),
            pltpu.VMEM((features, tokens), bf16),
            pltpu.VMEM((TILE + tokens, LANES), f32),
            pltpu.VMEM((4, tokens // LANES, 8, LANES), f32),
            pltpu.VMEM((nz, 8, LANES), f32),
            pltpu.VMEM((nz, 8, LANES), f32),
            pltpu.VMEM((tiles, 8, LANES), f32),
            pltpu.VMEM((nw, 8, LANES), f32),
            pltpu.VMEM((nz, 1, LANES), f32),
            pltpu.VMEM((tiles, nz, 1, LANES), f32),
            [pltpu.VMEM((features, n), f32) for n in WIDTHS],
            [pltpu.VMEM((2, part // 2, n), f32) for n in WIDTHS],
            [pltpu.VMEM((2, part, n), f32) for n in WIDTHS],
            [pltpu.VMEM((part, n), f32) for n in WIDTHS],
            dma((chunks + 2,)), dma((chunks,)),
            dma((2 * nx,)), dma((2 * nx,)),
            dma((2, chunks)),
            dma((2, chunks, steps)), dma((2, chunks, steps)),
            dma((nz,)), dma((nz,)),
            dma((tiles,)), dma((nw,)),
            dma((nw,)), dma((tiles,)),
            dma((nz,)), dma((nz,)),
            *[dma((chunks, 2))] * 8,
        ],
        compiler_params=pltpu.CompilerParams(
            collective_id=0, has_side_effects=True, vmem_limit_bytes=50 * 1024 * 1024
        ),
        cost_estimate=pl.CostEstimate(
            flops=2 * tokens * features * hidden, bytes_accessed=1 << 23, transcendentals=0
        ),
    )(x_local, g_local, query_ids, clip_bound)


def solution(mesh):
    sizes = tuple(mesh.shape[a] for a in ("dp", "row", "col"))

    def run(activations, out_grads, query_ids, clip_bound):
        placed = (P("dp", "col", "row"), P("dp", "row", "col"), P("dp", None), P())
        return jax.shard_map(
            functools.partial(body, sizes + (query_ids.shape[1],)),
            mesh=mesh, in_specs=placed, out_specs=P("row", "col"), check_vma=False,
        )(activations, out_grads, query_ids, clip_bound)

    return run
```

```python
import functools

import jax
import jax.numpy as jnp
from jax import lax
from jax.experimental import pallas as pl
from jax.experimental.pallas import tpu as pltpu
from jax.sharding import PartitionSpec as P

TILE = 32
LANES = 128
WIDTHS = (256, 256, 256, 128, 256, 256, 256, 128)
FIRST_SLOTS = (0, 0, 0, 1, 4, 5, 7, 8)
STAGE_GAP = 3
MESH = pl.DeviceIdType.MESH


def packed(products):
    lane = lax.broadcasted_iota(jnp.int32, (TILE, LANES), 1)
    row = lax.broadcasted_iota(jnp.int32, (TILE, LANES), 0)
    near = jnp.where(lane <= row, pltpu.roll(products, LANES - TILE, 1), products)
    group = lax.broadcasted_iota(jnp.int32, (8, LANES), 1) // TILE
    out = near[:8]
    for k in range(1, 4):
        out = jnp.where(group == k, pltpu.roll(near[8 * k : 8 * k + 8], TILE * k, 1), out)
    return out


def kernel(
    sizes,
    x_ref, g_ref, ids_ref, clip_ref,
    out_ref,
    ids_vmem, bands, gbuf, xbuf, st, idcol, rows,
    asend, abuf, bsend, bbuf, wz, wall,
    pbuf, rfar, rnear, qbuf, rdir,
    lsem, osem, xs, xr, hs, rs, rr, asem, arec, bsem, brec, wsem, wrec, zsem, zrec,
    s1, r1, s2, r2, s3, r3, s4, r4, sd,
):
    ny, nz, nw, tokens = sizes
    nx = nw // 2
    tz = g_ref.shape[0]
    tc = x_ref.shape[0]
    tiles = tz // TILE
    chunks = len(WIDTHS)
    columns = [pl.ds(sum(WIDTHS[:c]), WIDTHS[c]) for c in range(chunks)]
    steps = nz // 2
    wide = bands.shape[1]
    blocks = tokens // LANES
    part = x_ref.shape[1] // ny

    y = lax.axis_index("dp")
    z = lax.axis_index("row")
    w = lax.axis_index("col")
    core = lax.rem(w, 2)
    chip = w // 2

    def z_at(d):
        return lax.rem(z + d, nz)

    def w_at(d):
        return lax.rem(w + d, nw)

    def y_at(d):
        return lax.rem(y + d, ny)

    def copy_to(src, dst, send, recv, **axis):
        return pltpu.make_async_remote_copy(
            src_ref=src, dst_ref=dst, send_sem=send, recv_sem=recv,
            device_id=axis, device_id_type=MESH,
        )

    own_rows = pl.ds(pl.multiple_of(z * tz, 32), tz)
    own_g = [
        pltpu.make_async_copy(
            g_ref.at[:, columns[c]], gbuf[c].at[own_rows], lsem.at[c]
        )
        for c in range(chunks)
    ]
    own_x = pltpu.make_async_copy(
        x_ref, xbuf.at[pl.ds(pl.multiple_of(TILE + w * tc, 32), tc)], lsem.at[chunks]
    )
    own_ids = pltpu.make_async_copy(ids_ref, ids_vmem, lsem.at[chunks + 1])
    for copy in own_g:
        copy.start()
    own_x.start()
    own_ids.start()

    barrier = pltpu.get_barrier_semaphore()
    for d in range(1, nz):
        pl.semaphore_signal(barrier, inc=1, device_id={"row": z_at(d)}, device_id_type=MESH)
    for d in range(1, nw):
        pl.semaphore_signal(barrier, inc=1, device_id={"col": w_at(d)}, device_id_type=MESH)
    for d in range(1, ny):
        pl.semaphore_signal(barrier, inc=1, device_id={"dp": y_at(d)}, device_id_type=MESH)
    pl.semaphore_wait(barrier, nz + nw + ny - 3)

    def x_rows(owner):
        return xbuf.at[pl.ds(pl.multiple_of(TILE + owner * tc, 32), tc)]

    sibling = chip * 2 + 1 - core

    def x_first(d):
        to = sibling if d == 0 else lax.rem(chip + d, nx) * 2 + core
        return copy_to(x_ref, x_rows(w), xs.at[d], xr.at[d], col=to)

    def x_came(d):
        owner = sibling if d == 0 else lax.rem(chip + nx - d, nx) * 2 + core
        return copy_to(x_rows(owner), x_rows(owner), xs.at[d], xr.at[d], col=sibling)

    def x_forward(d):
        owner = lax.rem(chip + nx - d, nx) * 2 + core
        return copy_to(
            x_rows(owner), x_rows(owner), xs.at[nx - 1 + d], xr.at[nx - 1 + d], col=sibling
        )

    def x_forwarded(d):
        owner = lax.rem(chip + nx - d, nx) * 2 + 1 - core
        return copy_to(
            x_rows(owner), x_rows(owner), xs.at[nx - 1 + d], xr.at[nx - 1 + d], col=sibling
        )

    def ring(way, c, s, incoming=False):
        hop = s + 1 if incoming else s
        owner = z_at(nz - hop) if way == 0 else z_at(hop)
        skip, count = 0, tz
        if s == steps - 1:
            skip, count = way * (tz // 2), tz // 2
        elif s == 0 and way == 0:
            count = tz - TILE
        block = gbuf[c].at[pl.ds(pl.multiple_of(owner * tz + skip, 32), count)]
        src = block
        if s == 0 and not incoming:
            src = g_ref.at[pl.ds(0, count), columns[c]]
        to = z_at(1) if way == 0 else z_at(nz - 1)
        return copy_to(src, block, rs.at[way, c, s], rr.at[way, c, s], row=to)

    def halo_copy(c, incoming=False):
        owner = z_at(nz - 1) if incoming else z
        there = gbuf[c].at[pl.ds(pl.multiple_of(owner * tz + tz - TILE, 32), TILE)]
        src = there if incoming else g_ref.at[pl.ds(tz - TILE, TILE), columns[c]]
        return copy_to(src, there, hs.at[0, c], hs.at[1, c], row=z_at(1))

    def act_send(d):
        return copy_to(asend.at[d], abuf.at[d], asem.at[d], arec.at[d], row=z_at(d))

    def grad_send(j):
        return copy_to(bsend.at[j], bbuf.at[w], bsem.at[j], brec.at[w], col=j)

    def grad_came(owner):
        return copy_to(bbuf.at[owner], bbuf.at[owner], bsem.at[0], brec.at[owner], col=w_at(1))

    def weight_send(d):
        return copy_to(wz.at[z], wz.at[z], zsem.at[d], zrec.at[d], row=z_at(d))

    def weight_came(d):
        owner = z_at(nz - d)
        return copy_to(wz.at[owner], wz.at[owner], zsem.at[d], zrec.at[d], row=z_at(1))

    def slab_send(d):
        return copy_to(wz, wall.at[w], wsem.at[d], wrec.at[w], col=w_at(d))

    def slab_came(owner):
        return copy_to(wall.at[owner], wall.at[owner], wsem.at[1], wrec.at[owner], col=w_at(1))

    up, far, down = y_at(1), y_at(2), y_at(3)
    half = part // 2

    def quarter(owner, side=None):
        if side is None:
            return pl.ds(pl.multiple_of(owner * part, part), part)
        return pl.ds(pl.multiple_of(owner * part + side * half, half), half)

    def far_send(c, side):
        return copy_to(
            pbuf[c].at[quarter(far, side)], rfar[c].at[side], s1.at[c, side], r1.at[c, side],
            dp=(up, down)[side],
        )

    def near_send(c, side):
        to = (up, down)[side]
        return copy_to(
            pbuf[c].at[quarter(to)], rnear[c].at[side], s2.at[c, side], r2.at[c, side], dp=to
        )

    def out_at(c, where):
        return out_ref.at[where, columns[c]]

    def out_send(c, side, incoming=False):
        at = out_at(c, quarter((down, up)[side] if incoming else y))
        return copy_to(
            at if incoming else qbuf[c], at, s3.at[c, side], r3.at[c, side],
            dp=(up, down)[side],
        )

    def out_forward(c, side, incoming=False):
        at = out_at(c, quarter(far if incoming else (down, up)[side], side))
        return copy_to(at, at, s4.at[c, side], r4.at[c, side], dp=(up, down)[side])

    def direct_send(c, d):
        to = y_at(d)
        return copy_to(
            pbuf[c].at[quarter(to)], rdir.at[d - 1], sd.at[0, d - 1], sd.at[1, d - 1], dp=to
        )

    def direct_out(c, d, incoming=False):
        at = out_at(c, quarter(y_at(ny - d) if incoming else y))
        return copy_to(
            at if incoming else qbuf[c], at, sd.at[2, d - 1], sd.at[3, d - 1], dp=y_at(d)
        )

    def out_own(c):
        return pltpu.make_async_copy(qbuf[c], out_at(c, quarter(y)), osem.at[c])

    def product(c):
        depth = tokens // 3 if tokens % (3 * LANES) == 0 else LANES
        for k in range(tokens // depth):
            at = pl.ds(k * depth, depth)
            term = jnp.dot(st[:, at], gbuf[c][at], preferred_element_type=jnp.float32)
            pbuf[c][...] = term if k == 0 else pbuf[c][...] + term
        for side in range(2):
            far_send(c, side).start()

    def product_pair(c, i):
        pair = lax.rem(lax.rem(z + steps, nz) // 2 + i, steps)
        at = pl.ds(pl.multiple_of(pair * 2 * tz, LANES), 2 * tz)
        return jnp.dot(st[:, at], gbuf[c][at], preferred_element_type=jnp.float32)

    def product_most(c):
        pbuf[c][...] = product_pair(c, 1)

        def one(i, carry):
            pbuf[c][...] = pbuf[c][...] + product_pair(c, i)
            return carry

        lax.fori_loop(2, steps, one, 0)

    def product_rest(c):
        pbuf[c][...] = pbuf[c][...] + product_pair(c, 0)
        for d in range(1, ny):
            direct_send(c, d).start()

    def direct_finish(c):
        total = pbuf[c][quarter(y)]
        for d in range(1, ny):
            direct_send(c, d).wait_recv()
            total = total + rdir[d - 1]
        qbuf[c][...] = total
        for d in range(1, ny):
            direct_out(c, d).start()
        out_own(c).start()

    def direct_done(c):
        for d in range(1, ny):
            direct_out(c, d, incoming=True).wait_recv()
            direct_send(c, d).wait_send()
            direct_out(c, d).wait_send()
        out_own(c).wait()

    def near(c):
        for side in range(2):
            far_send(c, side).wait_recv()
            where = quarter((up, down)[side], side)
            pbuf[c][where] = pbuf[c][where] + rfar[c][side]
            near_send(c, side).start()

    def finish(c):
        total = pbuf[c][quarter(y)]
        for side in range(2):
            near_send(c, side).wait_recv()
            total = total + rnear[c][side]
        qbuf[c][...] = total
        for side in range(2):
            out_send(c, side).start()
        out_own(c).start()

    def forward_out(c):
        for side in range(2):
            out_send(c, side, incoming=True).wait_recv()
            out_forward(c, side).start()

    def out_done(c):
        for side in range(2):
            out_forward(c, side, incoming=True).wait_recv()
            far_send(c, side).wait_send()
            near_send(c, side).wait_send()
            out_send(c, side).wait_send()
            out_forward(c, side).wait_send()
        out_own(c).wait()

    def prepare():
        own_ids.wait()
        idcol[0:TILE] = jnp.full((TILE, LANES), -1.0, jnp.float32)
        xbuf[0:TILE] = jnp.zeros((TILE, xbuf.shape[1]), xbuf.dtype)
        lane = lax.broadcasted_iota(jnp.int32, (8, LANES), 1)
        none = jnp.full((8, LANES), -1.0, jnp.float32)
        flat = []
        for b in range(blocks):
            row = ids_vmem[0:1, b * LANES : (b + 1) * LANES].astype(jnp.float32)
            flat.append(jnp.broadcast_to(row, (8, LANES)))
            idcol[TILE + b * LANES : TILE + (b + 1) * LANES] = jnp.broadcast_to(
                row, (LANES, LANES)
            ).T
        for b in range(blocks):
            before = flat[b - 1] if b > 0 else none
            after = flat[b + 1] if b < blocks - 1 else none
            rows[0, b] = flat[b]
            rows[1, b] = jnp.where(
                lane < TILE, after, jnp.where(lane >= LANES - TILE, before, none)
            )

    def grad_bands():
        before = pl.ds(pl.multiple_of(z_at(nz - 1) * tz + tz - TILE, 32), TILE)
        dims = (((1,), (1,)), ((), ()))
        band = jnp.zeros((tz, wide), jnp.float32)
        for c in range(chunks):
            own = gbuf[c][own_rows]
            pad = jnp.zeros((wide - tz - TILE, WIDTHS[c]), own.dtype)
            window = jnp.concatenate([gbuf[c][before], own, pad], 0)
            band = band + lax.dot_general(own, window, dims, preferred_element_type=jnp.float32)
        bands[...] = band
        for j in range(tiles):
            turned = bands[j * TILE : (j + 1) * TILE]
            if j > 0:
                turned = pltpu.roll(turned, wide - j * TILE, 1)
            bsend[j] = packed(turned[:, :LANES])
            @pl.when(w != j)
            def _():
                grad_send(j).start()

    def act_bands():
        x_came(0).wait_recv()
        for d in range(1, nx):
            x_forwarded(d).wait_recv()

        @pl.when(w < tiles)
        def _():
            def one(d, carry):
                first = pl.multiple_of(z_at(d) * tz + w * TILE, 32)
                window = xbuf[pl.ds(first, 2 * TILE)]
                window = jnp.concatenate([window, jnp.zeros_like(window)], 0)
                dims = (((1,), (1,)), ((), ()))
                asend[d] = packed(
                    lax.dot_general(
                        window[TILE : 2 * TILE], window, dims, preferred_element_type=jnp.float32
                    )
                )
                @pl.when(d > 0)
                def _():
                    act_send(d).start()
                return carry
            lax.fori_loop(0, nz, one, 0)

    def weights():
        @pl.when(w < tiles)
        def _():
            act = asend[0]
            for d in range(1, nz):
                act_send(d).wait_recv()
                act = act + abuf[d]
            bbuf[w] = bsend[w]
            for d in range(1, nw):
                grad_came(w_at(d)).wait_recv()
            grad = bbuf[0]
            for u in range(1, nw):
                grad = grad + bbuf[u]
            tile = z * tiles + w
            first = pl.multiple_of(tile * TILE, 32)
            ids = idcol[pl.ds(first, 2 * TILE)]
            lane = lax.broadcasted_iota(jnp.int32, (8, LANES), 1)
            row = lax.broadcasted_iota(jnp.int32, (8, LANES), 0)
            group, partner = lane // TILE, lax.rem(lane, TILE)
            token = row + 8 * group
            mine = ids[TILE : TILE + 8]
            for k in range(1, 4):
                mine = jnp.where(group == k, ids[TILE + 8 * k : TILE + 8 * k + 8], mine)
            wide_lane = lax.broadcasted_iota(jnp.int32, (TILE, LANES), 1)
            wide_row = lax.broadcasted_iota(jnp.int32, (TILE, LANES), 0)
            pick = lax.rem(wide_lane, TILE) == wide_row
            before = jnp.sum(jnp.where(pick, ids[:TILE], 0.0), 0, keepdims=True)
            same = jnp.sum(jnp.where(pick, ids[TILE:], 0.0), 0, keepdims=True)
            theirs = jnp.where(partner <= token, same, before)
            factor = jnp.where(partner == token, 1.0, 2.0)
            factor = jnp.where(partner <= token, factor, jnp.where(tile > 0, 2.0, 0.0))
            term = jnp.where(mine == theirs, act * grad * factor, 0.0)
            at = lax.rem(tile, LANES // TILE) * TILE
            spread = jnp.zeros((8, LANES), jnp.float32)
            for k in range(4):
                one = jnp.sum(jnp.where(group == k, term, 0.0), 1, keepdims=True)
                spread = spread + jnp.where(lane == row + 8 * k + at, one, 0.0)
            wz[z] = jnp.sum(spread, 0, keepdims=True)
            for d in range(1, nz):
                weight_send(d).start()

    def slabs():
        @pl.when(w < tiles)
        def _():
            for d in range(1, nz):
                weight_came(d).wait_recv()
            wall[w] = wz[...]
            for d in range(1, nw):
                slab_send(d).start()

    def scales():
        for u in range(tiles):
            @pl.when(w != u)
            def _():
                slab_came(u).wait_recv()
        lane = lax.broadcasted_iota(jnp.int32, (8, LANES), 1)
        none = jnp.zeros((8, LANES), jnp.float32)
        flat = []
        for b in range(blocks):
            row = none
            for k in range(b * (LANES // TILE), (b + 1) * (LANES // TILE)):
                owner, j = divmod(k, tiles)
                row = row + jnp.broadcast_to(wall[j, owner], (8, LANES))
            flat.append(row)
        for b in range(blocks):
            before = flat[b - 1] if b > 0 else none
            after = flat[b + 1] if b < blocks - 1 else none
            rows[2, b] = flat[b]
            rows[3, b] = jnp.where(
                lane < TILE, after, jnp.where(lane >= LANES - TILE, before, none)
            )
        limit = clip_ref[0].astype(jnp.float32)

        def one(b, carry):
            at = pl.multiple_of(TILE + b * LANES, 32)
            ids = idcol[pl.ds(at, LANES)]
            found = jnp.where(ids == rows[0, b][0:1], rows[2, b][0:1], 0.0)
            found = found + jnp.where(ids == rows[1, b][0:1], rows[3, b][0:1], 0.0)
            squares = jnp.sum(found, 1, keepdims=True)
            factor = limit / jnp.maximum(jnp.sqrt(jnp.maximum(squares, 0.0)), limit)
            scaled = xbuf[pl.ds(at, LANES)].astype(jnp.float32) * factor
            st[:, pl.ds(pl.multiple_of(b * LANES, LANES), LANES)] = scaled.T.astype(st.dtype)
            return carry

        lax.fori_loop(0, blocks, one, 0)

    def forward_x():
        for d in range(1, nx):
            x_came(d).wait_recv()
            x_forward(d).start()

    first_slot = FIRST_SLOTS
    final_slot = first_slot[-1] + steps
    between = {0: (prepare,), 1: (grad_bands,), 2: (forward_x,), 3: (act_bands,), 4: (weights,),
               5: (slabs,), 6: (scales,)}

    def ring_sent(c):
        for s in range(steps):
            for way in range(2):
                ring(way, c, s).wait_send()

    def hop(t, c):
        s = t - first_slot[c]
        if 0 <= s < steps:
            for way in range(2):
                if s > 0:
                    ring(way, c, s - 1, incoming=True).wait_recv()
                ring(way, c, s).start()

    def first(c):
        for way in range(2):
            ring(way, c, steps - 1, incoming=True).wait_recv()
        if c == chunks - 1:
            product_rest(c)
        else:
            product(c)
        ring_sent(c)

    def stages(p):
        for c in range(chunks):
            calls = (first, near, finish, forward_out, out_done)
            if c == chunks - 1:
                calls = (first, direct_finish, direct_done)
            stage, rest = divmod(p - 2 * (first_slot[c] + steps) - c % 2, STAGE_GAP)
            if 0 <= stage < len(calls) and rest == 0:
                calls[stage](c)

    for t in range(final_slot):
        if t == 1:
            for c in range(chunks):
                halo_copy(c, incoming=True).wait_recv()
                own_g[c].wait()
        for c in range(0, chunks, 2):
            hop(t, c)
        if t == 0:
            for d in range(nx):
                x_first(d).start()
            for c in range(chunks):
                halo_copy(c).start()
            own_x.wait()
        for step in between.get(t, ()):
            step()
        stages(2 * t)
        for c in range(1, chunks, 2):
            hop(t, c)
        stages(2 * t + 1)
    product_most(chunks - 1)

    for c in range(chunks):
        halo_copy(c).wait_send()
    for d in range(nx):
        x_first(d).wait_send()
    for d in range(1, nx):
        x_forward(d).wait_send()
    for j in range(tiles):
        @pl.when(w != j)
        def _():
            grad_send(j).wait_send()

    @pl.when(w < tiles)
    def _():
        for d in range(1, nz):
            act_send(d).wait_send()
            weight_send(d).wait_send()
        for d in range(1, nw):
            slab_send(d).wait_send()

    for p in range(2 * final_slot, 2 * final_slot + 5 * STAGE_GAP):
        stages(p)


def body(sizes, activations, out_grads, query_ids, clip_bound):
    x_local = activations[0]
    g_local = out_grads[0]
    ny, nz, nw, tokens = sizes
    nx = nw // 2
    features, hidden = x_local.shape[1], g_local.shape[1]
    tz = g_local.shape[0]
    tiles = tz // TILE
    chunks = len(WIDTHS)
    assert sum(WIDTHS) == hidden
    steps = nz // 2
    part = features // ny
    dma = pltpu.SemaphoreType.DMA
    f32, bf16 = jnp.float32, jnp.bfloat16
    return pl.pallas_call(
        functools.partial(kernel, sizes),
        out_shape=jax.ShapeDtypeStruct((features, hidden), f32),
        in_specs=[
            pl.BlockSpec(memory_space=pltpu.HBM),
            pl.BlockSpec(memory_space=pltpu.HBM),
            pl.BlockSpec(memory_space=pltpu.HBM),
            pl.BlockSpec(memory_space=pltpu.SMEM),
        ],
        out_specs=pl.BlockSpec(memory_space=pl.ANY),
        scratch_shapes=[
            pltpu.VMEM((1, tokens), jnp.int32),
            pltpu.VMEM((tz, -(-(tz + TILE) // LANES) * LANES), f32),
            [pltpu.VMEM((tokens, n), bf16) for n in WIDTHS],
            pltpu.VMEM((TILE + tokens, features), bf16),
            pltpu.VMEM((features, tokens), bf16),
            pltpu.VMEM((TILE + tokens, LANES), f32),
            pltpu.VMEM((4, tokens // LANES, 8, LANES), f32),
            pltpu.VMEM((nz, 8, LANES), f32),
            pltpu.VMEM((nz, 8, LANES), f32),
            pltpu.VMEM((tiles, 8, LANES), f32),
            pltpu.VMEM((nw, 8, LANES), f32),
            pltpu.VMEM((nz, 1, LANES), f32),
            pltpu.VMEM((tiles, nz, 1, LANES), f32),
            [pltpu.VMEM((features, n), f32) for n in WIDTHS],
            [pltpu.VMEM((2, part // 2, n), f32) for n in WIDTHS],
            [pltpu.VMEM((2, part, n), f32) for n in WIDTHS],
            [pltpu.VMEM((part, n), f32) for n in WIDTHS],
            pltpu.VMEM((ny - 1, part, WIDTHS[-1]), f32),
            dma((chunks + 2,)), dma((chunks,)),
            dma((2 * nx,)), dma((2 * nx,)),
            dma((2, chunks)),
            dma((2, chunks, steps)), dma((2, chunks, steps)),
            dma((nz,)), dma((nz,)),
            dma((tiles,)), dma((nw,)),
            dma((nw,)), dma((tiles,)),
            dma((nz,)), dma((nz,)),
            *[dma((chunks, 2))] * 8,
            dma((4, ny - 1)),
        ],
        compiler_params=pltpu.CompilerParams(
            collective_id=0, has_side_effects=True, vmem_limit_bytes=50 * 1024 * 1024
        ),
        cost_estimate=pl.CostEstimate(
            flops=2 * tokens * features * hidden, bytes_accessed=1 << 23, transcendentals=0
        ),
    )(x_local, g_local, query_ids, clip_bound)


def solution(mesh):
    sizes = tuple(mesh.shape[a] for a in ("dp", "row", "col"))

    def run(activations, out_grads, query_ids, clip_bound):
        placed = (P("dp", "col", "row"), P("dp", "row", "col"), P("dp", None), P())
        return jax.shard_map(
            functools.partial(body, sizes + (query_ids.shape[1],)),
            mesh=mesh, in_specs=placed, out_specs=P("row", "col"), check_vma=False,
        )(activations, out_grads, query_ids, clip_bound)

    return run
```

```python
import functools

import jax
import jax.numpy as jnp
from jax import lax
from jax.experimental import pallas as pl
from jax.experimental.pallas import tpu as pltpu
from jax.sharding import PartitionSpec as P

TILE = 32
LANES = 128
WIDTHS = (256, 256, 256, 128, 256, 256, 256, 128)
FIRST_SLOTS = (0, 0, 0, 1, 4, 5, 7, 8)
STAGE_GAP = 3
MESH = pl.DeviceIdType.MESH


def packed(products):
    lane = lax.broadcasted_iota(jnp.int32, (TILE, LANES), 1)
    row = lax.broadcasted_iota(jnp.int32, (TILE, LANES), 0)
    near = jnp.where(lane <= row, pltpu.roll(products, LANES - TILE, 1), products)
    group = lax.broadcasted_iota(jnp.int32, (8, LANES), 1) // TILE
    out = near[:8]
    for k in range(1, 4):
        out = jnp.where(group == k, pltpu.roll(near[8 * k : 8 * k + 8], TILE * k, 1), out)
    return out


def kernel(
    sizes,
    x_ref, g_ref, ids_ref, clip_ref,
    out_ref,
    ids_vmem, bands, gbuf, xbuf, st, idcol, rows,
    asend, abuf, bsend, bbuf, wz, wall,
    pbuf, rfar, rnear, qbuf, rdir,
    lsem, osem, xs, xr, hs, rs, rr, asem, arec, bsem, brec, wsem, wrec, zsem, zrec,
    s1, r1, s2, r2, s3, r3, s4, r4, sd,
):
    ny, nz, nw, tokens = sizes
    nx = nw // 2
    tz = g_ref.shape[0]
    tc = x_ref.shape[0]
    tiles = tz // TILE
    chunks = len(WIDTHS)
    columns = [pl.ds(sum(WIDTHS[:c]), WIDTHS[c]) for c in range(chunks)]
    steps = nz // 2
    wide = bands.shape[1]
    blocks = tokens // LANES
    part = x_ref.shape[1] // ny

    y = lax.axis_index("dp")
    z = lax.axis_index("row")
    w = lax.axis_index("col")
    core = lax.rem(w, 2)
    chip = w // 2

    def z_at(d):
        return lax.rem(z + d, nz)

    def w_at(d):
        return lax.rem(w + d, nw)

    def y_at(d):
        return lax.rem(y + d, ny)

    def copy_to(src, dst, send, recv, **axis):
        return pltpu.make_async_remote_copy(
            src_ref=src, dst_ref=dst, send_sem=send, recv_sem=recv,
            device_id=axis, device_id_type=MESH,
        )

    own_rows = pl.ds(pl.multiple_of(z * tz, 32), tz)
    own_g = [
        pltpu.make_async_copy(
            g_ref.at[:, columns[c]], gbuf[c].at[own_rows], lsem.at[c]
        )
        for c in range(chunks)
    ]
    own_x = pltpu.make_async_copy(
        x_ref, xbuf.at[pl.ds(pl.multiple_of(TILE + w * tc, 32), tc)], lsem.at[chunks]
    )
    own_ids = pltpu.make_async_copy(ids_ref, ids_vmem, lsem.at[chunks + 1])
    for copy in own_g:
        copy.start()
    own_x.start()
    own_ids.start()

    barrier = pltpu.get_barrier_semaphore()
    for d in range(1, nz):
        pl.semaphore_signal(barrier, inc=1, device_id={"row": z_at(d)}, device_id_type=MESH)
    for d in range(1, nw):
        pl.semaphore_signal(barrier, inc=1, device_id={"col": w_at(d)}, device_id_type=MESH)
    for d in range(1, ny):
        pl.semaphore_signal(barrier, inc=1, device_id={"dp": y_at(d)}, device_id_type=MESH)
    pl.semaphore_wait(barrier, nz + nw + ny - 3)

    def x_rows(owner):
        return xbuf.at[pl.ds(pl.multiple_of(TILE + owner * tc, 32), tc)]

    sibling = chip * 2 + 1 - core

    def x_first(d):
        to = sibling if d == 0 else lax.rem(chip + d, nx) * 2 + core
        return copy_to(x_ref, x_rows(w), xs.at[d], xr.at[d], col=to)

    def x_came(d):
        owner = sibling if d == 0 else lax.rem(chip + nx - d, nx) * 2 + core
        return copy_to(x_rows(owner), x_rows(owner), xs.at[d], xr.at[d], col=sibling)

    def x_forward(d):
        owner = lax.rem(chip + nx - d, nx) * 2 + core
        return copy_to(
            x_rows(owner), x_rows(owner), xs.at[nx - 1 + d], xr.at[nx - 1 + d], col=sibling
        )

    def x_forwarded(d):
        owner = lax.rem(chip + nx - d, nx) * 2 + 1 - core
        return copy_to(
            x_rows(owner), x_rows(owner), xs.at[nx - 1 + d], xr.at[nx - 1 + d], col=sibling
        )

    def ring(way, c, s, incoming=False):
        hop = s + 1 if incoming else s
        owner = z_at(nz - hop) if way == 0 else z_at(hop)
        skip, count = 0, tz
        if s == steps - 1:
            skip, count = way * (tz // 2), tz // 2
        elif s == 0 and way == 0:
            count = tz - TILE
        block = gbuf[c].at[pl.ds(pl.multiple_of(owner * tz + skip, 32), count)]
        src = block
        if s == 0 and not incoming:
            src = g_ref.at[pl.ds(0, count), columns[c]]
        to = z_at(1) if way == 0 else z_at(nz - 1)
        return copy_to(src, block, rs.at[way, c, s], rr.at[way, c, s], row=to)

    def halo_copy(c, incoming=False):
        owner = z_at(nz - 1) if incoming else z
        there = gbuf[c].at[pl.ds(pl.multiple_of(owner * tz + tz - TILE, 32), TILE)]
        src = there if incoming else g_ref.at[pl.ds(tz - TILE, TILE), columns[c]]
        return copy_to(src, there, hs.at[0, c], hs.at[1, c], row=z_at(1))

    def act_send(d):
        return copy_to(asend.at[d], abuf.at[d], asem.at[d], arec.at[d], row=z_at(d))

    def grad_send(j):
        return copy_to(bsend.at[j], bbuf.at[w], bsem.at[j], brec.at[w], col=j)

    def grad_came(owner):
        return copy_to(bbuf.at[owner], bbuf.at[owner], bsem.at[0], brec.at[owner], col=w_at(1))

    def weight_send(d):
        return copy_to(wz.at[z], wz.at[z], zsem.at[d], zrec.at[d], row=z_at(d))

    def weight_came(d):
        owner = z_at(nz - d)
        return copy_to(wz.at[owner], wz.at[owner], zsem.at[d], zrec.at[d], row=z_at(1))

    def slab_send(d):
        return copy_to(wz, wall.at[w], wsem.at[d], wrec.at[w], col=w_at(d))

    def slab_came(owner):
        return copy_to(wall.at[owner], wall.at[owner], wsem.at[1], wrec.at[owner], col=w_at(1))

    up, far, down = y_at(1), y_at(2), y_at(3)
    half = part // 2

    def quarter(owner, side=None):
        if side is None:
            return pl.ds(pl.multiple_of(owner * part, part), part)
        return pl.ds(pl.multiple_of(owner * part + side * half, half), half)

    def far_send(c, side):
        return copy_to(
            pbuf[c].at[quarter(far, side)], rfar[c].at[side], s1.at[c, side], r1.at[c, side],
            dp=(up, down)[side],
        )

    def near_send(c, side):
        to = (up, down)[side]
        return copy_to(
            pbuf[c].at[quarter(to)], rnear[c].at[side], s2.at[c, side], r2.at[c, side], dp=to
        )

    def out_at(c, where):
        return out_ref.at[where, columns[c]]

    def out_send(c, side, incoming=False):
        at = out_at(c, quarter((down, up)[side] if incoming else y))
        return copy_to(
            at if incoming else qbuf[c], at, s3.at[c, side], r3.at[c, side],
            dp=(up, down)[side],
        )

    def out_forward(c, side, incoming=False):
        at = out_at(c, quarter(far if incoming else (down, up)[side], side))
        return copy_to(at, at, s4.at[c, side], r4.at[c, side], dp=(up, down)[side])

    def direct_send(c, d):
        to = y_at(d)
        return copy_to(
            pbuf[c].at[quarter(to)], rdir.at[d - 1], sd.at[0, d - 1], sd.at[1, d - 1], dp=to
        )

    def direct_out(c, d, incoming=False):
        at = out_at(c, quarter(y_at(ny - d) if incoming else y))
        return copy_to(
            at if incoming else qbuf[c], at, sd.at[2, d - 1], sd.at[3, d - 1], dp=y_at(d)
        )

    def out_own(c):
        return pltpu.make_async_copy(qbuf[c], out_at(c, quarter(y)), osem.at[c])

    def product(c):
        depth = tokens // 3 if tokens % (3 * LANES) == 0 else LANES
        for k in range(tokens // depth):
            at = pl.ds(k * depth, depth)
            term = jnp.dot(st[:, at], gbuf[c][at], preferred_element_type=jnp.float32)
            pbuf[c][...] = term if k == 0 else pbuf[c][...] + term
        for side in range(2):
            far_send(c, side).start()

    def product_pair(c, i):
        pair = lax.rem(lax.rem(z + steps, nz) // 2 + i, steps)
        at = pl.ds(pl.multiple_of(pair * 2 * tz, LANES), 2 * tz)
        return jnp.dot(st[:, at], gbuf[c][at], preferred_element_type=jnp.float32)

    def product_most(c):
        pbuf[c][...] = product_pair(c, 1)

        def one(i, carry):
            pbuf[c][...] = pbuf[c][...] + product_pair(c, i)
            return carry

        lax.fori_loop(2, steps, one, 0)

    def product_rest(c):
        pbuf[c][...] = pbuf[c][...] + product_pair(c, 0)
        for d in range(1, ny):
            direct_send(c, d).start()

    def direct_finish(c):
        total = pbuf[c][quarter(y)]
        for d in range(1, ny):
            direct_send(c, d).wait_recv()
            total = total + rdir[d - 1]
        qbuf[c][...] = total
        for d in range(1, ny):
            direct_out(c, d).start()
        out_own(c).start()

    def direct_done(c):
        for d in range(1, ny):
            direct_out(c, d, incoming=True).wait_recv()
            direct_send(c, d).wait_send()
            direct_out(c, d).wait_send()
        out_own(c).wait()

    def near(c):
        for side in range(2):
            far_send(c, side).wait_recv()
            where = quarter((up, down)[side], side)
            pbuf[c][where] = pbuf[c][where] + rfar[c][side]
            near_send(c, side).start()

    def finish(c):
        total = pbuf[c][quarter(y)]
        for side in range(2):
            near_send(c, side).wait_recv()
            total = total + rnear[c][side]
        qbuf[c][...] = total
        for side in range(2):
            out_send(c, side).start()
        out_own(c).start()

    def forward_out(c):
        for side in range(2):
            out_send(c, side, incoming=True).wait_recv()
            out_forward(c, side).start()

    def out_done(c):
        for side in range(2):
            out_forward(c, side, incoming=True).wait_recv()
            far_send(c, side).wait_send()
            near_send(c, side).wait_send()
            out_send(c, side).wait_send()
            out_forward(c, side).wait_send()
        out_own(c).wait()

    def prepare():
        own_ids.wait()
        idcol[0:TILE] = jnp.full((TILE, LANES), -1.0, jnp.float32)
        xbuf[0:TILE] = jnp.zeros((TILE, xbuf.shape[1]), xbuf.dtype)
        lane = lax.broadcasted_iota(jnp.int32, (8, LANES), 1)
        none = jnp.full((8, LANES), -1.0, jnp.float32)
        flat = []
        for b in range(blocks):
            row = ids_vmem[0:1, b * LANES : (b + 1) * LANES].astype(jnp.float32)
            flat.append(jnp.broadcast_to(row, (8, LANES)))
            idcol[TILE + b * LANES : TILE + (b + 1) * LANES] = jnp.broadcast_to(
                row, (LANES, LANES)
            ).T
        for b in range(blocks):
            before = flat[b - 1] if b > 0 else none
            after = flat[b + 1] if b < blocks - 1 else none
            rows[0, b] = flat[b]
            rows[1, b] = jnp.where(
                lane < TILE, after, jnp.where(lane >= LANES - TILE, before, none)
            )

    def grad_bands():
        before = pl.ds(pl.multiple_of(z_at(nz - 1) * tz + tz - TILE, 32), TILE)
        dims = (((1,), (1,)), ((), ()))
        band = jnp.zeros((tz, wide), jnp.float32)
        for c in range(chunks):
            own = gbuf[c][own_rows]
            pad = jnp.zeros((wide - tz - TILE, WIDTHS[c]), own.dtype)
            window = jnp.concatenate([gbuf[c][before], own, pad], 0)
            band = band + lax.dot_general(own, window, dims, preferred_element_type=jnp.float32)
        bands[...] = band
        for j in range(tiles):
            turned = bands[j * TILE : (j + 1) * TILE]
            if j > 0:
                turned = pltpu.roll(turned, wide - j * TILE, 1)
            bsend[j] = packed(turned[:, :LANES])
            @pl.when(w != j)
            def _():
                grad_send(j).start()

    def act_bands():
        x_came(0).wait_recv()
        for d in range(1, nx):
            x_forwarded(d).wait_recv()

        @pl.when(w < tiles)
        def _():
            def one(d, carry):
                first = pl.multiple_of(z_at(d) * tz + w * TILE, 32)
                window = xbuf[pl.ds(first, 2 * TILE)]
                window = jnp.concatenate([window, jnp.zeros_like(window)], 0)
                dims = (((1,), (1,)), ((), ()))
                asend[d] = packed(
                    lax.dot_general(
                        window[TILE : 2 * TILE], window, dims, preferred_element_type=jnp.float32
                    )
                )
                @pl.when(d > 0)
                def _():
                    act_send(d).start()
                return carry
            lax.fori_loop(0, nz, one, 0)

    def weights():
        @pl.when(w < tiles)
        def _():
            act = asend[0]
            for d in range(1, nz):
                act_send(d).wait_recv()
                act = act + abuf[d]
            bbuf[w] = bsend[w]
            for d in range(1, nw):
                grad_came(w_at(d)).wait_recv()
            grad = bbuf[0]
            for u in range(1, nw):
                grad = grad + bbuf[u]
            tile = z * tiles + w
            first = pl.multiple_of(tile * TILE, 32)
            ids = idcol[pl.ds(first, 2 * TILE)]
            lane = lax.broadcasted_iota(jnp.int32, (8, LANES), 1)
            row = lax.broadcasted_iota(jnp.int32, (8, LANES), 0)
            group, partner = lane // TILE, lax.rem(lane, TILE)
            token = row + 8 * group
            mine = ids[TILE : TILE + 8]
            for k in range(1, 4):
                mine = jnp.where(group == k, ids[TILE + 8 * k : TILE + 8 * k + 8], mine)
            wide_lane = lax.broadcasted_iota(jnp.int32, (TILE, LANES), 1)
            wide_row = lax.broadcasted_iota(jnp.int32, (TILE, LANES), 0)
            pick = lax.rem(wide_lane, TILE) == wide_row
            before = jnp.sum(jnp.where(pick, ids[:TILE], 0.0), 0, keepdims=True)
            same = jnp.sum(jnp.where(pick, ids[TILE:], 0.0), 0, keepdims=True)
            theirs = jnp.where(partner <= token, same, before)
            factor = jnp.where(partner == token, 1.0, 2.0)
            factor = jnp.where(partner <= token, factor, jnp.where(tile > 0, 2.0, 0.0))
            term = jnp.where(mine == theirs, act * grad * factor, 0.0)
            at = lax.rem(tile, LANES // TILE) * TILE
            spread = jnp.zeros((8, LANES), jnp.float32)
            for k in range(4):
                one = jnp.sum(jnp.where(group == k, term, 0.0), 1, keepdims=True)
                spread = spread + jnp.where(lane == row + 8 * k + at, one, 0.0)
            wz[z] = jnp.sum(spread, 0, keepdims=True)
            for d in range(1, nz):
                weight_send(d).start()

    def slabs():
        @pl.when(w < tiles)
        def _():
            for d in range(1, nz):
                weight_came(d).wait_recv()
            wall[w] = wz[...]
            for d in range(1, nw):
                slab_send(d).start()

    def scales():
        for u in range(tiles):
            @pl.when(w != u)
            def _():
                slab_came(u).wait_recv()
        lane = lax.broadcasted_iota(jnp.int32, (8, LANES), 1)
        none = jnp.zeros((8, LANES), jnp.float32)
        flat = []
        for b in range(blocks):
            row = none
            for k in range(b * (LANES // TILE), (b + 1) * (LANES // TILE)):
                owner, j = divmod(k, tiles)
                row = row + jnp.broadcast_to(wall[j, owner], (8, LANES))
            flat.append(row)
        for b in range(blocks):
            before = flat[b - 1] if b > 0 else none
            after = flat[b + 1] if b < blocks - 1 else none
            rows[2, b] = flat[b]
            rows[3, b] = jnp.where(
                lane < TILE, after, jnp.where(lane >= LANES - TILE, before, none)
            )
        limit = clip_ref[0].astype(jnp.float32)

        def one(b, carry):
            at = pl.multiple_of(TILE + b * LANES, 32)
            ids = idcol[pl.ds(at, LANES)]
            found = jnp.where(ids == rows[0, b][0:1], rows[2, b][0:1], 0.0)
            found = found + jnp.where(ids == rows[1, b][0:1], rows[3, b][0:1], 0.0)
            squares = jnp.sum(found, 1, keepdims=True)
            factor = limit / jnp.maximum(jnp.sqrt(jnp.maximum(squares, 0.0)), limit)
            scaled = xbuf[pl.ds(at, LANES)].astype(jnp.float32) * factor
            st[:, pl.ds(pl.multiple_of(b * LANES, LANES), LANES)] = scaled.T.astype(st.dtype)
            return carry

        lax.fori_loop(0, blocks, one, 0)

    def forward_x():
        for d in range(1, nx):
            x_came(d).wait_recv()
            x_forward(d).start()

    first_slot = FIRST_SLOTS
    final_slot = first_slot[-1] + steps
    between = {0: (prepare,), 1: (grad_bands,), 2: (forward_x,), 3: (act_bands,), 5: (weights,),
               6: (slabs,), 7: (scales,)}

    def ring_sent(c):
        for s in range(steps):
            for way in range(2):
                ring(way, c, s).wait_send()

    def hop(t, c):
        s = t - first_slot[c]
        if 0 <= s < steps:
            for way in range(2):
                if s > 0:
                    ring(way, c, s - 1, incoming=True).wait_recv()
                ring(way, c, s).start()

    def first(c):
        for way in range(2):
            ring(way, c, steps - 1, incoming=True).wait_recv()
        if c == chunks - 1:
            product_rest(c)
        else:
            product(c)
        ring_sent(c)

    def stages(p):
        for c in range(chunks):
            calls = (first, near, finish, forward_out, out_done)
            if c == chunks - 1:
                calls = (first, direct_finish, direct_done)
            stage, rest = divmod(p - 2 * (first_slot[c] + steps) - c % 2, STAGE_GAP)
            if 0 <= stage < len(calls) and rest == 0:
                calls[stage](c)

    for t in range(final_slot):
        if t == 1:
            for c in range(chunks):
                halo_copy(c, incoming=True).wait_recv()
                own_g[c].wait()
        for c in range(0, chunks, 2):
            hop(t, c)
        if t == 0:
            for d in range(nx):
                x_first(d).start()
            for c in range(chunks):
                halo_copy(c).start()
            own_x.wait()
        for step in between.get(t, ()):
            step()
        stages(2 * t)
        for c in range(1, chunks, 2):
            hop(t, c)
        stages(2 * t + 1)
    product_most(chunks - 1)

    for c in range(chunks):
        halo_copy(c).wait_send()
    for d in range(nx):
        x_first(d).wait_send()
    for d in range(1, nx):
        x_forward(d).wait_send()
    for j in range(tiles):
        @pl.when(w != j)
        def _():
            grad_send(j).wait_send()

    @pl.when(w < tiles)
    def _():
        for d in range(1, nz):
            act_send(d).wait_send()
            weight_send(d).wait_send()
        for d in range(1, nw):
            slab_send(d).wait_send()

    for p in range(2 * final_slot, 2 * final_slot + 5 * STAGE_GAP):
        stages(p)


def body(sizes, activations, out_grads, query_ids, clip_bound):
    x_local = activations[0]
    g_local = out_grads[0]
    ny, nz, nw, tokens = sizes
    nx = nw // 2
    features, hidden = x_local.shape[1], g_local.shape[1]
    tz = g_local.shape[0]
    tiles = tz // TILE
    chunks = len(WIDTHS)
    assert sum(WIDTHS) == hidden
    steps = nz // 2
    part = features // ny
    dma = pltpu.SemaphoreType.DMA
    f32, bf16 = jnp.float32, jnp.bfloat16
    stay = [
        pltpu.with_memory_space_constraint(a, pltpu.HBM) for a in (x_local, g_local, query_ids)
    ]
    return pl.pallas_call(
        functools.partial(kernel, sizes),
        out_shape=jax.ShapeDtypeStruct((features, hidden), f32),
        in_specs=[
            pl.BlockSpec(memory_space=pltpu.HBM),
            pl.BlockSpec(memory_space=pltpu.HBM),
            pl.BlockSpec(memory_space=pltpu.HBM),
            pl.BlockSpec(memory_space=pltpu.SMEM),
        ],
        out_specs=pl.BlockSpec(memory_space=pl.ANY),
        scratch_shapes=[
            pltpu.VMEM((1, tokens), jnp.int32),
            pltpu.VMEM((tz, -(-(tz + TILE) // LANES) * LANES), f32),
            [pltpu.VMEM((tokens, n), bf16) for n in WIDTHS],
            pltpu.VMEM((TILE + tokens, features), bf16),
            pltpu.VMEM((features, tokens), bf16),
            pltpu.VMEM((TILE + tokens, LANES), f32),
            pltpu.VMEM((4, tokens // LANES, 8, LANES), f32),
            pltpu.VMEM((nz, 8, LANES), f32),
            pltpu.VMEM((nz, 8, LANES), f32),
            pltpu.VMEM((tiles, 8, LANES), f32),
            pltpu.VMEM((nw, 8, LANES), f32),
            pltpu.VMEM((nz, 1, LANES), f32),
            pltpu.VMEM((tiles, nz, 1, LANES), f32),
            [pltpu.VMEM((features, n), f32) for n in WIDTHS],
            [pltpu.VMEM((2, part // 2, n), f32) for n in WIDTHS],
            [pltpu.VMEM((2, part, n), f32) for n in WIDTHS],
            [pltpu.VMEM((part, n), f32) for n in WIDTHS],
            pltpu.VMEM((ny - 1, part, WIDTHS[-1]), f32),
            dma((chunks + 2,)), dma((chunks,)),
            dma((2 * nx,)), dma((2 * nx,)),
            dma((2, chunks)),
            dma((2, chunks, steps)), dma((2, chunks, steps)),
            dma((nz,)), dma((nz,)),
            dma((tiles,)), dma((nw,)),
            dma((nw,)), dma((tiles,)),
            dma((nz,)), dma((nz,)),
            *[dma((chunks, 2))] * 8,
            dma((4, ny - 1)),
        ],
        compiler_params=pltpu.CompilerParams(
            collective_id=0, has_side_effects=True, vmem_limit_bytes=50 * 1024 * 1024
        ),
        cost_estimate=pl.CostEstimate(
            flops=2 * tokens * features * hidden, bytes_accessed=1 << 23, transcendentals=0
        ),
    )(*stay, clip_bound)


def solution(mesh):
    sizes = tuple(mesh.shape[a] for a in ("dp", "row", "col"))

    def run(activations, out_grads, query_ids, clip_bound):
        placed = (P("dp", "col", "row"), P("dp", "row", "col"), P("dp", None), P())
        return jax.shard_map(
            functools.partial(body, sizes + (query_ids.shape[1],)),
            mesh=mesh, in_specs=placed, out_specs=P("row", "col"), check_vma=False,
        )(activations, out_grads, query_ids, clip_bound)

    return run
```

```python
import functools

import jax
import jax.numpy as jnp
from jax import lax
from jax.experimental import pallas as pl
from jax.experimental.pallas import tpu as pltpu
from jax.sharding import PartitionSpec as P

TILE = 32
LANES = 128
WIDTHS = (256, 256, 256, 256, 256, 256, 256)
FIRST_SLOTS = (0, 0, 0, 1, 3, 6, 7)
STAGE_GAP = 2
DIRECT = 2
MESH = pl.DeviceIdType.MESH


def packed(products):
    lane = lax.broadcasted_iota(jnp.int32, (TILE, LANES), 1)
    row = lax.broadcasted_iota(jnp.int32, (TILE, LANES), 0)
    near = jnp.where(lane <= row, pltpu.roll(products, LANES - TILE, 1), products)
    group = lax.broadcasted_iota(jnp.int32, (8, LANES), 1) // TILE
    out = near[:8]
    for k in range(1, 4):
        out = jnp.where(group == k, pltpu.roll(near[8 * k : 8 * k + 8], TILE * k, 1), out)
    return out


def kernel(
    sizes,
    x_ref, g_ref, ids_ref, clip_ref,
    out_ref,
    ids_vmem, bands, gbuf, xbuf, st, idcol, rows,
    asend, abuf, bsend, bbuf, wz, wall,
    pbuf, rfar, rnear, qbuf, rdir,
    lsem, osem, xs, xr, hs, rs, rr, asem, arec, bsem, brec, wsem, wrec, zsem, zrec,
    s1, r1, s2, r2, s3, r3, s4, r4, sd,
):
    ny, nz, nw, tokens = sizes
    nx = nw // 2
    tz = g_ref.shape[0]
    tc = x_ref.shape[0]
    tiles = tz // TILE
    chunks = len(WIDTHS)
    plain = chunks - DIRECT
    columns = [pl.ds(sum(WIDTHS[:c]), WIDTHS[c]) for c in range(chunks)]
    steps = nz // 2
    wide = bands.shape[1]
    blocks = tokens // LANES
    part = x_ref.shape[1] // ny

    y = lax.axis_index("dp")
    z = lax.axis_index("row")
    w = lax.axis_index("col")
    core = lax.rem(w, 2)
    chip = w // 2

    def z_at(d):
        return lax.rem(z + d, nz)

    def w_at(d):
        return lax.rem(w + d, nw)

    def y_at(d):
        return lax.rem(y + d, ny)

    def copy_to(src, dst, send, recv, **axis):
        return pltpu.make_async_remote_copy(
            src_ref=src, dst_ref=dst, send_sem=send, recv_sem=recv,
            device_id=axis, device_id_type=MESH,
        )

    own_rows = pl.ds(pl.multiple_of(z * tz, 32), tz)
    own_g = [
        pltpu.make_async_copy(
            g_ref.at[:, columns[c]], gbuf[c].at[own_rows], lsem.at[c]
        )
        for c in range(chunks)
    ]
    own_x = pltpu.make_async_copy(
        x_ref, xbuf.at[pl.ds(pl.multiple_of(TILE + w * tc, 32), tc)], lsem.at[chunks]
    )
    own_ids = pltpu.make_async_copy(ids_ref, ids_vmem, lsem.at[chunks + 1])
    for copy in own_g:
        copy.start()
    own_x.start()
    own_ids.start()

    barrier = pltpu.get_barrier_semaphore()
    for d in range(1, nz):
        pl.semaphore_signal(barrier, inc=1, device_id={"row": z_at(d)}, device_id_type=MESH)
    for d in range(1, nw):
        pl.semaphore_signal(barrier, inc=1, device_id={"col": w_at(d)}, device_id_type=MESH)
    for d in range(1, ny):
        pl.semaphore_signal(barrier, inc=1, device_id={"dp": y_at(d)}, device_id_type=MESH)
    pl.semaphore_wait(barrier, nz + nw + ny - 3)

    def x_rows(owner):
        return xbuf.at[pl.ds(pl.multiple_of(TILE + owner * tc, 32), tc)]

    sibling = chip * 2 + 1 - core

    def x_first(d):
        to = sibling if d == 0 else lax.rem(chip + d, nx) * 2 + core
        return copy_to(x_ref, x_rows(w), xs.at[d], xr.at[d], col=to)

    def x_came(d):
        owner = sibling if d == 0 else lax.rem(chip + nx - d, nx) * 2 + core
        return copy_to(x_rows(owner), x_rows(owner), xs.at[d], xr.at[d], col=sibling)

    def x_forward(d):
        owner = lax.rem(chip + nx - d, nx) * 2 + core
        return copy_to(
            x_rows(owner), x_rows(owner), xs.at[nx - 1 + d], xr.at[nx - 1 + d], col=sibling
        )

    def x_forwarded(d):
        owner = lax.rem(chip + nx - d, nx) * 2 + 1 - core
        return copy_to(
            x_rows(owner), x_rows(owner), xs.at[nx - 1 + d], xr.at[nx - 1 + d], col=sibling
        )

    def ring(way, c, s, incoming=False):
        hop = s + 1 if incoming else s
        owner = z_at(nz - hop) if way == 0 else z_at(hop)
        skip, count = 0, tz
        if s == steps - 1:
            skip, count = way * (tz // 2), tz // 2
        elif s == 0 and way == 0:
            count = tz - TILE
        block = gbuf[c].at[pl.ds(pl.multiple_of(owner * tz + skip, 32), count)]
        src = block
        if s == 0 and not incoming:
            src = g_ref.at[pl.ds(0, count), columns[c]]
        to = z_at(1) if way == 0 else z_at(nz - 1)
        return copy_to(src, block, rs.at[way, c, s], rr.at[way, c, s], row=to)

    def halo_copy(c, incoming=False):
        owner = z_at(nz - 1) if incoming else z
        there = gbuf[c].at[pl.ds(pl.multiple_of(owner * tz + tz - TILE, 32), TILE)]
        src = there if incoming else g_ref.at[pl.ds(tz - TILE, TILE), columns[c]]
        return copy_to(src, there, hs.at[0, c], hs.at[1, c], row=z_at(1))

    def act_send(d):
        return copy_to(asend.at[d], abuf.at[d], asem.at[d], arec.at[d], row=z_at(d))

    def grad_send(j):
        return copy_to(bsend.at[j], bbuf.at[w], bsem.at[j], brec.at[w], col=j)

    def grad_came(owner):
        return copy_to(bbuf.at[owner], bbuf.at[owner], bsem.at[0], brec.at[owner], col=w_at(1))

    def weight_send(d):
        return copy_to(wz.at[z], wz.at[z], zsem.at[d], zrec.at[d], row=z_at(d))

    def weight_came(d):
        owner = z_at(nz - d)
        return copy_to(wz.at[owner], wz.at[owner], zsem.at[d], zrec.at[d], row=z_at(1))

    def slab_send(d):
        return copy_to(wz, wall.at[w], wsem.at[d], wrec.at[w], col=w_at(d))

    def slab_came(owner):
        return copy_to(wall.at[owner], wall.at[owner], wsem.at[1], wrec.at[owner], col=w_at(1))

    up, far, down = y_at(1), y_at(2), y_at(3)
    half = part // 2

    def quarter(owner, side=None):
        if side is None:
            return pl.ds(pl.multiple_of(owner * part, part), part)
        return pl.ds(pl.multiple_of(owner * part + side * half, half), half)

    def far_send(c, side):
        return copy_to(
            pbuf[c].at[quarter(far, side)], rfar[c].at[side], s1.at[c, side], r1.at[c, side],
            dp=(up, down)[side],
        )

    def near_send(c, side):
        to = (up, down)[side]
        return copy_to(
            pbuf[c].at[quarter(to)], rnear[c].at[side], s2.at[c, side], r2.at[c, side], dp=to
        )

    def out_at(c, where):
        return out_ref.at[where, columns[c]]

    def out_send(c, side, incoming=False):
        at = out_at(c, quarter((down, up)[side] if incoming else y))
        return copy_to(
            at if incoming else qbuf[c], at, s3.at[c, side], r3.at[c, side],
            dp=(up, down)[side],
        )

    def out_forward(c, side, incoming=False):
        at = out_at(c, quarter(far if incoming else (down, up)[side], side))
        return copy_to(at, at, s4.at[c, side], r4.at[c, side], dp=(up, down)[side])

    def direct_send(c, d):
        to = y_at(d)
        return copy_to(
            pbuf[c].at[quarter(to)], rdir[c - plain].at[d - 1],
            sd.at[0, c - plain, d - 1], sd.at[1, c - plain, d - 1], dp=to,
        )

    def direct_out(c, d, incoming=False):
        at = out_at(c, quarter(y_at(ny - d) if incoming else y))
        return copy_to(
            at if incoming else qbuf[c], at,
            sd.at[2, c - plain, d - 1], sd.at[3, c - plain, d - 1], dp=y_at(d),
        )

    def out_own(c):
        return pltpu.make_async_copy(qbuf[c], out_at(c, quarter(y)), osem.at[c])

    def product(c):
        depth = tokens // 3 if tokens % (3 * LANES) == 0 else LANES
        for k in range(tokens // depth):
            at = pl.ds(k * depth, depth)
            term = jnp.dot(st[:, at], gbuf[c][at], preferred_element_type=jnp.float32)
            pbuf[c][...] = term if k == 0 else pbuf[c][...] + term
        for side in range(2):
            far_send(c, side).start()

    def product_pair(c, i):
        pair = lax.rem(lax.rem(z + steps, nz) // 2 + i, steps)
        at = pl.ds(pl.multiple_of(pair * 2 * tz, LANES), 2 * tz)
        return jnp.dot(st[:, at], gbuf[c][at], preferred_element_type=jnp.float32)

    def product_most(c):
        pbuf[c][...] = product_pair(c, 1)

        def one(i, carry):
            pbuf[c][...] = pbuf[c][...] + product_pair(c, i)
            return carry

        lax.fori_loop(2, steps, one, 0)

    def product_rest(c):
        pbuf[c][...] = pbuf[c][...] + product_pair(c, 0)
        for d in range(1, ny):
            direct_send(c, d).start()

    def direct_finish(c):
        total = pbuf[c][quarter(y)]
        for d in range(1, ny):
            direct_send(c, d).wait_recv()
            total = total + rdir[c - plain][d - 1]
        qbuf[c][...] = total
        for d in range(1, ny):
            direct_out(c, d).start()
        out_own(c).start()

    def direct_done(c):
        for d in range(1, ny):
            direct_out(c, d, incoming=True).wait_recv()
            direct_send(c, d).wait_send()
            direct_out(c, d).wait_send()
        out_own(c).wait()

    def near(c):
        for side in range(2):
            far_send(c, side).wait_recv()
            where = quarter((up, down)[side], side)
            pbuf[c][where] = pbuf[c][where] + rfar[c][side]
            near_send(c, side).start()

    def finish(c):
        total = pbuf[c][quarter(y)]
        for side in range(2):
            near_send(c, side).wait_recv()
            total = total + rnear[c][side]
        qbuf[c][...] = total
        for side in range(2):
            out_send(c, side).start()
        out_own(c).start()

    def forward_out(c):
        for side in range(2):
            out_send(c, side, incoming=True).wait_recv()
            out_forward(c, side).start()

    def out_done(c):
        for side in range(2):
            out_forward(c, side, incoming=True).wait_recv()
            far_send(c, side).wait_send()
            near_send(c, side).wait_send()
            out_send(c, side).wait_send()
            out_forward(c, side).wait_send()
        out_own(c).wait()

    def prepare():
        own_ids.wait()
        idcol[0:TILE] = jnp.full((TILE, LANES), -1.0, jnp.float32)
        xbuf[0:TILE] = jnp.zeros((TILE, xbuf.shape[1]), xbuf.dtype)
        lane = lax.broadcasted_iota(jnp.int32, (8, LANES), 1)
        none = jnp.full((8, LANES), -1.0, jnp.float32)
        flat = []
        for b in range(blocks):
            row = ids_vmem[0:1, b * LANES : (b + 1) * LANES].astype(jnp.float32)
            flat.append(jnp.broadcast_to(row, (8, LANES)))
            idcol[TILE + b * LANES : TILE + (b + 1) * LANES] = jnp.broadcast_to(
                row, (LANES, LANES)
            ).T
        for b in range(blocks):
            before = flat[b - 1] if b > 0 else none
            after = flat[b + 1] if b < blocks - 1 else none
            rows[0, b] = flat[b]
            rows[1, b] = jnp.where(
                lane < TILE, after, jnp.where(lane >= LANES - TILE, before, none)
            )

    def grad_bands():
        before = pl.ds(pl.multiple_of(z_at(nz - 1) * tz + tz - TILE, 32), TILE)
        dims = (((1,), (1,)), ((), ()))
        band = jnp.zeros((tz, wide), jnp.float32)
        for c in range(chunks):
            own = gbuf[c][own_rows]
            pad = jnp.zeros((wide - tz - TILE, WIDTHS[c]), own.dtype)
            window = jnp.concatenate([gbuf[c][before], own, pad], 0)
            band = band + lax.dot_general(own, window, dims, preferred_element_type=jnp.float32)
        bands[...] = band
        for j in range(tiles):
            turned = bands[j * TILE : (j + 1) * TILE]
            if j > 0:
                turned = pltpu.roll(turned, wide - j * TILE, 1)
            bsend[j] = packed(turned[:, :LANES])
            @pl.when(w != j)
            def _():
                grad_send(j).start()

    def act_bands():
        x_came(0).wait_recv()
        for d in range(1, nx):
            x_forwarded(d).wait_recv()

        @pl.when(w < tiles)
        def _():
            def one(d, carry):
                first = pl.multiple_of(z_at(d) * tz + w * TILE, 32)
                window = xbuf[pl.ds(first, 2 * TILE)]
                window = jnp.concatenate([window, jnp.zeros_like(window)], 0)
                dims = (((1,), (1,)), ((), ()))
                asend[d] = packed(
                    lax.dot_general(
                        window[TILE : 2 * TILE], window, dims, preferred_element_type=jnp.float32
                    )
                )
                @pl.when(d > 0)
                def _():
                    act_send(d).start()
                return carry
            lax.fori_loop(0, nz, one, 0)

    def weights():
        @pl.when(w < tiles)
        def _():
            act = asend[0]
            for d in range(1, nz):
                act_send(d).wait_recv()
                act = act + abuf[d]
            bbuf[w] = bsend[w]
            for d in range(1, nw):
                grad_came(w_at(d)).wait_recv()
            grad = bbuf[0]
            for u in range(1, nw):
                grad = grad + bbuf[u]
            tile = z * tiles + w
            first = pl.multiple_of(tile * TILE, 32)
            ids = idcol[pl.ds(first, 2 * TILE)]
            lane = lax.broadcasted_iota(jnp.int32, (8, LANES), 1)
            row = lax.broadcasted_iota(jnp.int32, (8, LANES), 0)
            group, partner = lane // TILE, lax.rem(lane, TILE)
            token = row + 8 * group
            mine = ids[TILE : TILE + 8]
            for k in range(1, 4):
                mine = jnp.where(group == k, ids[TILE + 8 * k : TILE + 8 * k + 8], mine)
            wide_lane = lax.broadcasted_iota(jnp.int32, (TILE, LANES), 1)
            wide_row = lax.broadcasted_iota(jnp.int32, (TILE, LANES), 0)
            pick = lax.rem(wide_lane, TILE) == wide_row
            before = jnp.sum(jnp.where(pick, ids[:TILE], 0.0), 0, keepdims=True)
            same = jnp.sum(jnp.where(pick, ids[TILE:], 0.0), 0, keepdims=True)
            theirs = jnp.where(partner <= token, same, before)
            factor = jnp.where(partner == token, 1.0, 2.0)
            factor = jnp.where(partner <= token, factor, jnp.where(tile > 0, 2.0, 0.0))
            term = jnp.where(mine == theirs, act * grad * factor, 0.0)
            at = lax.rem(tile, LANES // TILE) * TILE
            spread = jnp.zeros((8, LANES), jnp.float32)
            for k in range(4):
                one = jnp.sum(jnp.where(group == k, term, 0.0), 1, keepdims=True)
                spread = spread + jnp.where(lane == row + 8 * k + at, one, 0.0)
            wz[z] = jnp.sum(spread, 0, keepdims=True)
            for d in range(1, nz):
                weight_send(d).start()

    def slabs():
        @pl.when(w < tiles)
        def _():
            for d in range(1, nz):
                weight_came(d).wait_recv()
            wall[w] = wz[...]
            for d in range(1, nw):
                slab_send(d).start()

    def scales():
        for u in range(tiles):
            @pl.when(w != u)
            def _():
                slab_came(u).wait_recv()
        lane = lax.broadcasted_iota(jnp.int32, (8, LANES), 1)
        none = jnp.zeros((8, LANES), jnp.float32)
        flat = []
        for b in range(blocks):
            row = none
            for k in range(b * (LANES // TILE), (b + 1) * (LANES // TILE)):
                owner, j = divmod(k, tiles)
                row = row + jnp.broadcast_to(wall[j, owner], (8, LANES))
            flat.append(row)
        for b in range(blocks):
            before = flat[b - 1] if b > 0 else none
            after = flat[b + 1] if b < blocks - 1 else none
            rows[2, b] = flat[b]
            rows[3, b] = jnp.where(
                lane < TILE, after, jnp.where(lane >= LANES - TILE, before, none)
            )
        limit = clip_ref[0].astype(jnp.float32)

        def one(b, carry):
            at = pl.multiple_of(TILE + b * LANES, 32)
            ids = idcol[pl.ds(at, LANES)]
            found = jnp.where(ids == rows[0, b][0:1], rows[2, b][0:1], 0.0)
            found = found + jnp.where(ids == rows[1, b][0:1], rows[3, b][0:1], 0.0)
            squares = jnp.sum(found, 1, keepdims=True)
            factor = limit / jnp.maximum(jnp.sqrt(jnp.maximum(squares, 0.0)), limit)
            scaled = xbuf[pl.ds(at, LANES)].astype(jnp.float32) * factor
            st[:, pl.ds(pl.multiple_of(b * LANES, LANES), LANES)] = scaled.T.astype(st.dtype)
            return carry

        lax.fori_loop(0, blocks, one, 0)

    def forward_x():
        for d in range(1, nx):
            x_came(d).wait_recv()
            x_forward(d).start()

    first_slot = FIRST_SLOTS
    final_slot = first_slot[-1] + steps
    between = {0: (prepare,), 1: (grad_bands,), 2: (forward_x,), 3: (act_bands,), 5: (weights,),
               6: (slabs,), 7: (scales,)}

    def ring_sent(c):
        for s in range(steps):
            for way in range(2):
                ring(way, c, s).wait_send()

    def hop(t, c):
        s = t - first_slot[c]
        if 0 <= s < steps:
            for way in range(2):
                if s > 0:
                    ring(way, c, s - 1, incoming=True).wait_recv()
                ring(way, c, s).start()

    def first(c):
        for way in range(2):
            ring(way, c, steps - 1, incoming=True).wait_recv()
        if c >= plain:
            product_rest(c)
        else:
            product(c)
        ring_sent(c)

    def stages(p):
        for c in range(chunks):
            calls = (first, near, finish, forward_out, out_done)
            if c >= plain:
                calls = (first, direct_finish, direct_done)
            stage, rest = divmod(p - 2 * (first_slot[c] + steps) - c % 2, STAGE_GAP)
            if 0 <= stage < len(calls) and rest == 0:
                calls[stage](c)

    for t in range(final_slot):
        if t == 1:
            for c in range(chunks):
                halo_copy(c, incoming=True).wait_recv()
                own_g[c].wait()
        for c in range(0, chunks, 2):
            hop(t, c)
        if t == 0:
            for d in range(nx):
                x_first(d).start()
            for c in range(chunks):
                halo_copy(c).start()
            own_x.wait()
        for step in between.get(t, ()):
            step()
        stages(2 * t)
        for c in range(1, chunks, 2):
            hop(t, c)
        stages(2 * t + 1)
        for c in range(plain, chunks):
            if t == first_slot[c] + steps - 1:
                product_most(c)

    for c in range(chunks):
        halo_copy(c).wait_send()
    for d in range(nx):
        x_first(d).wait_send()
    for d in range(1, nx):
        x_forward(d).wait_send()
    for j in range(tiles):
        @pl.when(w != j)
        def _():
            grad_send(j).wait_send()

    @pl.when(w < tiles)
    def _():
        for d in range(1, nz):
            act_send(d).wait_send()
            weight_send(d).wait_send()
        for d in range(1, nw):
            slab_send(d).wait_send()

    for p in range(2 * final_slot, 2 * final_slot + 5 * STAGE_GAP):
        stages(p)


def body(sizes, activations, out_grads, query_ids, clip_bound):
    x_local = activations[0]
    g_local = out_grads[0]
    ny, nz, nw, tokens = sizes
    nx = nw // 2
    features, hidden = x_local.shape[1], g_local.shape[1]
    tz = g_local.shape[0]
    tiles = tz // TILE
    chunks = len(WIDTHS)
    assert sum(WIDTHS) == hidden
    steps = nz // 2
    part = features // ny
    dma = pltpu.SemaphoreType.DMA
    f32, bf16 = jnp.float32, jnp.bfloat16
    stay = [
        pltpu.with_memory_space_constraint(a, pltpu.HBM) for a in (x_local, g_local, query_ids)
    ]
    return pl.pallas_call(
        functools.partial(kernel, sizes),
        out_shape=jax.ShapeDtypeStruct((features, hidden), f32),
        in_specs=[
            pl.BlockSpec(memory_space=pltpu.HBM),
            pl.BlockSpec(memory_space=pltpu.HBM),
            pl.BlockSpec(memory_space=pltpu.HBM),
            pl.BlockSpec(memory_space=pltpu.SMEM),
        ],
        out_specs=pl.BlockSpec(memory_space=pl.ANY),
        scratch_shapes=[
            pltpu.VMEM((1, tokens), jnp.int32),
            pltpu.VMEM((tz, -(-(tz + TILE) // LANES) * LANES), f32),
            [pltpu.VMEM((tokens, n), bf16) for n in WIDTHS],
            pltpu.VMEM((TILE + tokens, features), bf16),
            pltpu.VMEM((features, tokens), bf16),
            pltpu.VMEM((TILE + tokens, LANES), f32),
            pltpu.VMEM((4, tokens // LANES, 8, LANES), f32),
            pltpu.VMEM((nz, 8, LANES), f32),
            pltpu.VMEM((nz, 8, LANES), f32),
            pltpu.VMEM((tiles, 8, LANES), f32),
            pltpu.VMEM((nw, 8, LANES), f32),
            pltpu.VMEM((nz, 1, LANES), f32),
            pltpu.VMEM((tiles, nz, 1, LANES), f32),
            [pltpu.VMEM((features, n), f32) for n in WIDTHS],
            [pltpu.VMEM((2, part // 2, n), f32) for n in WIDTHS],
            [pltpu.VMEM((2, part, n), f32) for n in WIDTHS],
            [pltpu.VMEM((part, n), f32) for n in WIDTHS],
            [pltpu.VMEM((ny - 1, part, n), f32) for n in WIDTHS[-DIRECT:]],
            dma((chunks + 2,)), dma((chunks,)),
            dma((2 * nx,)), dma((2 * nx,)),
            dma((2, chunks)),
            dma((2, chunks, steps)), dma((2, chunks, steps)),
            dma((nz,)), dma((nz,)),
            dma((tiles,)), dma((nw,)),
            dma((nw,)), dma((tiles,)),
            dma((nz,)), dma((nz,)),
            *[dma((chunks, 2))] * 8,
            dma((4, DIRECT, ny - 1)),
        ],
        compiler_params=pltpu.CompilerParams(
            collective_id=0, has_side_effects=True, vmem_limit_bytes=50 * 1024 * 1024
        ),
        cost_estimate=pl.CostEstimate(
            flops=2 * tokens * features * hidden, bytes_accessed=1 << 23, transcendentals=0
        ),
    )(*stay, clip_bound)


def solution(mesh):
    sizes = tuple(mesh.shape[a] for a in ("dp", "row", "col"))

    def run(activations, out_grads, query_ids, clip_bound):
        placed = (P("dp", "col", "row"), P("dp", "row", "col"), P("dp", None), P())
        return jax.shard_map(
            functools.partial(body, sizes + (query_ids.shape[1],)),
            mesh=mesh, in_specs=placed, out_specs=P("row", "col"), check_vma=False,
        )(activations, out_grads, query_ids, clip_bound)

    return run
```

```python
import functools

import jax
import jax.numpy as jnp
from jax import lax
from jax.experimental import pallas as pl
from jax.experimental.pallas import tpu as pltpu
from jax.sharding import PartitionSpec as P

TILE = 32
LANES = 128
WIDTHS = (256, 256, 256, 256, 256, 256, 256)
FIRST_SLOTS = (0, 0, 0, 1, 3, 6, 7)
STAGE_GAP = 2
DIRECT = 2
SPLIT = 3
AHEAD = 3
MESH = pl.DeviceIdType.MESH


def packed(products):
    lane = lax.broadcasted_iota(jnp.int32, (TILE, LANES), 1)
    row = lax.broadcasted_iota(jnp.int32, (TILE, LANES), 0)
    near = jnp.where(lane <= row, pltpu.roll(products, LANES - TILE, 1), products)
    group = lax.broadcasted_iota(jnp.int32, (8, LANES), 1) // TILE
    out = near[:8]
    for k in range(1, 4):
        out = jnp.where(group == k, pltpu.roll(near[8 * k : 8 * k + 8], TILE * k, 1), out)
    return out


def kernel(
    sizes,
    x_ref, g_ref, ids_ref, clip_ref,
    out_ref,
    ids_vmem, bands, gbuf, xbuf, st, idcol, rows,
    asend, abuf, bsend, bbuf, wz, wall,
    pbuf, rfar, rnear, qbuf, rdir,
    lsem, osem, xs, xr, hs, rs, rr, asem, arec, bsem, brec, wsem, wrec, zsem, zrec,
    s1, r1, s2, r2, s3, r3, s4, r4, sd,
):
    ny, nz, nw, tokens = sizes
    nx = nw // 2
    tz = g_ref.shape[0]
    tc = x_ref.shape[0]
    tiles = tz // TILE
    chunks = len(WIDTHS)
    plain = chunks - DIRECT
    columns = [pl.ds(sum(WIDTHS[:c]), WIDTHS[c]) for c in range(chunks)]
    steps = nz // 2
    wide = bands.shape[1]
    blocks = tokens // LANES
    part = x_ref.shape[1] // ny

    y = lax.axis_index("dp")
    z = lax.axis_index("row")
    w = lax.axis_index("col")
    core = lax.rem(w, 2)
    chip = w // 2

    def z_at(d):
        return lax.rem(z + d, nz)

    def w_at(d):
        return lax.rem(w + d, nw)

    def y_at(d):
        return lax.rem(y + d, ny)

    def copy_to(src, dst, send, recv, **axis):
        return pltpu.make_async_remote_copy(
            src_ref=src, dst_ref=dst, send_sem=send, recv_sem=recv,
            device_id=axis, device_id_type=MESH,
        )

    own_rows = pl.ds(pl.multiple_of(z * tz, 32), tz)
    own_g = [
        pltpu.make_async_copy(
            g_ref.at[:, columns[c]], gbuf[c].at[own_rows], lsem.at[c]
        )
        for c in range(chunks)
    ]
    own_x = pltpu.make_async_copy(
        x_ref, xbuf.at[pl.ds(pl.multiple_of(TILE + w * tc, 32), tc)], lsem.at[chunks]
    )
    own_ids = pltpu.make_async_copy(ids_ref, ids_vmem, lsem.at[chunks + 1])
    for copy in own_g:
        copy.start()
    own_x.start()
    own_ids.start()

    barrier = pltpu.get_barrier_semaphore()
    for d in range(1, nz):
        pl.semaphore_signal(barrier, inc=1, device_id={"row": z_at(d)}, device_id_type=MESH)
    for d in range(1, nw):
        pl.semaphore_signal(barrier, inc=1, device_id={"col": w_at(d)}, device_id_type=MESH)
    for d in range(1, ny):
        pl.semaphore_signal(barrier, inc=1, device_id={"dp": y_at(d)}, device_id_type=MESH)
    pl.semaphore_wait(barrier, nz + nw + ny - 3)

    def x_rows(owner):
        return xbuf.at[pl.ds(pl.multiple_of(TILE + owner * tc, 32), tc)]

    sibling = chip * 2 + 1 - core

    def x_first(d):
        to = sibling if d == 0 else lax.rem(chip + d, nx) * 2 + core
        return copy_to(x_ref, x_rows(w), xs.at[d], xr.at[d], col=to)

    def x_came(d):
        owner = sibling if d == 0 else lax.rem(chip + nx - d, nx) * 2 + core
        return copy_to(x_rows(owner), x_rows(owner), xs.at[d], xr.at[d], col=sibling)

    def x_forward(d):
        owner = lax.rem(chip + nx - d, nx) * 2 + core
        return copy_to(
            x_rows(owner), x_rows(owner), xs.at[nx - 1 + d], xr.at[nx - 1 + d], col=sibling
        )

    def x_forwarded(d):
        owner = lax.rem(chip + nx - d, nx) * 2 + 1 - core
        return copy_to(
            x_rows(owner), x_rows(owner), xs.at[nx - 1 + d], xr.at[nx - 1 + d], col=sibling
        )

    def ring(way, c, s, incoming=False):
        hop = s + 1 if incoming else s
        owner = z_at(nz - hop) if way == 0 else z_at(hop)
        skip, count = 0, tz
        if s == steps - 1:
            skip, count = way * (tz // 2), tz // 2
        elif s == 0 and way == 0:
            count = tz - TILE
        block = gbuf[c].at[pl.ds(pl.multiple_of(owner * tz + skip, 32), count)]
        src = block
        if s == 0 and not incoming:
            src = g_ref.at[pl.ds(0, count), columns[c]]
        to = z_at(1) if way == 0 else z_at(nz - 1)
        return copy_to(src, block, rs.at[way, c, s], rr.at[way, c, s], row=to)

    def halo_copy(c, incoming=False):
        owner = z_at(nz - 1) if incoming else z
        there = gbuf[c].at[pl.ds(pl.multiple_of(owner * tz + tz - TILE, 32), TILE)]
        src = there if incoming else g_ref.at[pl.ds(tz - TILE, TILE), columns[c]]
        return copy_to(src, there, hs.at[0, c], hs.at[1, c], row=z_at(1))

    def act_send(d):
        return copy_to(asend.at[d], abuf.at[d], asem.at[d], arec.at[d], row=z_at(d))

    def grad_send(j):
        return copy_to(bsend.at[j], bbuf.at[w], bsem.at[j], brec.at[w], col=j)

    def grad_came(owner):
        return copy_to(bbuf.at[owner], bbuf.at[owner], bsem.at[0], brec.at[owner], col=w_at(1))

    def weight_send(d):
        return copy_to(wz.at[z], wz.at[z], zsem.at[d], zrec.at[d], row=z_at(d))

    def weight_came(d):
        owner = z_at(nz - d)
        return copy_to(wz.at[owner], wz.at[owner], zsem.at[d], zrec.at[d], row=z_at(1))

    def slab_send(d):
        return copy_to(wz, wall.at[w], wsem.at[d], wrec.at[w], col=w_at(d))

    def slab_came(owner):
        return copy_to(wall.at[owner], wall.at[owner], wsem.at[1], wrec.at[owner], col=w_at(1))

    up, far, down = y_at(1), y_at(2), y_at(3)
    half = part // 2

    def quarter(owner, side=None):
        if side is None:
            return pl.ds(pl.multiple_of(owner * part, part), part)
        return pl.ds(pl.multiple_of(owner * part + side * half, half), half)

    def far_send(c, side):
        return copy_to(
            pbuf[c].at[quarter(far, side)], rfar[c].at[side], s1.at[c, side], r1.at[c, side],
            dp=(up, down)[side],
        )

    def near_send(c, side):
        to = (up, down)[side]
        return copy_to(
            pbuf[c].at[quarter(to)], rnear[c].at[side], s2.at[c, side], r2.at[c, side], dp=to
        )

    def out_at(c, where):
        return out_ref.at[where, columns[c]]

    def out_send(c, side, incoming=False):
        at = out_at(c, quarter((down, up)[side] if incoming else y))
        return copy_to(
            at if incoming else qbuf[c], at, s3.at[c, side], r3.at[c, side],
            dp=(up, down)[side],
        )

    def out_forward(c, side, incoming=False):
        at = out_at(c, quarter(far if incoming else (down, up)[side], side))
        return copy_to(at, at, s4.at[c, side], r4.at[c, side], dp=(up, down)[side])

    def direct_send(c, d):
        to = y_at(d)
        return copy_to(
            pbuf[c].at[quarter(to)], rdir[c - plain].at[d - 1],
            sd.at[0, c - plain, d - 1], sd.at[1, c - plain, d - 1], dp=to,
        )

    def direct_out(c, d, incoming=False):
        at = out_at(c, quarter(y_at(ny - d) if incoming else y))
        return copy_to(
            at if incoming else qbuf[c], at,
            sd.at[2, c - plain, d - 1], sd.at[3, c - plain, d - 1], dp=y_at(d),
        )

    def out_own(c):
        return pltpu.make_async_copy(qbuf[c], out_at(c, quarter(y)), osem.at[c])

    def product(c):
        depth = tokens // 3 if tokens % (3 * LANES) == 0 else LANES
        for k in range(tokens // depth):
            at = pl.ds(k * depth, depth)
            term = jnp.dot(st[:, at], gbuf[c][at], preferred_element_type=jnp.float32)
            pbuf[c][...] = term if k == 0 else pbuf[c][...] + term
        for side in range(2):
            far_send(c, side).start()

    def product_pair(c, i):
        pair = lax.rem(lax.rem(z + steps, nz) // 2 + i, steps)
        at = pl.ds(pl.multiple_of(pair * 2 * tz, LANES), 2 * tz)
        return jnp.dot(st[:, at], gbuf[c][at], preferred_element_type=jnp.float32)

    def product_most(c):
        pbuf[c][...] = product_pair(c, 1)

        def one(i, carry):
            pbuf[c][...] = pbuf[c][...] + product_pair(c, i)
            return carry

        lax.fori_loop(2, steps, one, 0)

    def product_rest(c):
        pbuf[c][...] = pbuf[c][...] + product_pair(c, 0)
        if c < plain:
            for side in range(2):
                far_send(c, side).start()
        else:
            for d in range(1, ny):
                direct_send(c, d).start()

    def direct_finish(c):
        total = pbuf[c][quarter(y)]
        for d in range(1, ny):
            direct_send(c, d).wait_recv()
            total = total + rdir[c - plain][d - 1]
        qbuf[c][...] = total
        for d in range(1, ny):
            direct_out(c, d).start()
        out_own(c).start()

    def direct_done(c):
        for d in range(1, ny):
            direct_out(c, d, incoming=True).wait_recv()
            direct_send(c, d).wait_send()
            direct_out(c, d).wait_send()
        out_own(c).wait()

    def near(c):
        for side in range(2):
            far_send(c, side).wait_recv()
            where = quarter((up, down)[side], side)
            pbuf[c][where] = pbuf[c][where] + rfar[c][side]
            near_send(c, side).start()

    def finish(c):
        total = pbuf[c][quarter(y)]
        for side in range(2):
            near_send(c, side).wait_recv()
            total = total + rnear[c][side]
        qbuf[c][...] = total
        for side in range(2):
            out_send(c, side).start()
        out_own(c).start()

    def forward_out(c):
        for side in range(2):
            out_send(c, side, incoming=True).wait_recv()
            out_forward(c, side).start()

    def out_done(c):
        for side in range(2):
            out_forward(c, side, incoming=True).wait_recv()
            far_send(c, side).wait_send()
            near_send(c, side).wait_send()
            out_send(c, side).wait_send()
            out_forward(c, side).wait_send()
        out_own(c).wait()

    def prepare():
        own_ids.wait()
        idcol[0:TILE] = jnp.full((TILE, LANES), -1.0, jnp.float32)
        xbuf[0:TILE] = jnp.zeros((TILE, xbuf.shape[1]), xbuf.dtype)
        lane = lax.broadcasted_iota(jnp.int32, (8, LANES), 1)
        none = jnp.full((8, LANES), -1.0, jnp.float32)
        flat = []
        for b in range(blocks):
            row = ids_vmem[0:1, b * LANES : (b + 1) * LANES].astype(jnp.float32)
            flat.append(jnp.broadcast_to(row, (8, LANES)))
            idcol[TILE + b * LANES : TILE + (b + 1) * LANES] = jnp.broadcast_to(
                row, (LANES, LANES)
            ).T
        for b in range(blocks):
            before = flat[b - 1] if b > 0 else none
            after = flat[b + 1] if b < blocks - 1 else none
            rows[0, b] = flat[b]
            rows[1, b] = jnp.where(
                lane < TILE, after, jnp.where(lane >= LANES - TILE, before, none)
            )

    def grad_bands():
        before = pl.ds(pl.multiple_of(z_at(nz - 1) * tz + tz - TILE, 32), TILE)
        dims = (((1,), (1,)), ((), ()))
        band = jnp.zeros((tz, wide), jnp.float32)
        for c in range(chunks):
            own = gbuf[c][own_rows]
            pad = jnp.zeros((wide - tz - TILE, WIDTHS[c]), own.dtype)
            window = jnp.concatenate([gbuf[c][before], own, pad], 0)
            band = band + lax.dot_general(own, window, dims, preferred_element_type=jnp.float32)
        bands[...] = band
        for j in range(tiles):
            turned = bands[j * TILE : (j + 1) * TILE]
            if j > 0:
                turned = pltpu.roll(turned, wide - j * TILE, 1)
            bsend[j] = packed(turned[:, :LANES])
            @pl.when(w != j)
            def _():
                grad_send(j).start()

    def act_bands():
        x_came(0).wait_recv()
        for d in range(1, nx):
            x_forwarded(d).wait_recv()

        @pl.when(w < tiles)
        def _():
            def one(d, carry):
                first = pl.multiple_of(z_at(d) * tz + w * TILE, 32)
                window = xbuf[pl.ds(first, 2 * TILE)]
                window = jnp.concatenate([window, jnp.zeros_like(window)], 0)
                dims = (((1,), (1,)), ((), ()))
                asend[d] = packed(
                    lax.dot_general(
                        window[TILE : 2 * TILE], window, dims, preferred_element_type=jnp.float32
                    )
                )
                @pl.when(d > 0)
                def _():
                    act_send(d).start()
                return carry
            lax.fori_loop(0, nz, one, 0)

    def weights():
        @pl.when(w < tiles)
        def _():
            act = asend[0]
            for d in range(1, nz):
                act_send(d).wait_recv()
                act = act + abuf[d]
            bbuf[w] = bsend[w]
            for d in range(1, nw):
                grad_came(w_at(d)).wait_recv()
            grad = bbuf[0]
            for u in range(1, nw):
                grad = grad + bbuf[u]
            tile = z * tiles + w
            first = pl.multiple_of(tile * TILE, 32)
            ids = idcol[pl.ds(first, 2 * TILE)]
            lane = lax.broadcasted_iota(jnp.int32, (8, LANES), 1)
            row = lax.broadcasted_iota(jnp.int32, (8, LANES), 0)
            group, partner = lane // TILE, lax.rem(lane, TILE)
            token = row + 8 * group
            mine = ids[TILE : TILE + 8]
            for k in range(1, 4):
                mine = jnp.where(group == k, ids[TILE + 8 * k : TILE + 8 * k + 8], mine)
            wide_lane = lax.broadcasted_iota(jnp.int32, (TILE, LANES), 1)
            wide_row = lax.broadcasted_iota(jnp.int32, (TILE, LANES), 0)
            pick = lax.rem(wide_lane, TILE) == wide_row
            before = jnp.sum(jnp.where(pick, ids[:TILE], 0.0), 0, keepdims=True)
            same = jnp.sum(jnp.where(pick, ids[TILE:], 0.0), 0, keepdims=True)
            theirs = jnp.where(partner <= token, same, before)
            factor = jnp.where(partner == token, 1.0, 2.0)
            factor = jnp.where(partner <= token, factor, jnp.where(tile > 0, 2.0, 0.0))
            term = jnp.where(mine == theirs, act * grad * factor, 0.0)
            at = lax.rem(tile, LANES // TILE) * TILE
            spread = jnp.zeros((8, LANES), jnp.float32)
            for k in range(4):
                one = jnp.sum(jnp.where(group == k, term, 0.0), 1, keepdims=True)
                spread = spread + jnp.where(lane == row + 8 * k + at, one, 0.0)
            wz[z] = jnp.sum(spread, 0, keepdims=True)
            for d in range(1, nz):
                weight_send(d).start()

    def slabs():
        @pl.when(w < tiles)
        def _():
            for d in range(1, nz):
                weight_came(d).wait_recv()
            wall[w] = wz[...]
            for d in range(1, nw):
                slab_send(d).start()

    def scales():
        for u in range(tiles):
            @pl.when(w != u)
            def _():
                slab_came(u).wait_recv()
        lane = lax.broadcasted_iota(jnp.int32, (8, LANES), 1)
        none = jnp.zeros((8, LANES), jnp.float32)
        flat = []
        for b in range(blocks):
            row = none
            for k in range(b * (LANES // TILE), (b + 1) * (LANES // TILE)):
                owner, j = divmod(k, tiles)
                row = row + jnp.broadcast_to(wall[j, owner], (8, LANES))
            flat.append(row)
        for b in range(blocks):
            before = flat[b - 1] if b > 0 else none
            after = flat[b + 1] if b < blocks - 1 else none
            rows[2, b] = flat[b]
            rows[3, b] = jnp.where(
                lane < TILE, after, jnp.where(lane >= LANES - TILE, before, none)
            )
        limit = clip_ref[0].astype(jnp.float32)

        def one(b, carry):
            at = pl.multiple_of(TILE + b * LANES, 32)
            ids = idcol[pl.ds(at, LANES)]
            found = jnp.where(ids == rows[0, b][0:1], rows[2, b][0:1], 0.0)
            found = found + jnp.where(ids == rows[1, b][0:1], rows[3, b][0:1], 0.0)
            squares = jnp.sum(found, 1, keepdims=True)
            factor = limit / jnp.maximum(jnp.sqrt(jnp.maximum(squares, 0.0)), limit)
            scaled = xbuf[pl.ds(at, LANES)].astype(jnp.float32) * factor
            st[:, pl.ds(pl.multiple_of(b * LANES, LANES), LANES)] = scaled.T.astype(st.dtype)
            return carry

        lax.fori_loop(0, blocks, one, 0)

    def forward_x():
        for d in range(1, nx):
            x_came(d).wait_recv()
            x_forward(d).start()

    first_slot = FIRST_SLOTS
    final_slot = first_slot[-1] + steps
    between = {0: (prepare,), 1: (grad_bands,), 2: (forward_x,), 3: (act_bands,), 5: (weights,),
               6: (slabs,), 7: (scales,)}

    def ring_sent(c):
        for s in range(steps):
            for way in range(2):
                ring(way, c, s).wait_send()

    def hop(t, c):
        s = t - first_slot[c]
        if 0 <= s < steps:
            for way in range(2):
                if s > 0:
                    ring(way, c, s - 1, incoming=True).wait_recv()
                if (s, c) == (0, AHEAD):
                    @pl.when(core == 1)
                    def _():
                        ring(way, c, s).start()
                else:
                    ring(way, c, s).start()

    def first(c):
        for way in range(2):
            ring(way, c, steps - 1, incoming=True).wait_recv()
        if c >= chunks - SPLIT:
            product_rest(c)
        else:
            product(c)
        ring_sent(c)

    def stages(p):
        for c in range(chunks):
            calls = (first, near, finish, forward_out, out_done)
            if c >= plain:
                calls = (first, direct_finish, direct_done)
            stage, rest = divmod(p - 2 * (first_slot[c] + steps) - c % 2, STAGE_GAP)
            if 0 <= stage < len(calls) and rest == 0:
                calls[stage](c)

    for t in range(final_slot):
        if t == 1:
            for c in range(chunks):
                halo_copy(c, incoming=True).wait_recv()
                own_g[c].wait()
        for c in range(0, chunks, 2):
            hop(t, c)
        if t == 0:
            @pl.when(core == 0)
            def _():
                for way in range(2):
                    ring(way, AHEAD, 0).start()
            for d in range(nx):
                x_first(d).start()
            for c in range(chunks):
                halo_copy(c).start()
            own_x.wait()
        for step in between.get(t, ()):
            step()
        stages(2 * t)
        for c in range(1, chunks, 2):
            hop(t, c)
        stages(2 * t + 1)
        for c in range(chunks - SPLIT, chunks):
            if t == first_slot[c] + steps - 1:
                product_most(c)

    for c in range(chunks):
        halo_copy(c).wait_send()
    for d in range(nx):
        x_first(d).wait_send()
    for d in range(1, nx):
        x_forward(d).wait_send()
    for j in range(tiles):
        @pl.when(w != j)
        def _():
            grad_send(j).wait_send()

    @pl.when(w < tiles)
    def _():
        for d in range(1, nz):
            act_send(d).wait_send()
            weight_send(d).wait_send()
        for d in range(1, nw):
            slab_send(d).wait_send()

    for p in range(2 * final_slot, 2 * final_slot + 5 * STAGE_GAP):
        stages(p)


def body(sizes, activations, out_grads, query_ids, clip_bound):
    x_local = activations[0]
    g_local = out_grads[0]
    ny, nz, nw, tokens = sizes
    nx = nw // 2
    features, hidden = x_local.shape[1], g_local.shape[1]
    tz = g_local.shape[0]
    tiles = tz // TILE
    chunks = len(WIDTHS)
    assert sum(WIDTHS) == hidden
    steps = nz // 2
    part = features // ny
    dma = pltpu.SemaphoreType.DMA
    f32, bf16 = jnp.float32, jnp.bfloat16
    stay = [
        pltpu.with_memory_space_constraint(a, pltpu.HBM) for a in (x_local, g_local, query_ids)
    ]
    return pl.pallas_call(
        functools.partial(kernel, sizes),
        out_shape=jax.ShapeDtypeStruct((features, hidden), f32),
        in_specs=[
            pl.BlockSpec(memory_space=pltpu.HBM),
            pl.BlockSpec(memory_space=pltpu.HBM),
            pl.BlockSpec(memory_space=pltpu.HBM),
            pl.BlockSpec(memory_space=pltpu.SMEM),
        ],
        out_specs=pl.BlockSpec(memory_space=pl.ANY),
        scratch_shapes=[
            pltpu.VMEM((1, tokens), jnp.int32),
            pltpu.VMEM((tz, -(-(tz + TILE) // LANES) * LANES), f32),
            [pltpu.VMEM((tokens, n), bf16) for n in WIDTHS],
            pltpu.VMEM((TILE + tokens, features), bf16),
            pltpu.VMEM((features, tokens), bf16),
            pltpu.VMEM((TILE + tokens, LANES), f32),
            pltpu.VMEM((4, tokens // LANES, 8, LANES), f32),
            pltpu.VMEM((nz, 8, LANES), f32),
            pltpu.VMEM((nz, 8, LANES), f32),
            pltpu.VMEM((tiles, 8, LANES), f32),
            pltpu.VMEM((nw, 8, LANES), f32),
            pltpu.VMEM((nz, 1, LANES), f32),
            pltpu.VMEM((tiles, nz, 1, LANES), f32),
            [pltpu.VMEM((features, n), f32) for n in WIDTHS],
            [pltpu.VMEM((2, part // 2, n), f32) for n in WIDTHS],
            [pltpu.VMEM((2, part, n), f32) for n in WIDTHS],
            [pltpu.VMEM((part, n), f32) for n in WIDTHS],
            [pltpu.VMEM((ny - 1, part, n), f32) for n in WIDTHS[-DIRECT:]],
            dma((chunks + 2,)), dma((chunks,)),
            dma((2 * nx,)), dma((2 * nx,)),
            dma((2, chunks)),
            dma((2, chunks, steps)), dma((2, chunks, steps)),
            dma((nz,)), dma((nz,)),
            dma((tiles,)), dma((nw,)),
            dma((nw,)), dma((tiles,)),
            dma((nz,)), dma((nz,)),
            *[dma((chunks, 2))] * 8,
            dma((4, DIRECT, ny - 1)),
        ],
        compiler_params=pltpu.CompilerParams(
            collective_id=0, has_side_effects=True, vmem_limit_bytes=50 * 1024 * 1024
        ),
        cost_estimate=pl.CostEstimate(
            flops=2 * tokens * features * hidden, bytes_accessed=1 << 23, transcendentals=0
        ),
    )(*stay, clip_bound)


def solution(mesh):
    sizes = tuple(mesh.shape[a] for a in ("dp", "row", "col"))

    def run(activations, out_grads, query_ids, clip_bound):
        placed = (P("dp", "col", "row"), P("dp", "row", "col"), P("dp", None), P())
        return jax.shard_map(
            functools.partial(body, sizes + (query_ids.shape[1],)),
            mesh=mesh, in_specs=placed, out_specs=P("row", "col"), check_vma=False,
        )(activations, out_grads, query_ids, clip_bound)

    return run
```

```python
import functools

import jax
import jax.numpy as jnp
from jax import lax
from jax.experimental import pallas as pl
from jax.experimental.pallas import tpu as pltpu
from jax.sharding import PartitionSpec as P

TILE = 32
LANES = 128
WIDTHS = (256, 256, 256, 256, 256, 256, 256)
FIRST_SLOTS = (0, 0, 0, 1, 2, 6, 7)
STAGE_GAP = 2
DIRECT = 2
MESH = pl.DeviceIdType.MESH


def packed(products):
    lane = lax.broadcasted_iota(jnp.int32, (TILE, LANES), 1)
    row = lax.broadcasted_iota(jnp.int32, (TILE, LANES), 0)
    near = jnp.where(lane <= row, pltpu.roll(products, LANES - TILE, 1), products)
    group = lax.broadcasted_iota(jnp.int32, (8, LANES), 1) // TILE
    out = near[:8]
    for k in range(1, 4):
        out = jnp.where(group == k, pltpu.roll(near[8 * k : 8 * k + 8], TILE * k, 1), out)
    return out


def kernel(
    sizes,
    x_ref, g_ref, ids_ref, clip_ref,
    out_ref,
    ids_vmem, bands, gbuf, xbuf, st, idcol, rows,
    asend, abuf, bsend, bbuf, wz, wall,
    pbuf, rfar, rnear, qbuf, rdir,
    lsem, osem, xs, xr, hs, rs, rr, asem, arec, bsem, brec, wsem, wrec, zsem, zrec,
    s1, r1, s2, r2, s3, r3, s4, r4, sd,
):
    ny, nz, nw, tokens = sizes
    nx = nw // 2
    tz = g_ref.shape[0]
    tc = x_ref.shape[0]
    tiles = tz // TILE
    chunks = len(WIDTHS)
    plain = chunks - DIRECT
    columns = [pl.ds(sum(WIDTHS[:c]), WIDTHS[c]) for c in range(chunks)]
    steps = nz // 2
    wide = bands.shape[1]
    blocks = tokens // LANES
    part = x_ref.shape[1] // ny

    y = lax.axis_index("dp")
    z = lax.axis_index("row")
    w = lax.axis_index("col")
    core = lax.rem(w, 2)
    chip = w // 2

    def z_at(d):
        return lax.rem(z + d, nz)

    def w_at(d):
        return lax.rem(w + d, nw)

    def y_at(d):
        return lax.rem(y + d, ny)

    def copy_to(src, dst, send, recv, **axis):
        return pltpu.make_async_remote_copy(
            src_ref=src, dst_ref=dst, send_sem=send, recv_sem=recv,
            device_id=axis, device_id_type=MESH,
        )

    own_rows = pl.ds(pl.multiple_of(z * tz, 32), tz)
    own_g = [
        pltpu.make_async_copy(
            g_ref.at[:, columns[c]], gbuf[c].at[own_rows], lsem.at[c]
        )
        for c in range(chunks)
    ]
    own_x = pltpu.make_async_copy(
        x_ref, xbuf.at[pl.ds(pl.multiple_of(TILE + w * tc, 32), tc)], lsem.at[chunks]
    )
    own_ids = pltpu.make_async_copy(ids_ref, ids_vmem, lsem.at[chunks + 1])
    for copy in own_g:
        copy.start()
    own_x.start()
    own_ids.start()

    barrier = pltpu.get_barrier_semaphore()
    for d in range(1, nz):
        pl.semaphore_signal(barrier, inc=1, device_id={"row": z_at(d)}, device_id_type=MESH)
    for d in range(1, nw):
        pl.semaphore_signal(barrier, inc=1, device_id={"col": w_at(d)}, device_id_type=MESH)
    for d in range(1, ny):
        pl.semaphore_signal(barrier, inc=1, device_id={"dp": y_at(d)}, device_id_type=MESH)
    pl.semaphore_wait(barrier, nz + nw + ny - 3)

    def x_rows(owner):
        return xbuf.at[pl.ds(pl.multiple_of(TILE + owner * tc, 32), tc)]

    sibling = chip * 2 + 1 - core

    def x_first(d):
        to = sibling if d == 0 else lax.rem(chip + d, nx) * 2 + core
        return copy_to(x_ref, x_rows(w), xs.at[d], xr.at[d], col=to)

    def x_came(d):
        owner = sibling if d == 0 else lax.rem(chip + nx - d, nx) * 2 + core
        return copy_to(x_rows(owner), x_rows(owner), xs.at[d], xr.at[d], col=sibling)

    def x_forward(d):
        owner = lax.rem(chip + nx - d, nx) * 2 + core
        return copy_to(
            x_rows(owner), x_rows(owner), xs.at[nx - 1 + d], xr.at[nx - 1 + d], col=sibling
        )

    def x_forwarded(d):
        owner = lax.rem(chip + nx - d, nx) * 2 + 1 - core
        return copy_to(
            x_rows(owner), x_rows(owner), xs.at[nx - 1 + d], xr.at[nx - 1 + d], col=sibling
        )

    def ring(way, c, s, incoming=False):
        hop = s + 1 if incoming else s
        owner = z_at(nz - hop) if way == 0 else z_at(hop)
        skip, count = 0, tz
        if s == steps - 1:
            skip, count = way * (tz // 2), tz // 2
        elif s == 0 and way == 0:
            count = tz - TILE
        block = gbuf[c].at[pl.ds(pl.multiple_of(owner * tz + skip, 32), count)]
        src = block
        if s == 0 and not incoming:
            src = g_ref.at[pl.ds(0, count), columns[c]]
        to = z_at(1) if way == 0 else z_at(nz - 1)
        return copy_to(src, block, rs.at[way, c, s], rr.at[way, c, s], row=to)

    def halo_copy(c, incoming=False):
        owner = z_at(nz - 1) if incoming else z
        there = gbuf[c].at[pl.ds(pl.multiple_of(owner * tz + tz - TILE, 32), TILE)]
        src = there if incoming else g_ref.at[pl.ds(tz - TILE, TILE), columns[c]]
        return copy_to(src, there, hs.at[0, c], hs.at[1, c], row=z_at(1))

    def act_send(d):
        return copy_to(asend.at[d], abuf.at[d], asem.at[d], arec.at[d], row=z_at(d))

    def grad_send(j):
        return copy_to(bsend.at[j], bbuf.at[w], bsem.at[j], brec.at[w], col=j)

    def grad_came(owner):
        return copy_to(bbuf.at[owner], bbuf.at[owner], bsem.at[0], brec.at[owner], col=w_at(1))

    def weight_send(d):
        return copy_to(wz.at[z], wz.at[z], zsem.at[d], zrec.at[d], row=z_at(d))

    def weight_came(d):
        owner = z_at(nz - d)
        return copy_to(wz.at[owner], wz.at[owner], zsem.at[d], zrec.at[d], row=z_at(1))

    def slab_send(d):
        return copy_to(wz, wall.at[w], wsem.at[d], wrec.at[w], col=w_at(d))

    def slab_came(owner):
        return copy_to(wall.at[owner], wall.at[owner], wsem.at[1], wrec.at[owner], col=w_at(1))

    up, far, down = y_at(1), y_at(2), y_at(3)
    half = part // 2

    def quarter(owner, side=None):
        if side is None:
            return pl.ds(pl.multiple_of(owner * part, part), part)
        return pl.ds(pl.multiple_of(owner * part + side * half, half), half)

    def far_send(c, side):
        return copy_to(
            pbuf[c].at[quarter(far, side)], rfar[c].at[side], s1.at[c, side], r1.at[c, side],
            dp=(up, down)[side],
        )

    def near_send(c, side):
        to = (up, down)[side]
        return copy_to(
            pbuf[c].at[quarter(to)], rnear[c].at[side], s2.at[c, side], r2.at[c, side], dp=to
        )

    def out_at(c, where):
        return out_ref.at[where, columns[c]]

    def out_send(c, side, incoming=False):
        at = out_at(c, quarter((down, up)[side] if incoming else y))
        return copy_to(
            at if incoming else qbuf[c], at, s3.at[c, side], r3.at[c, side],
            dp=(up, down)[side],
        )

    def out_forward(c, side, incoming=False):
        at = out_at(c, quarter(far if incoming else (down, up)[side], side))
        return copy_to(at, at, s4.at[c, side], r4.at[c, side], dp=(up, down)[side])

    def direct_send(c, d):
        to = y_at(d)
        return copy_to(
            pbuf[c].at[quarter(to)], rdir[c - plain].at[d - 1],
            sd.at[0, c - plain, d - 1], sd.at[1, c - plain, d - 1], dp=to,
        )

    def direct_out(c, d, incoming=False):
        at = out_at(c, quarter(y_at(ny - d) if incoming else y))
        return copy_to(
            at if incoming else qbuf[c], at,
            sd.at[2, c - plain, d - 1], sd.at[3, c - plain, d - 1], dp=y_at(d),
        )

    def out_own(c):
        return pltpu.make_async_copy(qbuf[c], out_at(c, quarter(y)), osem.at[c])

    def product(c):
        depth = tokens // 3 if tokens % (3 * LANES) == 0 else LANES
        for k in range(tokens // depth):
            at = pl.ds(k * depth, depth)
            term = jnp.dot(st[:, at], gbuf[c][at], preferred_element_type=jnp.float32)
            pbuf[c][...] = term if k == 0 else pbuf[c][...] + term
        for side in range(2):
            far_send(c, side).start()

    def product_pair(c, i):
        pair = lax.rem(lax.rem(z + steps, nz) // 2 + i, steps)
        at = pl.ds(pl.multiple_of(pair * 2 * tz, LANES), 2 * tz)
        return jnp.dot(st[:, at], gbuf[c][at], preferred_element_type=jnp.float32)

    def product_most(c):
        pbuf[c][...] = product_pair(c, 1)

        def one(i, carry):
            pbuf[c][...] = pbuf[c][...] + product_pair(c, i)
            return carry

        lax.fori_loop(2, steps, one, 0)

    def product_rest(c):
        pbuf[c][...] = pbuf[c][...] + product_pair(c, 0)
        for d in range(1, ny):
            direct_send(c, d).start()

    def direct_finish(c):
        total = pbuf[c][quarter(y)]
        for d in range(1, ny):
            direct_send(c, d).wait_recv()
            total = total + rdir[c - plain][d - 1]
        qbuf[c][...] = total
        for d in range(1, ny):
            direct_out(c, d).start()
        out_own(c).start()

    def direct_done(c):
        for d in range(1, ny):
            direct_out(c, d, incoming=True).wait_recv()
            direct_send(c, d).wait_send()
            direct_out(c, d).wait_send()
        out_own(c).wait()

    def near(c):
        for side in range(2):
            far_send(c, side).wait_recv()
            where = quarter((up, down)[side], side)
            pbuf[c][where] = pbuf[c][where] + rfar[c][side]
            near_send(c, side).start()

    def finish(c):
        total = pbuf[c][quarter(y)]
        for side in range(2):
            near_send(c, side).wait_recv()
            total = total + rnear[c][side]
        qbuf[c][...] = total
        for side in range(2):
            out_send(c, side).start()
        out_own(c).start()

    def forward_out(c):
        for side in range(2):
            out_send(c, side, incoming=True).wait_recv()
            out_forward(c, side).start()

    def out_done(c):
        for side in range(2):
            out_forward(c, side, incoming=True).wait_recv()
            far_send(c, side).wait_send()
            near_send(c, side).wait_send()
            out_send(c, side).wait_send()
            out_forward(c, side).wait_send()
        out_own(c).wait()

    def prepare():
        own_ids.wait()
        idcol[0:TILE] = jnp.full((TILE, LANES), -1.0, jnp.float32)
        xbuf[0:TILE] = jnp.zeros((TILE, xbuf.shape[1]), xbuf.dtype)
        lane = lax.broadcasted_iota(jnp.int32, (8, LANES), 1)
        none = jnp.full((8, LANES), -1.0, jnp.float32)
        flat = []
        for b in range(blocks):
            row = ids_vmem[0:1, b * LANES : (b + 1) * LANES].astype(jnp.float32)
            flat.append(jnp.broadcast_to(row, (8, LANES)))
            idcol[TILE + b * LANES : TILE + (b + 1) * LANES] = jnp.broadcast_to(
                row, (LANES, LANES)
            ).T
        for b in range(blocks):
            before = flat[b - 1] if b > 0 else none
            after = flat[b + 1] if b < blocks - 1 else none
            rows[0, b] = flat[b]
            rows[1, b] = jnp.where(
                lane < TILE, after, jnp.where(lane >= LANES - TILE, before, none)
            )

    def grad_bands():
        before = pl.ds(pl.multiple_of(z_at(nz - 1) * tz + tz - TILE, 32), TILE)
        dims = (((1,), (1,)), ((), ()))
        band = jnp.zeros((tz, wide), jnp.float32)
        for c in range(chunks):
            own = gbuf[c][own_rows]
            pad = jnp.zeros((wide - tz - TILE, WIDTHS[c]), own.dtype)
            window = jnp.concatenate([gbuf[c][before], own, pad], 0)
            band = band + lax.dot_general(own, window, dims, preferred_element_type=jnp.float32)
        bands[...] = band
        for j in range(tiles):
            turned = bands[j * TILE : (j + 1) * TILE]
            if j > 0:
                turned = pltpu.roll(turned, wide - j * TILE, 1)
            bsend[j] = packed(turned[:, :LANES])
            @pl.when(w != j)
            def _():
                grad_send(j).start()

    def act_bands():
        x_came(0).wait_recv()
        for d in range(1, nx):
            x_forwarded(d).wait_recv()

        @pl.when(w < tiles)
        def _():
            def one(d, carry):
                first = pl.multiple_of(z_at(d) * tz + w * TILE, 32)
                window = xbuf[pl.ds(first, 2 * TILE)]
                window = jnp.concatenate([window, jnp.zeros_like(window)], 0)
                dims = (((1,), (1,)), ((), ()))
                asend[d] = packed(
                    lax.dot_general(
                        window[TILE : 2 * TILE], window, dims, preferred_element_type=jnp.float32
                    )
                )
                @pl.when(d > 0)
                def _():
                    act_send(d).start()
                return carry
            lax.fori_loop(0, nz, one, 0)

    def weights():
        @pl.when(w < tiles)
        def _():
            act = asend[0]
            for d in range(1, nz):
                act_send(d).wait_recv()
                act = act + abuf[d]
            bbuf[w] = bsend[w]
            for d in range(1, nw):
                grad_came(w_at(d)).wait_recv()
            grad = bbuf[0]
            for u in range(1, nw):
                grad = grad + bbuf[u]
            tile = z * tiles + w
            first = pl.multiple_of(tile * TILE, 32)
            ids = idcol[pl.ds(first, 2 * TILE)]
            lane = lax.broadcasted_iota(jnp.int32, (8, LANES), 1)
            row = lax.broadcasted_iota(jnp.int32, (8, LANES), 0)
            group, partner = lane // TILE, lax.rem(lane, TILE)
            token = row + 8 * group
            mine = ids[TILE : TILE + 8]
            for k in range(1, 4):
                mine = jnp.where(group == k, ids[TILE + 8 * k : TILE + 8 * k + 8], mine)
            wide_lane = lax.broadcasted_iota(jnp.int32, (TILE, LANES), 1)
            wide_row = lax.broadcasted_iota(jnp.int32, (TILE, LANES), 0)
            pick = lax.rem(wide_lane, TILE) == wide_row
            before = jnp.sum(jnp.where(pick, ids[:TILE], 0.0), 0, keepdims=True)
            same = jnp.sum(jnp.where(pick, ids[TILE:], 0.0), 0, keepdims=True)
            theirs = jnp.where(partner <= token, same, before)
            factor = jnp.where(partner == token, 1.0, 2.0)
            factor = jnp.where(partner <= token, factor, jnp.where(tile > 0, 2.0, 0.0))
            term = jnp.where(mine == theirs, act * grad * factor, 0.0)
            at = lax.rem(tile, LANES // TILE) * TILE
            spread = jnp.zeros((8, LANES), jnp.float32)
            for k in range(4):
                one = jnp.sum(jnp.where(group == k, term, 0.0), 1, keepdims=True)
                spread = spread + jnp.where(lane == row + 8 * k + at, one, 0.0)
            wz[z] = jnp.sum(spread, 0, keepdims=True)
            for d in range(1, nz):
                weight_send(d).start()

    def slabs():
        @pl.when(w < tiles)
        def _():
            for d in range(1, nz):
                weight_came(d).wait_recv()
            wall[w] = wz[...]
            for d in range(1, nw):
                slab_send(d).start()

    def scales():
        for u in range(tiles):
            @pl.when(w != u)
            def _():
                slab_came(u).wait_recv()
        lane = lax.broadcasted_iota(jnp.int32, (8, LANES), 1)
        none = jnp.zeros((8, LANES), jnp.float32)
        flat = []
        for b in range(blocks):
            row = none
            for k in range(b * (LANES // TILE), (b + 1) * (LANES // TILE)):
                owner, j = divmod(k, tiles)
                row = row + jnp.broadcast_to(wall[j, owner], (8, LANES))
            flat.append(row)
        for b in range(blocks):
            before = flat[b - 1] if b > 0 else none
            after = flat[b + 1] if b < blocks - 1 else none
            rows[2, b] = flat[b]
            rows[3, b] = jnp.where(
                lane < TILE, after, jnp.where(lane >= LANES - TILE, before, none)
            )
        limit = clip_ref[0].astype(jnp.float32)

        def one(b, carry):
            at = pl.multiple_of(TILE + b * LANES, 32)
            ids = idcol[pl.ds(at, LANES)]
            found = jnp.where(ids == rows[0, b][0:1], rows[2, b][0:1], 0.0)
            found = found + jnp.where(ids == rows[1, b][0:1], rows[3, b][0:1], 0.0)
            squares = jnp.sum(found, 1, keepdims=True)
            factor = limit / jnp.maximum(jnp.sqrt(jnp.maximum(squares, 0.0)), limit)
            scaled = xbuf[pl.ds(at, LANES)].astype(jnp.float32) * factor
            st[:, pl.ds(pl.multiple_of(b * LANES, LANES), LANES)] = scaled.T.astype(st.dtype)
            return carry

        lax.fori_loop(0, blocks, one, 0)

    def forward_x():
        for d in range(1, nx):
            x_came(d).wait_recv()
            x_forward(d).start()

    first_slot = FIRST_SLOTS
    final_slot = first_slot[-1] + steps
    between = {0: (prepare,), 1: (grad_bands,), 2: (forward_x,), 3: (act_bands,), 5: (weights,),
               6: (slabs,), 7: (scales,)}

    def ring_sent(c):
        for s in range(steps):
            for way in range(2):
                ring(way, c, s).wait_send()

    def hop(t, c):
        s = t - first_slot[c]
        if 0 <= s < steps:
            for way in range(2):
                if s > 0:
                    ring(way, c, s - 1, incoming=True).wait_recv()
                ring(way, c, s).start()

    def first(c):
        for way in range(2):
            ring(way, c, steps - 1, incoming=True).wait_recv()
        if c >= plain:
            product_rest(c)
        else:
            product(c)
        ring_sent(c)

    def stages(p):
        for c in range(chunks):
            calls = (first, near, finish, forward_out, out_done)
            if c >= plain:
                calls = (first, direct_finish, direct_done)
            stage, rest = divmod(p - 2 * (first_slot[c] + steps) - c % 2, STAGE_GAP)
            if 0 <= stage < len(calls) and rest == 0:
                calls[stage](c)

    for t in range(final_slot):
        if t == 1:
            for c in range(chunks):
                halo_copy(c, incoming=True).wait_recv()
                own_g[c].wait()
        for c in range(0, chunks, 2):
            hop(t, c)
        if t == 0:
            for d in range(nx):
                x_first(d).start()
            for c in range(chunks):
                halo_copy(c).start()
            own_x.wait()
        for step in between.get(t, ()):
            step()
        stages(2 * t)
        for c in range(1, chunks, 2):
            hop(t, c)
        stages(2 * t + 1)
        for c in range(plain, chunks):
            if t == first_slot[c] + steps - 1:
                product_most(c)

    for c in range(chunks):
        halo_copy(c).wait_send()
    for d in range(nx):
        x_first(d).wait_send()
    for d in range(1, nx):
        x_forward(d).wait_send()
    for j in range(tiles):
        @pl.when(w != j)
        def _():
            grad_send(j).wait_send()

    @pl.when(w < tiles)
    def _():
        for d in range(1, nz):
            act_send(d).wait_send()
            weight_send(d).wait_send()
        for d in range(1, nw):
            slab_send(d).wait_send()

    for p in range(2 * final_slot, 2 * final_slot + 5 * STAGE_GAP):
        stages(p)


def body(sizes, activations, out_grads, query_ids, clip_bound):
    x_local = activations[0]
    g_local = out_grads[0]
    ny, nz, nw, tokens = sizes
    nx = nw // 2
    features, hidden = x_local.shape[1], g_local.shape[1]
    tz = g_local.shape[0]
    tiles = tz // TILE
    chunks = len(WIDTHS)
    assert sum(WIDTHS) == hidden
    steps = nz // 2
    part = features // ny
    dma = pltpu.SemaphoreType.DMA
    f32, bf16 = jnp.float32, jnp.bfloat16
    stay = [
        pltpu.with_memory_space_constraint(a, pltpu.HBM) for a in (x_local, g_local, query_ids)
    ]
    return pl.pallas_call(
        functools.partial(kernel, sizes),
        out_shape=jax.ShapeDtypeStruct((features, hidden), f32),
        in_specs=[
            pl.BlockSpec(memory_space=pltpu.HBM),
            pl.BlockSpec(memory_space=pltpu.HBM),
            pl.BlockSpec(memory_space=pltpu.HBM),
            pl.BlockSpec(memory_space=pltpu.SMEM),
        ],
        out_specs=pl.BlockSpec(memory_space=pl.ANY),
        scratch_shapes=[
            pltpu.VMEM((1, tokens), jnp.int32),
            pltpu.VMEM((tz, -(-(tz + TILE) // LANES) * LANES), f32),
            [pltpu.VMEM((tokens, n), bf16) for n in WIDTHS],
            pltpu.VMEM((TILE + tokens, features), bf16),
            pltpu.VMEM((features, tokens), bf16),
            pltpu.VMEM((TILE + tokens, LANES), f32),
            pltpu.VMEM((4, tokens // LANES, 8, LANES), f32),
            pltpu.VMEM((nz, 8, LANES), f32),
            pltpu.VMEM((nz, 8, LANES), f32),
            pltpu.VMEM((tiles, 8, LANES), f32),
            pltpu.VMEM((nw, 8, LANES), f32),
            pltpu.VMEM((nz, 1, LANES), f32),
            pltpu.VMEM((tiles, nz, 1, LANES), f32),
            [pltpu.VMEM((features, n), f32) for n in WIDTHS],
            [pltpu.VMEM((2, part // 2, n), f32) for n in WIDTHS],
            [pltpu.VMEM((2, part, n), f32) for n in WIDTHS],
            [pltpu.VMEM((part, n), f32) for n in WIDTHS],
            [pltpu.VMEM((ny - 1, part, n), f32) for n in WIDTHS[-DIRECT:]],
            dma((chunks + 2,)), dma((chunks,)),
            dma((2 * nx,)), dma((2 * nx,)),
            dma((2, chunks)),
            dma((2, chunks, steps)), dma((2, chunks, steps)),
            dma((nz,)), dma((nz,)),
            dma((tiles,)), dma((nw,)),
            dma((nw,)), dma((tiles,)),
            dma((nz,)), dma((nz,)),
            *[dma((chunks, 2))] * 8,
            dma((4, DIRECT, ny - 1)),
        ],
        compiler_params=pltpu.CompilerParams(
            collective_id=0, has_side_effects=True, vmem_limit_bytes=50 * 1024 * 1024
        ),
        cost_estimate=pl.CostEstimate(
            flops=2 * tokens * features * hidden, bytes_accessed=1 << 23, transcendentals=0
        ),
    )(*stay, clip_bound)


def solution(mesh):
    sizes = tuple(mesh.shape[a] for a in ("dp", "row", "col"))

    def run(activations, out_grads, query_ids, clip_bound):
        placed = (P("dp", "col", "row"), P("dp", "row", "col"), P("dp", None), P())
        return jax.shard_map(
            functools.partial(body, sizes + (query_ids.shape[1],)),
            mesh=mesh, in_specs=placed, out_specs=P("row", "col"), check_vma=False,
        )(activations, out_grads, query_ids, clip_bound)

    return run
```

```python
import functools

import jax
import jax.numpy as jnp
from jax import lax
from jax.experimental import pallas as pl
from jax.experimental.pallas import tpu as pltpu
from jax.sharding import PartitionSpec as P

TILE = 32
LANES = 128
WIDTHS = (256, 256, 256, 256, 256, 256, 256)
FIRST_SLOTS = (0, 0, 0, 1, 3, 6, 7)
STAGE_GAP = 2
DIRECT = 2
SPLIT = 3
MESH = pl.DeviceIdType.MESH


def packed(products):
    lane = lax.broadcasted_iota(jnp.int32, (TILE, LANES), 1)
    row = lax.broadcasted_iota(jnp.int32, (TILE, LANES), 0)
    near = jnp.where(lane <= row, pltpu.roll(products, LANES - TILE, 1), products)
    group = lax.broadcasted_iota(jnp.int32, (8, LANES), 1) // TILE
    out = near[:8]
    for k in range(1, 4):
        out = jnp.where(group == k, pltpu.roll(near[8 * k : 8 * k + 8], TILE * k, 1), out)
    return out


def kernel(
    sizes,
    x_ref, g_ref, ids_ref, clip_ref,
    out_ref,
    ids_vmem, bands, gbuf, xbuf, st, idcol, rows,
    asend, abuf, bsend, bbuf, wz, wall,
    pbuf, rfar, rnear, qbuf, rdir,
    lsem, osem, xs, xr, hs, rs, rr, asem, arec, bsem, brec, wsem, wrec, zsem, zrec,
    s1, r1, s2, r2, s3, r3, s4, r4, sd,
):
    ny, nz, nw, tokens = sizes
    nx = nw // 2
    tz = g_ref.shape[0]
    tc = x_ref.shape[0]
    tiles = tz // TILE
    chunks = len(WIDTHS)
    plain = chunks - DIRECT
    columns = [pl.ds(sum(WIDTHS[:c]), WIDTHS[c]) for c in range(chunks)]
    steps = nz // 2
    wide = bands.shape[1]
    blocks = tokens // LANES
    part = x_ref.shape[1] // ny

    y = lax.axis_index("dp")
    z = lax.axis_index("row")
    w = lax.axis_index("col")
    core = lax.rem(w, 2)
    chip = w // 2

    def z_at(d):
        return lax.rem(z + d, nz)

    def w_at(d):
        return lax.rem(w + d, nw)

    def y_at(d):
        return lax.rem(y + d, ny)

    def copy_to(src, dst, send, recv, **axis):
        return pltpu.make_async_remote_copy(
            src_ref=src, dst_ref=dst, send_sem=send, recv_sem=recv,
            device_id=axis, device_id_type=MESH,
        )

    own_rows = pl.ds(pl.multiple_of(z * tz, 32), tz)
    own_g = [
        pltpu.make_async_copy(
            g_ref.at[:, columns[c]], gbuf[c].at[own_rows], lsem.at[c]
        )
        for c in range(chunks)
    ]
    own_x = pltpu.make_async_copy(
        x_ref, xbuf.at[pl.ds(pl.multiple_of(TILE + w * tc, 32), tc)], lsem.at[chunks]
    )
    own_ids = pltpu.make_async_copy(ids_ref, ids_vmem, lsem.at[chunks + 1])
    for copy in own_g:
        copy.start()
    own_x.start()
    own_ids.start()

    barrier = pltpu.get_barrier_semaphore()
    for d in range(1, nz):
        pl.semaphore_signal(barrier, inc=1, device_id={"row": z_at(d)}, device_id_type=MESH)
    for d in range(1, nw):
        pl.semaphore_signal(barrier, inc=1, device_id={"col": w_at(d)}, device_id_type=MESH)
    for d in range(1, ny):
        pl.semaphore_signal(barrier, inc=1, device_id={"dp": y_at(d)}, device_id_type=MESH)
    pl.semaphore_wait(barrier, nz + nw + ny - 3)

    def x_rows(owner):
        return xbuf.at[pl.ds(pl.multiple_of(TILE + owner * tc, 32), tc)]

    sibling = chip * 2 + 1 - core

    def x_first(d):
        to = sibling if d == 0 else lax.rem(chip + d, nx) * 2 + core
        return copy_to(x_ref, x_rows(w), xs.at[d], xr.at[d], col=to)

    def x_came(d):
        owner = sibling if d == 0 else lax.rem(chip + nx - d, nx) * 2 + core
        return copy_to(x_rows(owner), x_rows(owner), xs.at[d], xr.at[d], col=sibling)

    def x_forward(d):
        owner = lax.rem(chip + nx - d, nx) * 2 + core
        return copy_to(
            x_rows(owner), x_rows(owner), xs.at[nx - 1 + d], xr.at[nx - 1 + d], col=sibling
        )

    def x_forwarded(d):
        owner = lax.rem(chip + nx - d, nx) * 2 + 1 - core
        return copy_to(
            x_rows(owner), x_rows(owner), xs.at[nx - 1 + d], xr.at[nx - 1 + d], col=sibling
        )

    def ring(way, c, s, incoming=False):
        hop = s + 1 if incoming else s
        owner = z_at(nz - hop) if way == 0 else z_at(hop)
        skip, count = 0, tz
        if s == steps - 1:
            skip, count = way * (tz // 2), tz // 2
        elif s == 0 and way == 0:
            count = tz - TILE
        block = gbuf[c].at[pl.ds(pl.multiple_of(owner * tz + skip, 32), count)]
        src = block
        if s == 0 and not incoming:
            src = g_ref.at[pl.ds(0, count), columns[c]]
        to = z_at(1) if way == 0 else z_at(nz - 1)
        return copy_to(src, block, rs.at[way, c, s], rr.at[way, c, s], row=to)

    def halo_copy(c, incoming=False):
        owner = z_at(nz - 1) if incoming else z
        there = gbuf[c].at[pl.ds(pl.multiple_of(owner * tz + tz - TILE, 32), TILE)]
        src = there if incoming else g_ref.at[pl.ds(tz - TILE, TILE), columns[c]]
        return copy_to(src, there, hs.at[0, c], hs.at[1, c], row=z_at(1))

    def act_send(d):
        return copy_to(asend.at[d], abuf.at[d], asem.at[d], arec.at[d], row=z_at(d))

    def grad_send(j):
        return copy_to(bsend.at[j], bbuf.at[w], bsem.at[j], brec.at[w], col=j)

    def grad_came(owner):
        return copy_to(bbuf.at[owner], bbuf.at[owner], bsem.at[0], brec.at[owner], col=w_at(1))

    def weight_send(d):
        return copy_to(wz.at[z], wz.at[z], zsem.at[d], zrec.at[d], row=z_at(d))

    def weight_came(d):
        owner = z_at(nz - d)
        return copy_to(wz.at[owner], wz.at[owner], zsem.at[d], zrec.at[d], row=z_at(1))

    def slab_send(d):
        return copy_to(wz, wall.at[w], wsem.at[d], wrec.at[w], col=w_at(d))

    def slab_came(owner):
        return copy_to(wall.at[owner], wall.at[owner], wsem.at[1], wrec.at[owner], col=w_at(1))

    up, far, down = y_at(1), y_at(2), y_at(3)
    half = part // 2

    def quarter(owner, side=None):
        if side is None:
            return pl.ds(pl.multiple_of(owner * part, part), part)
        return pl.ds(pl.multiple_of(owner * part + side * half, half), half)

    def far_send(c, side):
        return copy_to(
            pbuf[c].at[quarter(far, side)], rfar[c].at[side], s1.at[c, side], r1.at[c, side],
            dp=(up, down)[side],
        )

    def near_send(c, side):
        to = (up, down)[side]
        return copy_to(
            pbuf[c].at[quarter(to)], rnear[c].at[side], s2.at[c, side], r2.at[c, side], dp=to
        )

    def out_at(c, where):
        return out_ref.at[where, columns[c]]

    def out_send(c, side, incoming=False):
        at = out_at(c, quarter((down, up)[side] if incoming else y))
        return copy_to(
            at if incoming else qbuf[c], at, s3.at[c, side], r3.at[c, side],
            dp=(up, down)[side],
        )

    def out_forward(c, side, incoming=False):
        at = out_at(c, quarter(far if incoming else (down, up)[side], side))
        return copy_to(at, at, s4.at[c, side], r4.at[c, side], dp=(up, down)[side])

    def direct_send(c, d):
        to = y_at(d)
        return copy_to(
            pbuf[c].at[quarter(to)], rdir[c - plain].at[d - 1],
            sd.at[0, c - plain, d - 1], sd.at[1, c - plain, d - 1], dp=to,
        )

    def direct_out(c, d, incoming=False):
        at = out_at(c, quarter(y_at(ny - d) if incoming else y))
        return copy_to(
            at if incoming else qbuf[c], at,
            sd.at[2, c - plain, d - 1], sd.at[3, c - plain, d - 1], dp=y_at(d),
        )

    def out_own(c):
        return pltpu.make_async_copy(qbuf[c], out_at(c, quarter(y)), osem.at[c])

    def product(c):
        depth = tokens // 3 if tokens % (3 * LANES) == 0 else LANES
        for k in range(tokens // depth):
            at = pl.ds(k * depth, depth)
            term = jnp.dot(st[:, at], gbuf[c][at], preferred_element_type=jnp.float32)
            pbuf[c][...] = term if k == 0 else pbuf[c][...] + term
        for side in range(2):
            far_send(c, side).start()

    def product_pair(c, i):
        pair = lax.rem(lax.rem(z + steps, nz) // 2 + i, steps)
        at = pl.ds(pl.multiple_of(pair * 2 * tz, LANES), 2 * tz)
        return jnp.dot(st[:, at], gbuf[c][at], preferred_element_type=jnp.float32)

    def product_most(c):
        pbuf[c][...] = product_pair(c, 1)

        def one(i, carry):
            pbuf[c][...] = pbuf[c][...] + product_pair(c, i)
            return carry

        lax.fori_loop(2, steps, one, 0)

    def product_rest(c):
        pbuf[c][...] = pbuf[c][...] + product_pair(c, 0)
        if c < plain:
            for side in range(2):
                far_send(c, side).start()
        else:
            for d in range(1, ny):
                direct_send(c, d).start()

    def direct_finish(c):
        total = pbuf[c][quarter(y)]
        for d in range(1, ny):
            direct_send(c, d).wait_recv()
            total = total + rdir[c - plain][d - 1]
        qbuf[c][...] = total
        for d in range(1, ny):
            direct_out(c, d).start()
        out_own(c).start()

    def direct_done(c):
        for d in range(1, ny):
            direct_out(c, d, incoming=True).wait_recv()
            direct_send(c, d).wait_send()
            direct_out(c, d).wait_send()
        out_own(c).wait()

    def near(c):
        for side in range(2):
            far_send(c, side).wait_recv()
            where = quarter((up, down)[side], side)
            pbuf[c][where] = pbuf[c][where] + rfar[c][side]
            near_send(c, side).start()

    def finish(c):
        total = pbuf[c][quarter(y)]
        for side in range(2):
            near_send(c, side).wait_recv()
            total = total + rnear[c][side]
        qbuf[c][...] = total
        for side in range(2):
            out_send(c, side).start()
        out_own(c).start()

    def forward_out(c):
        for side in range(2):
            out_send(c, side, incoming=True).wait_recv()
            out_forward(c, side).start()

    def out_done(c):
        for side in range(2):
            out_forward(c, side, incoming=True).wait_recv()
            far_send(c, side).wait_send()
            near_send(c, side).wait_send()
            out_send(c, side).wait_send()
            out_forward(c, side).wait_send()
        out_own(c).wait()

    def prepare():
        own_ids.wait()
        idcol[0:TILE] = jnp.full((TILE, LANES), -1.0, jnp.float32)
        xbuf[0:TILE] = jnp.zeros((TILE, xbuf.shape[1]), xbuf.dtype)
        lane = lax.broadcasted_iota(jnp.int32, (8, LANES), 1)
        none = jnp.full((8, LANES), -1.0, jnp.float32)
        flat = []
        for b in range(blocks):
            row = ids_vmem[0:1, b * LANES : (b + 1) * LANES].astype(jnp.float32)
            flat.append(jnp.broadcast_to(row, (8, LANES)))
            idcol[TILE + b * LANES : TILE + (b + 1) * LANES] = jnp.broadcast_to(
                row, (LANES, LANES)
            ).T
        for b in range(blocks):
            before = flat[b - 1] if b > 0 else none
            after = flat[b + 1] if b < blocks - 1 else none
            rows[0, b] = flat[b]
            rows[1, b] = jnp.where(
                lane < TILE, after, jnp.where(lane >= LANES - TILE, before, none)
            )

    def grad_bands():
        before = pl.ds(pl.multiple_of(z_at(nz - 1) * tz + tz - TILE, 32), TILE)
        dims = (((1,), (1,)), ((), ()))
        band = jnp.zeros((tz, wide), jnp.float32)
        for c in range(chunks):
            own = gbuf[c][own_rows]
            pad = jnp.zeros((wide - tz - TILE, WIDTHS[c]), own.dtype)
            window = jnp.concatenate([gbuf[c][before], own, pad], 0)
            band = band + lax.dot_general(own, window, dims, preferred_element_type=jnp.float32)
        bands[...] = band
        for j in range(tiles):
            turned = bands[j * TILE : (j + 1) * TILE]
            if j > 0:
                turned = pltpu.roll(turned, wide - j * TILE, 1)
            bsend[j] = packed(turned[:, :LANES])
            @pl.when(w != j)
            def _():
                grad_send(j).start()

    def act_bands():
        x_came(0).wait_recv()
        for d in range(1, nx):
            x_forwarded(d).wait_recv()

        @pl.when(w < tiles)
        def _():
            def one(d, carry):
                first = pl.multiple_of(z_at(d) * tz + w * TILE, 32)
                window = xbuf[pl.ds(first, 2 * TILE)]
                window = jnp.concatenate([window, jnp.zeros_like(window)], 0)
                dims = (((1,), (1,)), ((), ()))
                asend[d] = packed(
                    lax.dot_general(
                        window[TILE : 2 * TILE], window, dims, preferred_element_type=jnp.float32
                    )
                )
                @pl.when(d > 0)
                def _():
                    act_send(d).start()
                return carry
            lax.fori_loop(0, nz, one, 0)

    def weights():
        @pl.when(w < tiles)
        def _():
            act = asend[0]
            for d in range(1, nz):
                act_send(d).wait_recv()
                act = act + abuf[d]
            bbuf[w] = bsend[w]
            for d in range(1, nw):
                grad_came(w_at(d)).wait_recv()
            grad = bbuf[0]
            for u in range(1, nw):
                grad = grad + bbuf[u]
            tile = z * tiles + w
            first = pl.multiple_of(tile * TILE, 32)
            ids = idcol[pl.ds(first, 2 * TILE)]
            lane = lax.broadcasted_iota(jnp.int32, (8, LANES), 1)
            row = lax.broadcasted_iota(jnp.int32, (8, LANES), 0)
            group, partner = lane // TILE, lax.rem(lane, TILE)
            token = row + 8 * group
            mine = ids[TILE : TILE + 8]
            for k in range(1, 4):
                mine = jnp.where(group == k, ids[TILE + 8 * k : TILE + 8 * k + 8], mine)
            wide_lane = lax.broadcasted_iota(jnp.int32, (TILE, LANES), 1)
            wide_row = lax.broadcasted_iota(jnp.int32, (TILE, LANES), 0)
            pick = lax.rem(wide_lane, TILE) == wide_row
            before = jnp.sum(jnp.where(pick, ids[:TILE], 0.0), 0, keepdims=True)
            same = jnp.sum(jnp.where(pick, ids[TILE:], 0.0), 0, keepdims=True)
            theirs = jnp.where(partner <= token, same, before)
            factor = jnp.where(partner == token, 1.0, 2.0)
            factor = jnp.where(partner <= token, factor, jnp.where(tile > 0, 2.0, 0.0))
            term = jnp.where(mine == theirs, act * grad * factor, 0.0)
            at = lax.rem(tile, LANES // TILE) * TILE
            spread = jnp.zeros((8, LANES), jnp.float32)
            for k in range(4):
                one = jnp.sum(jnp.where(group == k, term, 0.0), 1, keepdims=True)
                spread = spread + jnp.where(lane == row + 8 * k + at, one, 0.0)
            wz[z] = jnp.sum(spread, 0, keepdims=True)
            for d in range(1, nz):
                weight_send(d).start()

    def slabs():
        @pl.when(w < tiles)
        def _():
            for d in range(1, nz):
                weight_came(d).wait_recv()
            wall[w] = wz[...]
            for d in range(1, nw):
                slab_send(d).start()

    def scales():
        for u in range(tiles):
            @pl.when(w != u)
            def _():
                slab_came(u).wait_recv()
        lane = lax.broadcasted_iota(jnp.int32, (8, LANES), 1)
        none = jnp.zeros((8, LANES), jnp.float32)
        flat = []
        for b in range(blocks):
            row = none
            for k in range(b * (LANES // TILE), (b + 1) * (LANES // TILE)):
                owner, j = divmod(k, tiles)
                row = row + jnp.broadcast_to(wall[j, owner], (8, LANES))
            flat.append(row)
        for b in range(blocks):
            before = flat[b - 1] if b > 0 else none
            after = flat[b + 1] if b < blocks - 1 else none
            rows[2, b] = flat[b]
            rows[3, b] = jnp.where(
                lane < TILE, after, jnp.where(lane >= LANES - TILE, before, none)
            )
        limit = clip_ref[0].astype(jnp.float32)

        def one(b, carry):
            at = pl.multiple_of(TILE + b * LANES, 32)
            ids = idcol[pl.ds(at, LANES)]
            found = jnp.where(ids == rows[0, b][0:1], rows[2, b][0:1], 0.0)
            found = found + jnp.where(ids == rows[1, b][0:1], rows[3, b][0:1], 0.0)
            squares = jnp.sum(found, 1, keepdims=True)
            factor = limit / jnp.maximum(jnp.sqrt(jnp.maximum(squares, 0.0)), limit)
            scaled = xbuf[pl.ds(at, LANES)].astype(jnp.float32) * factor
            st[:, pl.ds(pl.multiple_of(b * LANES, LANES), LANES)] = scaled.T.astype(st.dtype)
            return carry

        lax.fori_loop(0, blocks, one, 0)

    def forward_x():
        for d in range(1, nx):
            x_came(d).wait_recv()
            x_forward(d).start()

    first_slot = FIRST_SLOTS
    final_slot = first_slot[-1] + steps
    between = {0: (prepare,), 1: (grad_bands,), 2: (forward_x,), 3: (act_bands,), 5: (weights,),
               6: (slabs,), 7: (scales,)}

    def ring_sent(c):
        for s in range(steps):
            for way in range(2):
                ring(way, c, s).wait_send()

    def hop(t, c):
        s = t - first_slot[c]
        if 0 <= s < steps:
            for way in range(2):
                if s > 0:
                    ring(way, c, s - 1, incoming=True).wait_recv()
                ring(way, c, s).start()

    def first(c):
        for way in range(2):
            ring(way, c, steps - 1, incoming=True).wait_recv()
        if c >= chunks - SPLIT:
            product_rest(c)
        else:
            product(c)
        ring_sent(c)

    def stages(p):
        for c in range(chunks):
            calls = (first, near, finish, forward_out, out_done)
            if c >= plain:
                calls = (first, direct_finish, direct_done)
            stage, rest = divmod(p - 2 * (first_slot[c] + steps) - c % 2, STAGE_GAP)
            if 0 <= stage < len(calls) and rest == 0:
                calls[stage](c)

    for t in range(final_slot):
        if t == 1:
            for c in range(chunks):
                halo_copy(c, incoming=True).wait_recv()
                own_g[c].wait()
        for c in range(0, chunks, 2):
            hop(t, c)
        if t == 0:
            for d in range(nx):
                x_first(d).start()
            for c in range(chunks):
                halo_copy(c).start()
            own_x.wait()
        for step in between.get(t, ()):
            step()
        stages(2 * t)
        for c in range(1, chunks, 2):
            hop(t, c)
        stages(2 * t + 1)
        for c in range(chunks - SPLIT, chunks):
            if t == first_slot[c] + steps - 1:
                product_most(c)

    for c in range(chunks):
        halo_copy(c).wait_send()
    for d in range(nx):
        x_first(d).wait_send()
    for d in range(1, nx):
        x_forward(d).wait_send()
    for j in range(tiles):
        @pl.when(w != j)
        def _():
            grad_send(j).wait_send()

    @pl.when(w < tiles)
    def _():
        for d in range(1, nz):
            act_send(d).wait_send()
            weight_send(d).wait_send()
        for d in range(1, nw):
            slab_send(d).wait_send()

    for p in range(2 * final_slot, 2 * final_slot + 5 * STAGE_GAP):
        stages(p)


def body(sizes, activations, out_grads, query_ids, clip_bound):
    x_local = activations[0]
    g_local = out_grads[0]
    ny, nz, nw, tokens = sizes
    nx = nw // 2
    features, hidden = x_local.shape[1], g_local.shape[1]
    tz = g_local.shape[0]
    tiles = tz // TILE
    chunks = len(WIDTHS)
    assert sum(WIDTHS) == hidden
    steps = nz // 2
    part = features // ny
    dma = pltpu.SemaphoreType.DMA
    f32, bf16 = jnp.float32, jnp.bfloat16
    stay = [
        pltpu.with_memory_space_constraint(a, pltpu.HBM) for a in (x_local, g_local, query_ids)
    ]
    return pl.pallas_call(
        functools.partial(kernel, sizes),
        out_shape=jax.ShapeDtypeStruct((features, hidden), f32),
        in_specs=[
            pl.BlockSpec(memory_space=pltpu.HBM),
            pl.BlockSpec(memory_space=pltpu.HBM),
            pl.BlockSpec(memory_space=pltpu.HBM),
            pl.BlockSpec(memory_space=pltpu.SMEM),
        ],
        out_specs=pl.BlockSpec(memory_space=pl.ANY),
        scratch_shapes=[
            pltpu.VMEM((1, tokens), jnp.int32),
            pltpu.VMEM((tz, -(-(tz + TILE) // LANES) * LANES), f32),
            [pltpu.VMEM((tokens, n), bf16) for n in WIDTHS],
            pltpu.VMEM((TILE + tokens, features), bf16),
            pltpu.VMEM((features, tokens), bf16),
            pltpu.VMEM((TILE + tokens, LANES), f32),
            pltpu.VMEM((4, tokens // LANES, 8, LANES), f32),
            pltpu.VMEM((nz, 8, LANES), f32),
            pltpu.VMEM((nz, 8, LANES), f32),
            pltpu.VMEM((tiles, 8, LANES), f32),
            pltpu.VMEM((nw, 8, LANES), f32),
            pltpu.VMEM((nz, 1, LANES), f32),
            pltpu.VMEM((tiles, nz, 1, LANES), f32),
            [pltpu.VMEM((features, n), f32) for n in WIDTHS],
            [pltpu.VMEM((2, part // 2, n), f32) for n in WIDTHS],
            [pltpu.VMEM((2, part, n), f32) for n in WIDTHS],
            [pltpu.VMEM((part, n), f32) for n in WIDTHS],
            [pltpu.VMEM((ny - 1, part, n), f32) for n in WIDTHS[-DIRECT:]],
            dma((chunks + 2,)), dma((chunks,)),
            dma((2 * nx,)), dma((2 * nx,)),
            dma((2, chunks)),
            dma((2, chunks, steps)), dma((2, chunks, steps)),
            dma((nz,)), dma((nz,)),
            dma((tiles,)), dma((nw,)),
            dma((nw,)), dma((tiles,)),
            dma((nz,)), dma((nz,)),
            *[dma((chunks, 2))] * 8,
            dma((4, DIRECT, ny - 1)),
        ],
        compiler_params=pltpu.CompilerParams(
            collective_id=0, has_side_effects=True, vmem_limit_bytes=50 * 1024 * 1024
        ),
        cost_estimate=pl.CostEstimate(
            flops=2 * tokens * features * hidden, bytes_accessed=1 << 23, transcendentals=0
        ),
    )(*stay, clip_bound)


def solution(mesh):
    sizes = tuple(mesh.shape[a] for a in ("dp", "row", "col"))

    def run(activations, out_grads, query_ids, clip_bound):
        placed = (P("dp", "col", "row"), P("dp", "row", "col"), P("dp", None), P())
        return jax.shard_map(
            functools.partial(body, sizes + (query_ids.shape[1],)),
            mesh=mesh, in_specs=placed, out_specs=P("row", "col"), check_vma=False,
        )(activations, out_grads, query_ids, clip_bound)

    return run
```
